32 devices in a mesh: spot: 16 (over z, x, core), grp: 2 (over y).
Axes of the slice: x: 2, y: 2, z: 4, core: 2. Of those that a mesh axis runs over, the one named last changes fastest.
Arguments:
- map_logits: bfloat16 [16384, 4096], P(None, ('spot', 'grp')), may hold values from -8 to 8
- single_cell: bfloat16 [16384, 2048], P(('spot', 'grp')), may hold values from -1.671875 to 1.71875
- spatial: bfloat16 [4096, 2048], P(('spot', 'grp')), may hold values from 0 to 2
- slide_ids: int32 [4096], P(('spot', 'grp')), may hold values from 0 to 2
- spot_mask: int32 [4096], P(('spot', 'grp')), may hold values 0 or 1
- cell_prior: float32 [16384], replicated, may hold values from 0.2 to 5
- gene_order: int32 [4], replicated, may hold values from 0 to 3, each once
Outputs:
- loss_terms: float32 [3], replicated
- grad_map: float32 [16384, 4096], P(None, ('spot', 'grp'))
- grad_single: float32 [16384, 2048], P(('spot', 'grp'))
The draws below stay inside these ranges and needn't reach their ends.
All inputs are finite; a program needn't handle non-finite values. No bound on the sum of `spot_mask` on one device may be relied on, other than what follows from the above.
Results may differ from the reference program's by a relative error of at most 0.0032.
Values may be sent and summed in bfloat16 or wider, within the bound.
A program may use at most 384 MiB of HBM per device.

```python
import math
import jax
import jax.numpy as jnp
from jax import lax

G = 2048
CELLS = 16384
NB = 4
SLIDES = 3
SPOTS = 4096


def touch_ends(array, stream_key, smallest, top_value):
    place = [jax.random.randint(jax.random.fold_in(stream_key, axis), (), 0, length) for axis, length in enumerate(array.shape)]
    widest = array.shape.index(max(array.shape))
    next_to = place[:widest] + [(place[widest] + 1) % array.shape[widest]] + place[widest + 1:]
    return array.at[tuple(place)].set(smallest).at[tuple(next_to)].set(top_value)


def level_of(stream_key, extent, split, low, largest):
    factor_of, own = 1.0, jax.random.fold_in(stream_key, 6)
    for position, parts in split:
        heights = jnp.exp(jax.random.uniform(jax.random.fold_in(own, position), (parts,), jnp.float32, low / len(split), largest / len(split)))
        factor_of = factor_of * jnp.repeat(heights, extent[position] // parts).reshape([-1 if axis == position else 1 for axis in range(len(extent))])
    return factor_of


def centred(key, extent, width, reach, pieces=(), held_as=jnp.bfloat16):
    values = jax.random.normal(key, extent, jnp.float32) * width
    if len(pieces) > 0:
        values = level_of(key, extent, pieces, -0.22, 0.18) * values
    return jnp.clip(values, min=-reach, max=reach).astype(held_as)


def setup_inputs(seed: int = 0) -> dict:
    streams_of = jax.random.split(jax.random.key(seed), 8)
    map_logits = centred(streams_of[0], (CELLS, SPOTS), 1.5, 8.0, ((1, 32),))
    single_cell = jnp.clip(-1.671875 + 3.390625 * jax.random.uniform(streams_of[1], (CELLS, G), jnp.float32) ** level_of(streams_of[1], (CELLS, G), ((0, 32),), -0.2, 0.2), -1.671875, 1.71875).astype(jnp.bfloat16)
    spatial = jnp.clip(2.0 * jax.random.uniform(streams_of[2], (SPOTS, G), jnp.float32) ** level_of(streams_of[2], (SPOTS, G), ((0, 32),), -0.2, 0.2), 0.0, 2.0).astype(jnp.bfloat16)
    slide_ids = touch_ends(jax.random.randint(streams_of[3], (SPOTS,), 0, SLIDES), jax.random.fold_in(streams_of[3], 1), 0, SLIDES - 1).astype(jnp.int32)
    spot_mask = touch_ends((jax.random.randint(streams_of[4], (SPOTS,), 0, 8) < 7).astype(jnp.int32), jax.random.fold_in(streams_of[4], 1), 0, 1)
    cell_prior = jnp.clip(jnp.exp(jax.random.uniform(streams_of[5], (CELLS,), jnp.float32, math.log(0.2), math.log(5.0))), 0.2, 5.0)
    gene_order = jax.random.permutation(streams_of[6], NB).astype(jnp.int32)
    return {"map_logits": map_logits, "single_cell": single_cell, "spatial": spatial, "slide_ids": slide_ids, "spot_mask": spot_mask, "cell_prior": cell_prior, "gene_order": gene_order}


@jax.custom_vjp
def low(v):
    return lax.optimization_barrier(v.astype(jnp.bfloat16)).astype(jnp.float32)

@jax.custom_vjp
def low_back(v):
    return v

def low_keep(v):
    return (low(v), None)

def low_pass(kept, grad):
    return (grad,)

def back_keep(v):
    return (v, None)

def back_low(kept, grad):
    return (low(grad),)
low.defvjp(low_keep, low_pass)
low_back.defvjp(back_keep, back_low)
STABILITY_FLOOR = 1e-06
FULL_ACCURACY = lax.Precision.HIGHEST

def reference(map_logits, single_cell, spatial, slide_ids, spot_mask, cell_prior, gene_order):
    weight_factor = spot_mask.astype(jnp.float32)
    group_members = (slide_ids[:, None] == jnp.arange(SLIDES, dtype=jnp.int32)[None, :]).astype(jnp.float32) * weight_factor[:, None]
    tally = jnp.maximum(lax.optimization_barrier(jnp.sum(group_members, axis=0)), 1.0)
    total = jnp.sum(tally)
    measured_expression = spatial.astype(jnp.float32)
    prior = cell_prior.astype(jnp.float32)
    prior = prior / jnp.sum(prior)

    def forward(scores, cells_all):
        shares = jax.nn.softmax(scores, axis=0)
        shares_low = low(shares)
        blocked = cells_all.reshape(CELLS, NB, G // NB)
        aligned = jnp.take(blocked, gene_order.astype(jnp.int32), axis=1).reshape(CELLS, G)
        predicted_expression = low_back(jnp.dot(shares_low.T, aligned, precision=FULL_ACCURACY))
        inverse_predicted_norm = lax.rsqrt(lax.optimization_barrier(jnp.sum(predicted_expression * predicted_expression, axis=1)) + STABILITY_FLOOR)
        inverse_measured_norm = lax.rsqrt(lax.optimization_barrier(jnp.sum(measured_expression * measured_expression, axis=1)) + STABILITY_FLOOR)
        spot_cosine_score = lax.optimization_barrier(jnp.sum(predicted_expression * measured_expression, axis=1)) * inverse_predicted_norm * inverse_measured_norm
        spot_total = jnp.sum(weight_factor * spot_cosine_score)
        gene_inner_product = jnp.dot(group_members.T, predicted_expression * measured_expression, precision=FULL_ACCURACY)
        gene_predicted_norm = jnp.dot(group_members.T, predicted_expression * predicted_expression, precision=FULL_ACCURACY)
        gene_measured_norm = jnp.dot(group_members.T, measured_expression * measured_expression, precision=FULL_ACCURACY)
        gene_cosine_score = gene_inner_product * lax.rsqrt(gene_predicted_norm + STABILITY_FLOOR) * lax.rsqrt(gene_measured_norm + STABILITY_FLOOR)
        gene_total = jnp.sum(tally / G * lax.optimization_barrier(jnp.sum(gene_cosine_score, axis=1)))
        mass = jnp.dot(group_members.T, shares.T, precision=FULL_ACCURACY)
        quota = mass / tally[:, None]
        diverge = lax.optimization_barrier(jnp.sum(prior[None, :] * (jnp.log(prior)[None, :] - jnp.log(quota)), axis=1))
        density_total = jnp.sum(tally * diverge)
        objective = -spot_total - gene_total + density_total
        return (objective, (spot_total / total, gene_total / total, density_total / total))
    objective, pullback, terms = jax.vjp(forward, map_logits.astype(jnp.float32), single_cell.astype(jnp.float32), has_aux=True)
    grad_scores, grad_cells = pullback(jnp.float32(1.0))
    loss_terms = jnp.stack([terms[0], terms[1], terms[2]])
    return (loss_terms, grad_scores * float(CELLS), grad_cells * float(CELLS) ** 0.5)
```

```python
import functools

import jax
import jax.numpy as jnp
from jax import lax
from jax.experimental import pallas as pl
from jax.experimental.pallas import tpu as pltpu
from jax.sharding import Mesh, PartitionSpec as P

SLIDES = 3
FLOOR = 1e-06
F32 = jnp.float32
BF16 = jnp.bfloat16
AXES = ("z", "x", "c", "y")
MESH_ID = pl.DeviceIdType.MESH


def flip(value, mask):
    bit = 1
    while bit <= mask:
        if mask & bit:
            value = value + (1 - 2 * ((value // bit) % 2)) * bit
        bit *= 2
    return value


class Sizes:
    def __init__(self, mesh, cells, genes, spots, blocks):
        n = mesh.shape["spot"] // 2
        zs = 1
        while zs * zs * 4 <= 2 * n:
            zs *= 2
        self.Z, self.X, self.Y = zs, n // zs, mesh.shape["grp"]
        assert self.Y == 2 and self.Z * self.X == n and self.Z >= 2
        self.LV = self.Z.bit_length() - 1
        self.A = 2 * self.Z
        self.Q = self.X * self.Y
        self.CELLS, self.G, self.S, self.NB = cells, genes, spots, blocks
        self.R = cells // (self.A * self.Q)
        self.H = self.R // 2
        self.YR = self.Y * self.R
        self.NC = self.X * self.YR
        self.GA = genes // self.A
        self.RC = min(256, self.YR)
        self.NN = min(512, genes)


def kernel(k, logits, logits_flat, own_cells, spatial, ids, mask, cell_prior, order,
           out_map, out_single, out_loss,
           lbuf, cells, slow, slow_t, ybuf, info, info2,
           pacc, p1, psib, rs_out, rs_in, pred, meas,
           gp, gsend, grecv,
           mass_out, mass_in, ratio_hl, mext, dpart, din,
           stat, s1, ubuf, s2, wall,
           loc_sem, lg_s, lg_r, cl_s, cl_r, in_s, in_r, ps_s, ps_r, rs_s, rs_r, ms_s, ms_r,
           d_s, d_r, s1_s, s1_r, s2_s, s2_r, s3_s, s3_r, gz_s, gz_r, gc_s, gc_r, i2_s, i2_r,
           y_s, y_r, gs_s, gs_r):
    Z, X, Y, A, Q, S, G, R, H = k.Z, k.X, k.Y, k.A, k.Q, k.S, k.G, k.R, k.H
    YR, NC, GA, RC, NN = k.YR, k.NC, k.GA, k.RC, k.NN
    z, x, c, y = [lax.axis_index(a) for a in AXES]
    yo = 1 - y

    def group(m, e):
        return (flip(z, m), x, flip(c, e), y)

    def plane(dx, dy):
        return (z, lax.rem(x + dx, X), c, flip(y, dy))

    def remote(src, dst, send, recv, where):
        return pltpu.make_async_remote_copy(
            src_ref=src, dst_ref=dst, send_sem=send, recv_sem=recv,
            device_id=where, device_id_type=MESH_ID)

    groups = [(m, e) for m in range(Z) for e in range(2) if (m, e) != (0, 0)]
    planes = [(dx, dy) for dx in range(X) for dy in range(Y) if (dx, dy) != (0, 0)]
    me = z * 2 + c
    pending = []

    cp_flat = pltpu.make_async_copy(logits_flat, ybuf, loc_sem.at[0])
    cp_flat.start()
    cp_own = pltpu.make_async_copy(logits.at[z, :, c], lbuf.at[0, 0], loc_sem.at[1])
    cp_own.start()
    cp_cells = pltpu.make_async_copy(
        own_cells, cells.at[pl.ds(pl.multiple_of((x * Y + y) * R, R), R)], loc_sem.at[2])
    cp_cells.start()
    barrier = pltpu.get_barrier_semaphore()
    for m, e in groups:
        pl.semaphore_signal(barrier, inc=1, device_id=group(m, e), device_id_type=MESH_ID)
    for dx, dy in planes:
        pl.semaphore_signal(barrier, inc=1, device_id=plane(dx, dy), device_id_type=MESH_ID)
    pl.semaphore_wait(barrier, len(groups) + len(planes))

    def rows(bx, by, half):
        return cells.at[pl.ds(pl.multiple_of(((bx * Y + by) * 2 + half) * H, H), H)]

    XN = X - 1

    def cell_copy(slot, src, bx, by, half, where):
        return remote(src, rows(bx, by, half), cl_s.at[slot], cl_r.at[slot], where)

    own_half = [own_cells.at[pl.ds(0, H)], own_cells.at[pl.ds(H, H)]]
    x_first = [cell_copy(d, own_half[0], x, y, 0, plane(d + 1, 0)) for d in range(XN)]
    x_last = [cell_copy(XN + d, own_half[1], x, y, 1, plane(d + 1, 0)) for d in range(XN)]
    y_first = cell_copy(2 * XN, own_half[1], x, y, 1, plane(0, 1))
    y_last = cell_copy(2 * XN + 1, own_half[0], x, y, 0, plane(0, 1))
    for cp in x_first + [y_first]:
        cp.start()

    lg = {}

    def send_logits(m, e):
        cp = remote(logits.at[flip(z, m), :, flip(c, e)], lbuf.at[m, e],
                    lg_s.at[m, e], lg_r.at[m, e], group(m, e))
        cp.start()
        lg[m, e] = cp
        pending.append(cp)

    high = Z // 2
    far = [m for m in range(Z) if m & high and m != high]
    near = [m for m in range(1, Z) if not m & high]
    for m in far + near + [high]:
        for e in range(2):
            send_logits(m, e)
    send_logits(0, 1)
    for cp in x_last + [y_last]:
        cp.start()
    pending.extend(x_first + x_last + [y_first, y_last])

    cp_flat.wait()

    def add_exp(i, acc):
        e = jnp.exp(ybuf[i].astype(F32))
        return acc + jnp.sum(e.reshape(YR // 8, 8, S), axis=0)

    acc = lax.fori_loop(0, A * X, add_exp, jnp.zeros((8, S), F32))
    inv_sum = 1.0 / jnp.sum(acc, axis=0, keepdims=True)
    idr = ids[...]
    maskf = mask[...].astype(F32)
    mrow = [jnp.where(idr == s, maskf, 0.0) for s in range(SLIDES)]
    info[0, 0] = jnp.concatenate([inv_sum] + mrow + [jnp.zeros((8 - 1 - SLIDES, S), F32)], axis=0)
    inf = {}
    for m, e in groups:
        inf[m, e] = remote(info.at[0, 0], info.at[m, e], in_s.at[m, e], in_r.at[m, e], group(m, e))
        inf[m, e].start()
        pending.append(inf[m, e])

    W = G // k.NB
    for b in range(k.NB):
        v = jnp.zeros((S, W), F32)
        for j in range(k.NB):
            here = (order[0:1, j:j + 1] == b).astype(F32)
            v = v + here * spatial[:, j * W:(j + 1) * W].astype(F32)
        meas[:, b * W:(b + 1) * W] = v.astype(BF16)
    mcols = jnp.concatenate(mrow + [maskf] + [jnp.zeros((8 - 1 - SLIDES, S), F32)], axis=0).T
    mcol = [mcols[:, s:s + 1] for s in range(SLIDES)]
    wcol = mcols[:, SLIDES:SLIDES + 1]
    meas_sq = jnp.zeros((S, 1), F32)
    for j in range(A):
        v = meas[:, j * GA:(j + 1) * GA].astype(F32)
        v = v * v
        meas_sq = meas_sq + jnp.sum(v, axis=1, keepdims=True)
        for s in range(SLIDES):
            stat[j, 6 + s:7 + s, :] = jnp.sum(mcol[s] * v, axis=0, keepdims=True)
    inv_meas = lax.rsqrt(meas_sq + FLOOR)

    fwd_a, fwd_b = [], []
    for d in range(XN):
        bx = lax.rem(x - (d + 1) + X, X)
        cell_copy(d, own_half[0], bx, y, 0, plane(d + 1, 0)).wait_recv()
        cp = cell_copy(2 * XN + 2 + d, rows(bx, y, 0), bx, y, 0, plane(0, 1))
        cp.start()
        fwd_a.append(cp)
    y_first.wait_recv()
    for d in range(XN):
        cp = cell_copy(3 * XN + 2 + d, rows(x, yo, 1), x, yo, 1, plane(d + 1, 0))
        cp.start()
        fwd_b.append(cp)
    pending.extend(fwd_a + fwd_b)

    cp_own.wait()
    cp_cells.wait()

    def shares_of(m, e, i):
        per = YR // RC
        l = lbuf[m, e, i // per, pl.ds(pl.multiple_of(lax.rem(i, per) * RC, RC), RC), :]
        return jnp.exp(l.astype(F32)) * info[m, e, 0:1, :]

    def make_shares(m):
        for e in range(2):
            if (m, e) != (0, 0):
                inf[m, e].wait_recv()
                lg[m, e].wait_recv()
        for e in range(2):
            lane = (m * 2 + e) * S

            def step(i, _):
                sh = shares_of(m, e, i)
                r0 = pl.multiple_of(i * RC, RC)
                slow[pl.ds(r0, RC), lane:lane + S] = sh.astype(BF16)
                slow_t[e * S:(e + 1) * S, pl.ds(r0, RC)] = sh.T.astype(BF16)
                return 0

            lax.fori_loop(0, NC // RC, step, 0)

    def predict(m):
        def step(i, _):
            lanes = pl.ds(pl.multiple_of(i * NN, NN), NN)
            r = jnp.dot(slow_t[...], cells[:, lanes], preferred_element_type=F32)
            pacc[m, :, lanes] = r[:S]
            p1[m, :, lanes] = r[S:].astype(BF16)
            return 0

        lax.fori_loop(0, G // NN, step, 0)
        cp = remote(p1.at[m], psib.at[m], ps_s.at[m], ps_r.at[m], group(0, 1))
        cp.start()
        pending.append(cp)
        return cp

    ps = {}
    first = True
    for m in far + near + [0, high] if Z > 2 else [0, high]:
        make_shares(m)
        if first:
            for cp in x_last + [y_last] + fwd_a + fwd_b:
                cp.wait_recv()
            first = False
        ps[m] = predict(m)

    rs = {}

    def level_slot(b, m):
        return sum(Z >> (j + 1) for j in range(b)) + (m >> (b + 1))

    def piece_sum(m, b):
        cps = [rs[j, m] for j in range(b)]
        ps[m].wait_recv()
        for cp in cps:
            cp.wait_recv()

        def total(lanes):
            t = pacc[m, :, lanes] + psib[m, :, lanes].astype(F32)
            for j in range(b):
                t = t + rs_in[level_slot(j, m), :, lanes].astype(F32)
            return t
        return total

    for b in range(k.LV):
        step_m = 1 << b
        ms = [m for m in range(step_m, Z, 2 * step_m)]
        for m in reversed(ms):
            total = piece_sum(m, b)
            slot = level_slot(b, m ^ step_m)
            rs_out[slot] = total(slice(0, G)).astype(BF16)
            cp = remote(rs_out.at[slot], rs_in.at[slot], rs_s.at[slot], rs_r.at[slot],
                        group(step_m, 0))
            cp.start()
            rs[b, m ^ step_m] = cp
            pending.append(cp)

    mem_rows = jnp.concatenate(
        [info[m, e, 1:1 + SLIDES, :] for m in range(Z) for e in range(2)], axis=1)
    mem16 = jnp.concatenate([mem_rows, jnp.zeros((16 - SLIDES, A * S), F32)], axis=0).astype(BF16)
    part = lax.dot_general(mem16, slow[...], (((1,), (1,)), ((), ())), preferred_element_type=F32)
    col_tally = jnp.sum(mem_rows, axis=1, keepdims=True)
    mass_out[...] = jnp.concatenate(
        [part[:SLIDES], jnp.broadcast_to(col_tally, (SLIDES, NC)), jnp.zeros((2, NC), F32)], axis=0)
    mcp = []
    for i, (dx, dy) in enumerate(planes):
        cp = remote(mass_out, mass_in.at[i], ms_s.at[i], ms_r.at[i], plane(dx, dy))
        cp.start()
        mcp.append(cp)
    pending.extend(mcp)
    for cp in mcp:
        cp.wait_recv()
    msum = mass_out[...]
    for i in range(Q - 1):
        msum = msum + mass_in[i]
    mass = msum[:SLIDES]
    tally = jnp.maximum(msum[SLIDES:2 * SLIDES, 0:1], 1.0)
    quota = mass / tally
    prior_sum = jnp.sum(jnp.sum(cell_prior[...], axis=0, keepdims=True), axis=1, keepdims=True)
    prior = jnp.concatenate(
        [cell_prior[pl.ds((z * X + bx) * 2 + c, 1), :] for bx in range(X)], axis=1) / prior_sum
    kl = jnp.sum(prior * (jnp.log(prior) - jnp.log(quota)), axis=1, keepdims=True)
    rat = prior / quota
    rat_hi = rat.astype(BF16)
    rat_lo = (rat - rat_hi.astype(F32)).astype(BF16)
    ratio_hl[...] = jnp.concatenate(
        [rat_hi, rat_lo, jnp.zeros((16 - 2 * SLIDES, NC), BF16)], axis=0)
    dd = jnp.dot(ratio_hl[...], slow[...], preferred_element_type=F32)
    dd = dd[:SLIDES] + dd[SLIDES:2 * SLIDES]
    dsum = jnp.sum(dd * mem_rows, axis=0, keepdims=True)
    mext[...] = jnp.concatenate(
        [mem_rows, mem_rows, jnp.zeros((16 - 2 * SLIDES, A * S), F32)], axis=0).astype(BF16)
    dcp = {}
    for m in range(Z):
        for e in range(2):
            lane = (m * 2 + e) * S
            dpart[m, e] = jnp.broadcast_to(dsum[:, lane:lane + S], (8, S))
    for m, e in groups:
        cp = remote(dpart.at[m, e], din.at[m, e], d_s.at[m, e], d_r.at[m, e], group(m, e))
        cp.start()
        dcp[m, e] = cp
        pending.append(cp)

    total = piece_sum(0, k.LV)
    pred_sq = jnp.zeros((S, 1), F32)
    pred_meas = jnp.zeros((S, 1), F32)
    lane_id = lax.broadcasted_iota(jnp.int32, (1, GA), 1)
    for j in range(A):
        lanes = slice(j * GA, (j + 1) * GA)
        p = total(lanes)
        pred[:, lanes] = p
        q = meas[:, lanes].astype(F32)
        pq, pp = p * q, p * p
        pred_sq = pred_sq + jnp.sum(pp, axis=1, keepdims=True)
        pred_meas = pred_meas + jnp.sum(pq, axis=1, keepdims=True)
        for s in range(SLIDES):
            stat[j, s:s + 1, :] = jnp.sum(mcol[s] * pq, axis=0, keepdims=True)
            stat[j, 3 + s:4 + s, :] = jnp.sum(mcol[s] * pp, axis=0, keepdims=True)
    inv_pred = lax.rsqrt(pred_sq + FLOOR)
    spot_cos = pred_meas * inv_pred * inv_meas
    spot_sum = jnp.sum(wcol * spot_cos, axis=0, keepdims=True)
    scal = jnp.where(lane_id == 0, spot_sum, 0.0)
    for s in range(SLIDES):
        scal = scal + jnp.where(lane_id == 1 + s, kl[s:s + 1] * (1.0 / Q), 0.0)
    for j in range(A):
        stat[j, 9:16, :] = jnp.concatenate([scal, jnp.zeros((6, GA), F32)], axis=0)

    cps = {}
    for m, e in groups:
        cp = remote(stat.at[flip(z, m) * 2 + flip(c, e)], s1.at[m, e],
                    s1_s.at[m, e], s1_r.at[m, e], group(m, e))
        cp.start()
        cps[m, e] = cp
        pending.append(cp)
    u = stat[me]
    for m, e in groups:
        cps[m, e].wait_recv()
        u = u + s1[m, e]
    ubuf[...] = u
    cps = []
    for i, (dx, dy) in enumerate(planes):
        cp = remote(ubuf, s2.at[i], s2_s.at[i], s2_r.at[i], plane(dx, dy))
        cp.start()
        cps.append(cp)
        pending.append(cp)
    for i, cp in enumerate(cps):
        cp.wait_recv()
        u = u + s2[i]
    share = tally * (1.0 / G)
    a = lax.rsqrt(u[3:6] + FLOOR)
    b = lax.rsqrt(u[6:9] + FLOOR)
    gcos = u[0:3] * a * b
    wall[me] = jnp.concatenate(
        [share * a * b, share * gcos * a * a,
         jnp.sum(share * gcos, axis=0, keepdims=True), jnp.zeros((1, GA), F32), u[8:16]], axis=0)
    cps = []
    for m, e in groups:
        cp = remote(wall.at[me], wall.at[me], s3_s.at[m, e], s3_r.at[m, e], group(m, e))
        cp.start()
        cps.append(cp)
        pending.append(cp)
    for (m, e) in groups:
        other = flip(z, m) * 2 + flip(c, e)
        remote(wall.at[other], wall.at[other], s3_s.at[m, e], s3_r.at[m, e], group(m, e)).wait_recv()

    lead = -(wcol * inv_pred * inv_meas)
    back = wcol * spot_cos * inv_pred * inv_pred
    dot1 = jnp.zeros((S, 1), F32)
    gene_total = jnp.zeros((1, GA), F32)
    for j in range(A):
        lanes = slice(j * GA, (j + 1) * GA)
        w = wall[j]
        direct = mcol[0] * w[0:1] + mcol[1] * w[1:2] + mcol[2] * w[2:3]
        damp = mcol[0] * w[3:4] + mcol[1] * w[4:5] + mcol[2] * w[5:6]
        gene_total = gene_total + w[6:7]
        p = pred[:, lanes]
        g = (lead - direct) * meas[:, lanes].astype(F32) + (back + damp) * p
        glow = g.astype(BF16)
        gp[0, 0, :, lanes] = glow
        dot1 = dot1 + jnp.sum(glow.astype(F32) * p, axis=1, keepdims=True)

    gz, gc = {}, {}

    def to_core(m):
        cp = remote(gp.at[m, 0], gp.at[m, 1], gc_s.at[m], gc_r.at[m], group(0, 1))
        cp.start()
        gc[m] = cp
        pending.append(cp)

    def to_plane(m, b):
        t = m ^ (1 << b)
        cp = remote(gp.at[m, 0], gp.at[t, 0], gz_s.at[t], gz_r.at[t], group(1 << b, 0))
        cp.start()
        gz[t] = cp
        pending.append(cp)

    for b in reversed(range(k.LV)):
        to_plane(0, b)
    to_core(0)

    for m, e in groups:
        dcp[m, e].wait_recv()
    dtot = dpart[0, 0]
    for m, e in groups:
        dtot = dtot + din[m, e]
    dot_row = jnp.broadcast_to(dot1, (S, S)).T[0:8] - dtot
    info2[0, 0] = dot_row
    i2 = {}
    for m, e in groups:
        cp = remote(info2.at[0, 0], info2.at[m, e], i2_s.at[m, e], i2_r.at[m, e], group(m, e))
        cp.start()
        i2[m, e] = cp
        pending.append(cp)

    fin = wall[0]
    total_tally = jnp.sum(tally, axis=0, keepdims=True)
    gsum = jnp.sum(gene_total, axis=1, keepdims=True)
    dens = jnp.zeros((1, 1), F32)
    for s in range(SLIDES):
        dens = dens + tally[s:s + 1] * fin[9:10, 1 + s:2 + s]
    lid = lax.broadcasted_iota(jnp.int32, (8, 128), 1)
    out_loss[...] = (jnp.where(lid == 0, fin[9:10, 0:1], 0.0) + jnp.where(lid == 1, gsum, 0.0)
                     + jnp.where(lid == 2, dens, 0.0)) / total_tally

    ycp = {}

    def map_piece(m):
        for e in range(2):
            if (m, e) != (0, 0):
                i2[m, e].wait_recv()
        gpm = gp.at[m]

        def step(i, _):
            r0 = pl.multiple_of(i * RC, RC)
            low = lax.dot_general(cells[pl.ds(r0, RC), :], gpm[...].reshape(2 * S, G),
                                  (((1,), (1,)), ((), ())), preferred_element_type=F32)
            rt = lax.dot_general(ratio_hl[:, pl.ds(r0, RC)], mext[:, m * 2 * S:(m + 1) * 2 * S],
                                 (((0,), (0,)), ((), ())), preferred_element_type=F32)
            low = low - rt
            per = YR // RC
            for e in range(2):
                sh = shares_of(m, e, i) * float(k.CELLS)
                v = sh * (low[:, e * S:(e + 1) * S] - info2[m, e, 0:1, :])
                ybuf[(m * 2 + e) * X + i // per,
                     pl.ds(pl.multiple_of(lax.rem(i, per) * RC, RC), RC), :] = v.astype(BF16)
            return 0

        lax.fori_loop(0, NC // RC, step, 0)
        for e in range(2):
            src = ybuf.at[pl.ds((m * 2 + e) * X, X)]
            if (m, e) == (0, 0):
                cp = pltpu.make_async_copy(src, out_map.at[z, :, c], loc_sem.at[3])
                cp.start()
                ycp[m, e] = cp
            else:
                cp = remote(src, out_map.at[z, :, c], y_s.at[m, e], y_r.at[m, e], group(m, e))
                cp.start()
                ycp[m, e] = cp
                pending.append(cp)

    gc[0].wait_recv()
    map_piece(0)
    held = [0, high]
    for b in reversed(range(k.LV)):
        for m in range(1 << b, Z, 2 << b):
            gz[m].wait_recv()
            for b2 in reversed(range(b)):
                to_plane(m, b2)
            to_core(m)
    for m in [high] + far:
        gc[m].wait_recv()
        map_piece(m)

    for m in near:
        gc[m].wait_recv()

    def slot_of(dx, dy, half):
        return ((dx * Y + dy) - 1) * 2 + half

    def single_rows(dx, dy, half):
        bx = lax.rem(x + dx, X)
        by = flip(y, dy)
        return pl.multiple_of(((bx * Y + by) * 2 + half) * H, H)

    def single_part(dx, dy, half, put):
        r0 = single_rows(dx, dy, half)

        def step(i, _):
            lanes = pl.ds(pl.multiple_of(i * NN, NN), NN)
            v = jnp.dot(slow[pl.ds(r0, H), :], gp[:, :, :, lanes].reshape(A * S, NN),
                        preferred_element_type=F32)
            put(lanes, v)
            return 0

        lax.fori_loop(0, G // NN, step, 0)

    def put_send(slot, extra=()):
        def put(lanes, v):
            for i in extra:
                v = v + grecv[i, :, lanes].astype(F32)
            gsend[slot, :, lanes] = v.astype(BF16)
        return put

    r_m1 = lambda d: d
    r_m2 = lambda d: XN + d
    r_m3 = lambda d: 2 * XN + d
    r_m5 = lambda d: 3 * XN + d
    r_m4, r_m6 = 4 * XN, 4 * XN + 1
    gcp = {}

    def send_single(slot, r_slot, where):
        cp = remote(gsend.at[slot], grecv.at[r_slot], gs_s.at[r_slot], gs_r.at[r_slot], where)
        cp.start()
        gcp[r_slot] = cp
        pending.append(cp)

    for d in range(XN):
        s0, s1_ = slot_of(d + 1, 1, 0), slot_of(d + 1, 1, 1)
        single_part(d + 1, 1, 0, put_send(s0))
        send_single(s0, r_m1(d), plane(d + 1, 0))
        single_part(d + 1, 1, 1, put_send(s1_))
        send_single(s1_, r_m2(d), plane(0, 1))
    for d in range(XN):
        s0 = slot_of(d + 1, 0, 0)
        single_part(d + 1, 0, 0, put_send(s0))
        send_single(s0, r_m3(d), plane(d + 1, 0))
    s0 = slot_of(0, 1, 1)
    single_part(0, 1, 1, put_send(s0))
    send_single(s0, r_m4, plane(0, 1))

    for m in near:
        map_piece(m)

    for d in range(XN):
        gcp[r_m2(d)].wait_recv()
        s0 = slot_of(d + 1, 0, 1)
        single_part(d + 1, 0, 1, put_send(s0, [r_m2(d)]))
        send_single(s0, r_m5(d), plane(d + 1, 0))
    for d in range(XN):
        gcp[r_m1(d)].wait_recv()
    s0 = slot_of(0, 1, 0)
    single_part(0, 1, 0, put_send(s0, [r_m1(d) for d in range(XN)]))
    send_single(s0, r_m6, plane(0, 1))

    def put_own(half):
        def put(lanes, v):
            out_single[half * H:(half + 1) * H, lanes] = v
        return put

    for half in range(2):
        single_part(0, 0, half, put_own(half))
    halves = [[r_m3(d) for d in range(XN)] + [r_m6], [r_m5(d) for d in range(XN)] + [r_m4]]
    for half in range(2):
        for i in halves[half]:
            gcp[i].wait_recv()

        def step(i, _):
            lanes = pl.ds(pl.multiple_of(i * NN, NN), NN)
            v = out_single[half * H:(half + 1) * H, lanes]
            for i2_ in halves[half]:
                v = v + grecv[i2_, :, lanes].astype(F32)
            out_single[half * H:(half + 1) * H, lanes] = v
            return 0

        lax.fori_loop(0, G // NN, step, 0)

    for m, e in groups:
        other = (flip(z, m), slice(None), flip(c, e))
        remote(ybuf.at[pl.ds(0, X)], out_map.at[other[0], :, other[2]], y_s.at[m, e], y_r.at[m, e],
               group(m, e)).wait_recv()
    ycp[0, 0].wait()
    for cp in pending:
        cp.wait_send()


def forward_and_back(k, logits, single_cell, spatial, ids, mask, cell_prior, order):
    Z, X, Y, A, Q, S, G, R, H = k.Z, k.X, k.Y, k.A, k.Q, k.S, k.G, k.R, k.H
    YR, NC, GA, XN = k.YR, k.NC, k.GA, k.X - 1
    vm = pl.BlockSpec(memory_space=pltpu.VMEM)
    hbm = pl.BlockSpec(memory_space=pl.ANY)
    dma = lambda *s: pltpu.SemaphoreType.DMA(s)
    ncl, ngs = 4 * XN + 2, 4 * XN + 2
    scratch = [
        pltpu.VMEM((Z, 2, X, YR, S), BF16),
        pltpu.VMEM((NC, G), BF16),
        pltpu.VMEM((NC, A * S), BF16),
        pltpu.VMEM((2 * S, NC), BF16),
        pltpu.VMEM((A * X, YR, S), BF16),
        pltpu.VMEM((Z, 2, 8, S), F32),
        pltpu.VMEM((Z, 2, 8, S), F32),
        pltpu.VMEM((Z, S, G), F32),
        pltpu.VMEM((Z, S, G), BF16),
        pltpu.VMEM((Z, S, G), BF16),
        pltpu.VMEM((Z - 1, S, G), BF16),
        pltpu.VMEM((Z - 1, S, G), BF16),
        pltpu.VMEM((S, G), F32),
        pltpu.VMEM((S, G), BF16),
        pltpu.VMEM((Z, 2, S, G), BF16),
        pltpu.VMEM((2 * (Q - 1), H, G), BF16),
        pltpu.VMEM((ngs, H, G), BF16),
        pltpu.VMEM((8, NC), F32),
        pltpu.VMEM((Q - 1, 8, NC), F32),
        pltpu.VMEM((16, NC), BF16),
        pltpu.VMEM((16, A * S), BF16),
        pltpu.VMEM((Z, 2, 8, S), F32),
        pltpu.VMEM((Z, 2, 8, S), F32),
        pltpu.VMEM((A, 16, GA), F32),
        pltpu.VMEM((Z, 2, 16, GA), F32),
        pltpu.VMEM((16, GA), F32),
        pltpu.VMEM((Q - 1, 16, GA), F32),
        pltpu.VMEM((A, 16, GA), F32),
        dma(4),
        dma(Z, 2), dma(Z, 2),
        dma(ncl), dma(ncl),
        dma(Z, 2), dma(Z, 2),
        dma(Z), dma(Z),
        dma(Z - 1), dma(Z - 1),
        dma(Q - 1), dma(Q - 1),
        dma(Z, 2), dma(Z, 2),
        dma(Z, 2), dma(Z, 2),
        dma(Q - 1), dma(Q - 1),
        dma(Z, 2), dma(Z, 2),
        dma(Z), dma(Z),
        dma(Z), dma(Z),
        dma(Z, 2), dma(Z, 2),
        dma(Z, 2), dma(Z, 2),
        dma(ngs), dma(ngs),
    ]
    return pl.pallas_call(
        functools.partial(kernel, k),
        name="mapping",
        out_shape=[
            jax.ShapeDtypeStruct((Z, X, 2, YR, S), BF16),
            jax.ShapeDtypeStruct((R, G), F32),
            jax.ShapeDtypeStruct((8, 128), F32),
        ],
        in_specs=[hbm, hbm, hbm, vm, vm, vm, vm, vm],
        out_specs=[hbm, vm, vm],
        scratch_shapes=scratch,
        compiler_params=pltpu.CompilerParams(
            collective_id=0, has_side_effects=True, vmem_limit_bytes=64000 * 1024),
        cost_estimate=pl.CostEstimate(
            flops=6 * NC * A * S * G, bytes_accessed=32 << 20, transcendentals=2 * NC * A * S),
    )(logits.reshape(Z, X, 2, YR, S), logits.reshape(A * X, YR, S), single_cell, spatial,
      ids.reshape(1, S), mask.reshape(1, S), cell_prior.reshape(A * X, YR), order.reshape(1, k.NB))


def body(mesh, map_logits, single_cell, spatial, slide_ids, spot_mask, cell_prior, gene_order):
    cells, spots = map_logits.shape
    k = Sizes(mesh, cells, spatial.shape[1], spots, gene_order.shape[0])
    gmap, gsingle, loss = forward_and_back(
        k, map_logits, single_cell, spatial, slide_ids, spot_mask, cell_prior, gene_order)
    grad_map = gmap.reshape(cells, spots).astype(F32)
    return loss[0, :3], grad_map, gsingle * float(cells) ** 0.5


def solution(mesh):
    k = Sizes(mesh, 1 << 20, 1 << 20, 128, 1)
    fine = Mesh(mesh.devices.reshape(k.Z, k.X, 2, k.Y), AXES)
    in_specs = (P(None, AXES), P(AXES, None), P(AXES, None), P(AXES), P(AXES), P(), P())
    out_specs = (P(), P(None, AXES), P(AXES, None))
    return jax.shard_map(functools.partial(body, mesh), mesh=fine, in_specs=in_specs,
                         out_specs=out_specs, check_vma=False)
```

```python
import functools

import jax
import jax.numpy as jnp
from jax import lax
from jax.experimental import pallas as pl
from jax.experimental.pallas import tpu as pltpu
from jax.sharding import Mesh, PartitionSpec as P

SLIDES = 3
FLOOR = 1e-06
F32 = jnp.float32
BF16 = jnp.bfloat16
AXES = ("z", "x", "c", "y")
MESH_ID = pl.DeviceIdType.MESH


def flip(value, mask):
    bit = 1
    while bit <= mask:
        if mask & bit:
            value = value + (1 - 2 * ((value // bit) % 2)) * bit
        bit *= 2
    return value


class Sizes:
    def __init__(self, mesh, cells, genes, spots, blocks):
        n = mesh.shape["spot"] // 2
        zs = 1
        while zs * zs * 4 <= 2 * n:
            zs *= 2
        self.Z, self.X, self.Y = zs, n // zs, mesh.shape["grp"]
        assert self.Y == 2 and self.Z * self.X == n and self.Z >= 2
        self.LV = self.Z.bit_length() - 1
        self.A = 2 * self.Z
        self.Q = self.X * self.Y
        self.CELLS, self.G, self.S, self.NB = cells, genes, spots, blocks
        self.R = cells // (self.A * self.Q)
        self.H = self.R // 2
        self.YR = self.Y * self.R
        self.NC = self.X * self.YR
        self.GA = genes // self.A
        self.RC = min(256, self.YR)
        self.PL = min(128, self.YR)
        self.NN = min(512, genes)


def kernel(k, logits, logits_flat, own_cells, spatial, ids, mask, cell_prior, order,
           out_map, out_single, out_loss,
           lbuf, cells, slow, slow_t, ybuf, info, info2,
           pacc, p1, psib, rs_out, rs_in, meas,
           gp, gsend, grecv,
           mass_out, mass_in, ratio_hl, mext, dpart, din,
           stat, s1, ubuf, s2, wall,
           loc_sem, lg_s, lg_r, cl_s, cl_r, in_s, in_r, ps_s, ps_r, rs_s, rs_r, ms_s, ms_r,
           d_s, d_r, s1_s, s1_r, s2_s, s2_r, s3_s, s3_r, gz_s, gz_r, gc_s, gc_r, i2_s, i2_r,
           y_s, y_r, gs_s, gs_r):
    Z, X, Y, A, Q, S, G, R, H = k.Z, k.X, k.Y, k.A, k.Q, k.S, k.G, k.R, k.H
    YR, NC, GA, RC, NN = k.YR, k.NC, k.GA, k.RC, k.NN
    z, x, c, y = [lax.axis_index(a) for a in AXES]
    yo = 1 - y

    def group(m, e):
        return (flip(z, m), x, c + e - 2 * c * e, y)

    def plane(dx, dy):
        return (z, lax.rem(x + dx, X), c, flip(y, dy))

    def remote(src, dst, send, recv, where):
        return pltpu.make_async_remote_copy(
            src_ref=src, dst_ref=dst, send_sem=send, recv_sem=recv,
            device_id=where, device_id_type=MESH_ID)

    groups = [(m, e) for m in range(Z) for e in range(2) if (m, e) != (0, 0)]
    planes = [(dx, dy) for dx in range(X) for dy in range(Y) if (dx, dy) != (0, 0)]
    me = z * 2 + c
    pending = []

    cp_flat = pltpu.make_async_copy(logits_flat, ybuf, loc_sem.at[0])
    cp_flat.start()
    cp_own = pltpu.make_async_copy(logits.at[z, :, c], lbuf.at[0, 0], loc_sem.at[1])
    cp_own.start()
    cp_cells = pltpu.make_async_copy(
        own_cells, cells.at[pl.ds(pl.multiple_of((x * Y + y) * R, R), R)], loc_sem.at[2])
    cp_cells.start()
    barrier = pltpu.get_barrier_semaphore()
    for m, e in groups:
        pl.semaphore_signal(barrier, inc=1, device_id=group(m, e), device_id_type=MESH_ID)
    for dx, dy in planes:
        pl.semaphore_signal(barrier, inc=1, device_id=plane(dx, dy), device_id_type=MESH_ID)
    pl.semaphore_wait(barrier, len(groups) + len(planes))

    def rows(bx, by, half):
        return cells.at[pl.ds(pl.multiple_of(((bx * Y + by) * 2 + half) * H, H), H)]

    XN = X - 1

    def cell_copy(slot, src, bx, by, half, where):
        return remote(src, rows(bx, by, half), cl_s.at[slot], cl_r.at[slot], where)

    own_half = [own_cells.at[pl.ds(0, H)], own_cells.at[pl.ds(H, H)]]
    x_first = [cell_copy(d, own_half[0], x, y, 0, plane(d + 1, 0)) for d in range(XN)]
    x_last = [cell_copy(XN + d, own_half[1], x, y, 1, plane(d + 1, 0)) for d in range(XN)]
    y_first = cell_copy(2 * XN, own_half[1], x, y, 1, plane(0, 1))
    y_last = cell_copy(2 * XN + 1, own_half[0], x, y, 0, plane(0, 1))
    for cp in x_first + [y_first]:
        cp.start()

    lg = {}

    def send_logits(m, e):
        cp = remote(logits.at[flip(z, m), :, flip(c, e)], lbuf.at[m, e],
                    lg_s.at[m, e], lg_r.at[m, e], group(m, e))
        cp.start()
        lg[m, e] = cp
        pending.append(cp)

    high = Z // 2
    far = [m for m in range(Z) if m & high and m != high]
    near = [m for m in range(1, Z) if not m & high]
    send_logits(0, 1)
    for m in far + near + [high]:
        for e in range(2):
            send_logits(m, e)
    for cp in x_last + [y_last]:
        cp.start()
    pending.extend(x_first + x_last + [y_first, y_last])

    cp_flat.wait()

    def add_exp(i, acc):
        e = jnp.exp(ybuf[i].astype(F32))
        return acc + jnp.sum(e.reshape(YR // 8, 8, S), axis=0)

    acc = lax.fori_loop(0, A * X, add_exp, jnp.zeros((8, S), F32))
    inv_sum = 1.0 / jnp.sum(acc, axis=0, keepdims=True)
    idr = ids[...]
    maskf = mask[...].astype(F32)
    mrow = [jnp.where(idr == s, maskf, 0.0) for s in range(SLIDES)]
    info[0, 0] = jnp.concatenate([inv_sum] + mrow + [jnp.zeros((8 - 1 - SLIDES, S), F32)], axis=0)
    inf = {}
    for m, e in groups:
        inf[m, e] = remote(info.at[0, 0], info.at[m, e], in_s.at[m, e], in_r.at[m, e], group(m, e))
        inf[m, e].start()
        pending.append(inf[m, e])

    W = G // k.NB
    for b in range(k.NB):
        v = jnp.zeros((S, W), F32)
        for j in range(k.NB):
            here = (order[0:1, j:j + 1] == b).astype(F32)
            v = v + here * spatial[:, j * W:(j + 1) * W].astype(F32)
        meas[:, b * W:(b + 1) * W] = v.astype(BF16)
    mcols = jnp.concatenate(mrow + [maskf] + [jnp.zeros((8 - 1 - SLIDES, S), F32)], axis=0).T
    mcol = [mcols[:, s:s + 1] for s in range(SLIDES)]
    wcol = mcols[:, SLIDES:SLIDES + 1]
    meas_sq = jnp.zeros((S, 1), F32)
    for j in range(A):
        v = meas[:, j * GA:(j + 1) * GA].astype(F32)
        v = v * v
        meas_sq = meas_sq + jnp.sum(v, axis=1, keepdims=True)
        for s in range(SLIDES):
            stat[j, 6 + s:7 + s, :] = jnp.sum(mcol[s] * v, axis=0, keepdims=True)
    inv_meas = lax.rsqrt(meas_sq + FLOOR)

    fwd_a, fwd_b = [], []
    for d in range(XN):
        bx = lax.rem(x - (d + 1) + X, X)
        cell_copy(d, own_half[0], bx, y, 0, plane(d + 1, 0)).wait_recv()
        cp = cell_copy(2 * XN + 2 + d, rows(bx, y, 0), bx, y, 0, plane(0, 1))
        cp.start()
        fwd_a.append(cp)
    y_first.wait_recv()
    for d in range(XN):
        cp = cell_copy(3 * XN + 2 + d, rows(x, yo, 1), x, yo, 1, plane(d + 1, 0))
        cp.start()
        fwd_b.append(cp)
    pending.extend(fwd_a + fwd_b)

    cp_own.wait()
    cp_cells.wait()

    def shares_of(m, e, i):
        per = YR // RC
        l = lbuf[m, e, i // per, pl.ds(pl.multiple_of(lax.rem(i, per) * RC, RC), RC), :]
        return jnp.exp(l.astype(F32)) * info[m, e, 0:1, :]

    def t_row(m, e):
        m = 0 if m == high else m - (m > high)
        return (m * 2 + e) * S

    def make_shares(m):
        for e in range(2):
            if (m, e) != (0, 0):
                inf[m, e].wait_recv()
                lg[m, e].wait_recv()
        for e in range(2):
            lane = (m * 2 + e) * S

            def step(i, _):
                sh = shares_of(m, e, i)
                r0 = pl.multiple_of(i * RC, RC)
                slow[pl.ds(r0, RC), lane:lane + S] = sh.astype(BF16)
                slow_t[t_row(m, e):t_row(m, e) + S, pl.ds(r0, RC)] = sh.astype(BF16).T
                return 0

            lax.fori_loop(0, NC // RC, step, 0)

    def predict(m):
        def step(i, _):
            lanes = pl.ds(pl.multiple_of(i * NN, NN), NN)
            r = jnp.dot(slow_t[t_row(m, 0):t_row(m, 0) + 2 * S, :], cells[:, lanes],
                        preferred_element_type=F32)
            pacc[m, :, lanes] = r[:S]
            p1[m, :, lanes] = r[S:].astype(BF16)
            return 0

        lax.fori_loop(0, G // NN, step, 0)
        cp = remote(p1.at[m], psib.at[m], ps_s.at[m], ps_r.at[m], group(0, 1))
        cp.start()
        pending.append(cp)
        return cp

    rs = {}

    def level_slot(b, m):
        return sum(Z >> (j + 1) for j in range(b)) + (m >> (b + 1))

    def piece_sum(m, b):
        cps = [rs[j, m] for j in range(b)]
        ps[m].wait_recv()
        for cp in cps:
            cp.wait_recv()

        def total(lanes):
            t = pacc[m, :, lanes] + psib[m, :, lanes].astype(F32)
            for j in range(b):
                t = t + rs_in[level_slot(j, m), :, lanes].astype(F32)
            return t
        return total

    def send_level(b):
        step_m = 1 << b
        for m in reversed(range(step_m, Z, 2 * step_m)):
            total = piece_sum(m, b)
            slot = level_slot(b, m ^ step_m)
            for j in range(A):
                lanes = slice(j * GA, (j + 1) * GA)
                rs_out[slot, :, lanes] = total(lanes).astype(BF16)
            cp = remote(rs_out.at[slot], rs_in.at[slot], rs_s.at[slot], rs_r.at[slot],
                        group(step_m, 0))
            cp.start()
            rs[b, m ^ step_m] = cp
            pending.append(cp)

    ps = {}
    for m in [0] + far + near:
        make_shares(m)
    for cp in x_last + [y_last] + fwd_a + fwd_b:
        cp.wait_recv()
    for b in range(k.LV):
        if b == k.LV - 1:
            ps[0] = predict(0)
            make_shares(high)
        for m in reversed(range(1 << b, Z, 2 << b)):
            ps[m] = predict(m)
        send_level(b)

    mem_rows = jnp.concatenate(
        [info[m, e, 1:1 + SLIDES, :] for m in range(Z) for e in range(2)], axis=1)
    mem16 = jnp.concatenate([mem_rows, jnp.zeros((16 - SLIDES, A * S), F32)], axis=0).astype(BF16)
    part = lax.dot_general(mem16, slow[...], (((1,), (1,)), ((), ())), preferred_element_type=F32)
    col_tally = jnp.sum(mem_rows, axis=1, keepdims=True)
    mass_out[...] = jnp.concatenate(
        [part[:SLIDES], jnp.broadcast_to(col_tally, (SLIDES, NC)), jnp.zeros((2, NC), F32)], axis=0)
    mcp = []
    for i, (dx, dy) in enumerate(planes):
        cp = remote(mass_out, mass_in.at[i], ms_s.at[i], ms_r.at[i], plane(dx, dy))
        cp.start()
        mcp.append(cp)
    pending.extend(mcp)
    for cp in mcp:
        cp.wait_recv()
    msum = mass_out[...]
    for i in range(Q - 1):
        msum = msum + mass_in[i]
    mass = msum[:SLIDES]
    tally = jnp.maximum(msum[SLIDES:2 * SLIDES, 0:1], 1.0)
    quota = mass / tally
    prior_sum = jnp.sum(jnp.sum(cell_prior[...], axis=0, keepdims=True), axis=1, keepdims=True)
    prior = jnp.concatenate(
        [cell_prior[pl.ds(((z * X + bx) * 2 + c) * (YR // k.PL) + i, 1), :]
         for bx in range(X) for i in range(YR // k.PL)], axis=1) / prior_sum
    kl = jnp.sum(prior * (jnp.log(prior) - jnp.log(quota)), axis=1, keepdims=True)
    rat = prior / quota
    rat_hi = rat.astype(BF16)
    rat_lo = (rat - rat_hi.astype(F32)).astype(BF16)
    ratio_hl[...] = jnp.concatenate(
        [rat_hi, rat_lo, jnp.zeros((16 - 2 * SLIDES, NC), BF16)], axis=0)
    dd = jnp.dot(ratio_hl[...], slow[...], preferred_element_type=F32)
    dd = dd[:SLIDES] + dd[SLIDES:2 * SLIDES]
    dsum = jnp.sum(dd * mem_rows, axis=0, keepdims=True)
    mext[...] = jnp.concatenate(
        [mem_rows, mem_rows, jnp.zeros((16 - 2 * SLIDES, A * S), F32)], axis=0).astype(BF16)
    dcp = {}
    for m in range(Z):
        for e in range(2):
            lane = (m * 2 + e) * S
            dpart[m, e] = jnp.broadcast_to(dsum[:, lane:lane + S], (8, S))
    for m, e in groups:
        cp = remote(dpart.at[m, e], din.at[m, e], d_s.at[m, e], d_r.at[m, e], group(m, e))
        cp.start()
        dcp[m, e] = cp
        pending.append(cp)

    total = piece_sum(0, k.LV)
    pred_sq = jnp.zeros((S, 1), F32)
    pred_meas = jnp.zeros((S, 1), F32)
    lane_id = lax.broadcasted_iota(jnp.int32, (1, GA), 1)
    for j in range(A):
        lanes = slice(j * GA, (j + 1) * GA)
        p = total(lanes)
        pacc[0, :, lanes] = p
        q = meas[:, lanes].astype(F32)
        pq, pp = p * q, p * p
        pred_sq = pred_sq + jnp.sum(pp, axis=1, keepdims=True)
        pred_meas = pred_meas + jnp.sum(pq, axis=1, keepdims=True)
        for s in range(SLIDES):
            stat[j, s:s + 1, :] = jnp.sum(mcol[s] * pq, axis=0, keepdims=True)
            stat[j, 3 + s:4 + s, :] = jnp.sum(mcol[s] * pp, axis=0, keepdims=True)
    inv_pred = lax.rsqrt(pred_sq + FLOOR)
    spot_cos = pred_meas * inv_pred * inv_meas
    spot_sum = jnp.sum(wcol * spot_cos, axis=0, keepdims=True)
    scal = jnp.where(lane_id == 0, spot_sum, 0.0)
    for s in range(SLIDES):
        scal = scal + jnp.where(lane_id == 1 + s, kl[s:s + 1] * (1.0 / Q), 0.0)
    for j in range(A):
        stat[j, 9:16, :] = jnp.concatenate([scal, jnp.zeros((6, GA), F32)], axis=0)

    cps = {}
    for m, e in groups:
        cp = remote(stat.at[flip(z, m) * 2 + flip(c, e)], s1.at[m, e],
                    s1_s.at[m, e], s1_r.at[m, e], group(m, e))
        cp.start()
        cps[m, e] = cp
        pending.append(cp)
    u = stat[me]
    for m, e in groups:
        cps[m, e].wait_recv()
        u = u + s1[m, e]
    ubuf[...] = u
    cps = []
    for i, (dx, dy) in enumerate(planes):
        cp = remote(ubuf, s2.at[i], s2_s.at[i], s2_r.at[i], plane(dx, dy))
        cp.start()
        cps.append(cp)
        pending.append(cp)
    for i, cp in enumerate(cps):
        cp.wait_recv()
        u = u + s2[i]
    share = tally * (1.0 / G)
    a = lax.rsqrt(u[3:6] + FLOOR)
    b = lax.rsqrt(u[6:9] + FLOOR)
    gcos = u[0:3] * a * b
    wall[me] = jnp.concatenate(
        [share * a * b, share * gcos * a * a,
         jnp.sum(share * gcos, axis=0, keepdims=True), jnp.zeros((1, GA), F32), u[8:16]], axis=0)
    cps = []
    for m, e in groups:
        cp = remote(wall.at[me], wall.at[me], s3_s.at[m, e], s3_r.at[m, e], group(m, e))
        cp.start()
        cps.append(cp)
        pending.append(cp)
    for (m, e) in groups:
        other = flip(z, m) * 2 + flip(c, e)
        remote(wall.at[other], wall.at[other], s3_s.at[m, e], s3_r.at[m, e], group(m, e)).wait_recv()

    lead = -(wcol * inv_pred * inv_meas)
    back = wcol * spot_cos * inv_pred * inv_pred
    dot1 = jnp.zeros((S, 1), F32)
    gene_total = jnp.zeros((1, GA), F32)
    for j in range(A):
        lanes = slice(j * GA, (j + 1) * GA)
        w = wall[j]
        direct = mcol[0] * w[0:1] + mcol[1] * w[1:2] + mcol[2] * w[2:3]
        damp = mcol[0] * w[3:4] + mcol[1] * w[4:5] + mcol[2] * w[5:6]
        gene_total = gene_total + w[6:7]
        p = pacc[0, :, lanes]
        g = (lead - direct) * meas[:, lanes].astype(F32) + (back + damp) * p
        glow = g.astype(BF16)
        gp[0, 0, :, lanes] = glow
        dot1 = dot1 + jnp.sum(glow.astype(F32) * p, axis=1, keepdims=True)

    gz, gc = {}, {}

    def to_core(m):
        cp = remote(gp.at[m, 0], gp.at[m, 1], gc_s.at[m], gc_r.at[m], group(0, 1))
        cp.start()
        gc[m] = cp
        pending.append(cp)

    def to_plane(m, b):
        t = m ^ (1 << b)
        cp = remote(gp.at[m, 0], gp.at[t, 0], gz_s.at[t], gz_r.at[t], group(1 << b, 0))
        cp.start()
        gz[t] = cp
        pending.append(cp)

    top = k.LV - 1
    to_core(0)
    gz[high] = remote(gp.at[0, 0], gp.at[high, 0], gz_s.at[high], gz_r.at[high], group(high, 0))
    pending.append(gz[high])

    @pl.when(c == 0)
    def _():
        gz[high].start()

    for b in reversed(range(top)):
        to_plane(0, b)

    for m, e in groups:
        dcp[m, e].wait_recv()
    dtot = dpart[0, 0]
    for m, e in groups:
        dtot = dtot + din[m, e]
    dot_row = jnp.broadcast_to(dot1, (S, S)).T[0:8] - dtot
    info2[0, 0] = dot_row
    i2 = {}
    for m, e in groups:
        cp = remote(info2.at[0, 0], info2.at[m, e], i2_s.at[m, e], i2_r.at[m, e], group(m, e))
        cp.start()
        i2[m, e] = cp
        pending.append(cp)

    fin = wall[0]
    total_tally = jnp.sum(tally, axis=0, keepdims=True)
    gsum = jnp.sum(gene_total, axis=1, keepdims=True)
    dens = jnp.zeros((1, 1), F32)
    for s in range(SLIDES):
        dens = dens + tally[s:s + 1] * fin[9:10, 1 + s:2 + s]
    lid = lax.broadcasted_iota(jnp.int32, (8, 128), 1)
    out_loss[...] = (jnp.where(lid == 0, fin[9:10, 0:1], 0.0) + jnp.where(lid == 1, gsum, 0.0)
                     + jnp.where(lid == 2, dens, 0.0)) / total_tally

    ycp = {}

    def map_rows(m, es, gpm):
        n = len(es)

        def step(i, _):
            r0 = pl.multiple_of(i * RC, RC)
            low = lax.dot_general(cells[pl.ds(r0, RC), :], gpm(),
                                  (((1,), (1,)), ((), ())), preferred_element_type=F32)
            mx = [mext[:, pl.ds(pl.multiple_of((m * 2 + e) * S, S), S)] for e in es]
            rt = lax.dot_general(ratio_hl[:, pl.ds(r0, RC)], jnp.concatenate(mx, axis=1),
                                 (((0,), (0,)), ((), ())), preferred_element_type=F32)
            low = low - rt
            per = YR // RC
            for i_e, e in enumerate(es):
                sh = shares_of(m, e, i) * float(k.CELLS)
                v = sh * (low[:, i_e * S:(i_e + 1) * S] - info2[m, e, 0:1, :])
                ybuf[(m * 2 + e) * X + i // per,
                     pl.ds(pl.multiple_of(lax.rem(i, per) * RC, RC), RC), :] = v.astype(BF16)
            return 0

        lax.fori_loop(0, NC // RC, step, 0)
        for e in es:
            src = ybuf.at[pl.ds((m * 2 + e) * X, X)]
            if m == 0 and type(e) is int and e == 0:
                cp = pltpu.make_async_copy(src, out_map.at[z, :, c], loc_sem.at[3])
                cp.start()
                ycp[0, 0] = cp
            else:
                cp = remote(src, out_map.at[z, :, c], y_s.at[m, e], y_r.at[m, e], group(m, e))
                cp.start()
                pending.append(cp)

    def map_piece(m):
        for e in range(2):
            if (m, e) != (0, 0):
                i2[m, e].wait_recv()
        map_rows(m, [0, 1], lambda: gp[m].reshape(2 * S, G))

    gc[0].wait_recv()
    map_piece(0)

    def pass_on(m, b):
        for b2 in reversed(range(b)):
            to_plane(m, b2)
        to_core(m)

    gc[high] = remote(gp.at[high, 0], gp.at[high, 1], gc_s.at[high], gc_r.at[high], group(0, 1))
    pending.append(gc[high])
    for b2 in range(top):
        t = high ^ (1 << b2)
        gz[t] = remote(gp.at[high, 0], gp.at[t, 0], gz_s.at[t], gz_r.at[t], group(1 << b2, 0))
        pending.append(gz[t])

    def high_on():
        gz[high].wait_recv()
        gc[high].start()
        for b2 in reversed(range(top)):
            gz[high ^ (1 << b2)].start()

    @pl.when(c == 0)
    def _():
        high_on()

    @pl.when(c == 1)
    def _():
        gc[high].wait_recv()
        gz[high].start()

    i2[high, 0].wait_recv()
    i2[high, 1].wait_recv()
    map_rows(high, [c], lambda: gp[high, c])

    @pl.when(c == 1)
    def _():
        high_on()

    @pl.when(c == 0)
    def _():
        gc[high].wait_recv()

    map_rows(high, [1 - c], lambda: gp[high, 1 - c])
    for b in reversed(range(top)):
        for m in range(1 << b, Z, 2 << b):
            gz[m].wait_recv()
            pass_on(m, b)
    for m in far + near:
        gc[m].wait_recv()

    def slot_of(dx, dy, half):
        return ((dx * Y + dy) - 1) * 2 + half

    def single_rows(dx, dy, half):
        bx = lax.rem(x + dx, X)
        by = flip(y, dy)
        return pl.multiple_of(((bx * Y + by) * 2 + half) * H, H)

    def single_part(dx, dy, half, put):
        r0 = single_rows(dx, dy, half)

        def step(i, _):
            lanes = pl.ds(pl.multiple_of(i * NN, NN), NN)
            v = jnp.dot(slow[pl.ds(r0, H), :], gp[:, :, :, lanes].reshape(A * S, NN),
                        preferred_element_type=F32)
            put(lanes, v)
            return 0

        lax.fori_loop(0, G // NN, step, 0)

    def put_send(slot, extra=()):
        def put(lanes, v):
            for i in extra:
                v = v + grecv[i, :, lanes].astype(F32)
            gsend[slot, :, lanes] = v.astype(BF16)
        return put

    r_m1 = lambda d: d
    r_m2 = lambda d: XN + d
    r_m3 = lambda d: 2 * XN + d
    r_m5 = lambda d: 3 * XN + d
    r_m4, r_m6 = 4 * XN, 4 * XN + 1
    gcp = {}

    def send_single(slot, r_slot, where):
        cp = remote(gsend.at[slot], grecv.at[r_slot], gs_s.at[r_slot], gs_r.at[r_slot], where)
        cp.start()
        gcp[r_slot] = cp
        pending.append(cp)

    for d in range(XN):
        s0, s1_ = slot_of(d + 1, 1, 0), slot_of(d + 1, 1, 1)
        single_part(d + 1, 1, 0, put_send(s0))
        send_single(s0, r_m1(d), plane(d + 1, 0))
        single_part(d + 1, 1, 1, put_send(s1_))
        send_single(s1_, r_m2(d), plane(0, 1))
    for m in far:
        map_piece(m)
    for d in range(XN):
        s0 = slot_of(d + 1, 0, 0)
        single_part(d + 1, 0, 0, put_send(s0))
        send_single(s0, r_m3(d), plane(d + 1, 0))
    s0 = slot_of(0, 1, 1)
    single_part(0, 1, 1, put_send(s0))
    send_single(s0, r_m4, plane(0, 1))

    for m in near:
        map_piece(m)

    for d in range(XN):
        gcp[r_m2(d)].wait_recv()
        s0 = slot_of(d + 1, 0, 1)
        single_part(d + 1, 0, 1, put_send(s0, [r_m2(d)]))
        send_single(s0, r_m5(d), plane(d + 1, 0))
    for d in range(XN):
        gcp[r_m1(d)].wait_recv()
    s0 = slot_of(0, 1, 0)
    single_part(0, 1, 0, put_send(s0, [r_m1(d) for d in range(XN)]))
    send_single(s0, r_m6, plane(0, 1))

    def put_own(half):
        def put(lanes, v):
            out_single[half * H:(half + 1) * H, lanes] = v
        return put

    for half in range(2):
        single_part(0, 0, half, put_own(half))
    halves = [[r_m3(d) for d in range(XN)] + [r_m6], [r_m5(d) for d in range(XN)] + [r_m4]]
    for half in range(2):
        for i in halves[half]:
            gcp[i].wait_recv()

        def step(i, _):
            lanes = pl.ds(pl.multiple_of(i * NN, NN), NN)
            v = out_single[half * H:(half + 1) * H, lanes]
            for i2_ in halves[half]:
                v = v + grecv[i2_, :, lanes].astype(F32)
            out_single[half * H:(half + 1) * H, lanes] = v * float(k.CELLS) ** 0.5
            return 0

        lax.fori_loop(0, G // NN, step, 0)

    for m, e in groups:
        other = (flip(z, m), slice(None), flip(c, e))
        remote(ybuf.at[pl.ds(0, X)], out_map.at[other[0], :, other[2]], y_s.at[m, e], y_r.at[m, e],
               group(m, e)).wait_recv()
    ycp[0, 0].wait()
    for cp in pending:
        cp.wait_send()


def forward_and_back(k, logits, single_cell, spatial, ids, mask, cell_prior, order):
    Z, X, Y, A, Q, S, G, R, H = k.Z, k.X, k.Y, k.A, k.Q, k.S, k.G, k.R, k.H
    YR, NC, GA, XN = k.YR, k.NC, k.GA, k.X - 1
    vm = pl.BlockSpec(memory_space=pltpu.VMEM)
    hbm = pl.BlockSpec(memory_space=pl.ANY)
    dma = lambda *s: pltpu.SemaphoreType.DMA(s)
    ncl, ngs = 4 * XN + 2, 4 * XN + 2
    scratch = [
        pltpu.VMEM((Z, 2, X, YR, S), BF16),
        pltpu.VMEM((NC, G), BF16),
        pltpu.VMEM((NC, A * S), BF16),
        pltpu.VMEM(((A - 2) * S, NC), BF16),
        pltpu.VMEM((A * X, YR, S), BF16),
        pltpu.VMEM((Z, 2, 8, S), F32),
        pltpu.VMEM((Z, 2, 8, S), F32),
        pltpu.VMEM((Z, S, G), F32),
        pltpu.VMEM((Z, S, G), BF16),
        pltpu.VMEM((Z, S, G), BF16),
        pltpu.VMEM((Z - 1, S, G), BF16),
        pltpu.VMEM((Z - 1, S, G), BF16),
        pltpu.VMEM((S, G), BF16),
        pltpu.VMEM((Z, 2, S, G), BF16),
        pltpu.VMEM((2 * (Q - 1), H, G), BF16),
        pltpu.VMEM((ngs, H, G), BF16),
        pltpu.VMEM((8, NC), F32),
        pltpu.VMEM((Q - 1, 8, NC), F32),
        pltpu.VMEM((16, NC), BF16),
        pltpu.VMEM((16, A * S), BF16),
        pltpu.VMEM((Z, 2, 8, S), F32),
        pltpu.VMEM((Z, 2, 8, S), F32),
        pltpu.VMEM((A, 16, GA), F32),
        pltpu.VMEM((Z, 2, 16, GA), F32),
        pltpu.VMEM((16, GA), F32),
        pltpu.VMEM((Q - 1, 16, GA), F32),
        pltpu.VMEM((A, 16, GA), F32),
        dma(4),
        dma(Z, 2), dma(Z, 2),
        dma(ncl), dma(ncl),
        dma(Z, 2), dma(Z, 2),
        dma(Z), dma(Z),
        dma(Z - 1), dma(Z - 1),
        dma(Q - 1), dma(Q - 1),
        dma(Z, 2), dma(Z, 2),
        dma(Z, 2), dma(Z, 2),
        dma(Q - 1), dma(Q - 1),
        dma(Z, 2), dma(Z, 2),
        dma(Z), dma(Z),
        dma(Z), dma(Z),
        dma(Z, 2), dma(Z, 2),
        dma(Z, 2), dma(Z, 2),
        dma(ngs), dma(ngs),
    ]
    return pl.pallas_call(
        functools.partial(kernel, k),
        name="mapping",
        out_shape=[
            jax.ShapeDtypeStruct((Z, X, 2, YR, S), BF16),
            jax.ShapeDtypeStruct((R, G), F32),
            jax.ShapeDtypeStruct((8, 128), F32),
        ],
        in_specs=[hbm, hbm, hbm, vm, vm, vm, vm, vm],
        out_specs=[hbm, vm, vm],
        scratch_shapes=scratch,
        compiler_params=pltpu.CompilerParams(
            collective_id=0, has_side_effects=True, vmem_limit_bytes=64000 * 1024),
        cost_estimate=pl.CostEstimate(
            flops=6 * NC * A * S * G, bytes_accessed=32 << 20, transcendentals=2 * NC * A * S),
    )(logits.reshape(Z, X, 2, YR, S), logits.reshape(A * X, YR, S), single_cell, spatial,
      ids.reshape(1, S), mask.reshape(1, S), cell_prior.reshape(-1, k.PL), order.reshape(1, k.NB))


def body(mesh, map_logits, single_cell, spatial, slide_ids, spot_mask, cell_prior, gene_order):
    cells, spots = map_logits.shape
    k = Sizes(mesh, cells, spatial.shape[1], spots, gene_order.shape[0])
    gmap, gsingle, loss = forward_and_back(
        k, map_logits, single_cell, spatial, slide_ids, spot_mask, cell_prior, gene_order)
    grad_map = gmap.reshape(cells, spots).astype(F32)
    return loss[0, :3], grad_map, gsingle


def solution(mesh):
    k = Sizes(mesh, 1 << 20, 1 << 20, 128, 1)
    fine = Mesh(mesh.devices.reshape(k.Z, k.X, 2, k.Y), AXES)
    in_specs = (P(None, AXES), P(AXES, None), P(AXES, None), P(AXES), P(AXES), P(), P())
    out_specs = (P(), P(None, AXES), P(AXES, None))
    return jax.shard_map(functools.partial(body, mesh), mesh=fine, in_specs=in_specs,
                         out_specs=out_specs, check_vma=False)
```

```python
import functools

import jax
import jax.numpy as jnp
from jax import lax
from jax.experimental import pallas as pl
from jax.experimental.pallas import tpu as pltpu
from jax.sharding import Mesh, PartitionSpec as P

SLIDES = 3
FLOOR = 1e-06
F32 = jnp.float32
BF16 = jnp.bfloat16
AXES = ("z", "x", "c", "y")
MESH_ID = pl.DeviceIdType.MESH


def flip(value, mask):
    bit = 1
    while bit <= mask:
        if mask & bit:
            value = value + (1 - 2 * ((value // bit) % 2)) * bit
        bit *= 2
    return value


class Sizes:
    def __init__(self, mesh, cells, genes, spots, blocks):
        n = mesh.shape["spot"] // 2
        zs = 1
        while zs * zs * 4 <= 2 * n:
            zs *= 2
        self.Z, self.X, self.Y = zs, n // zs, mesh.shape["grp"]
        assert self.Y == 2 and self.Z * self.X == n and self.Z >= 2
        self.LV = self.Z.bit_length() - 1
        self.A = 2 * self.Z
        self.Q = self.X * self.Y
        self.CELLS, self.G, self.S, self.NB = cells, genes, spots, blocks
        self.R = cells // (self.A * self.Q)
        self.H = self.R // 2
        self.YR = self.Y * self.R
        self.NC = self.X * self.YR
        self.GA = genes // self.A
        self.RC = min(256, self.YR)
        self.PL = min(128, self.YR)
        self.NN = min(512, genes)


def kernel(k, logits, logits_flat, own_cells, spatial, ids, mask, cell_prior, order,
           out_map, out_single, out_loss,
           lbuf, cells, slow, slow_t, ybuf, info, info2,
           pacc, p1, psib, rs_in, meas,
           gp, gsend, grecv,
           mass_out, mass_in, ratio_hl, mext, dpart, din,
           mstat, mstat_in, stat, s1, ubuf, s2, wall, own_single,
           loc_sem, lg_s, lg_r, cl_s, cl_r, in_s, in_r, ps_s, ps_r, rs_s, rs_r, ms_s, ms_r,
           d_s, d_r, s1_s, s1_r, s2_s, s2_r, s3_s, s3_r, gz_s, gz_r, gc_s, gc_r, i2_s, i2_r,
           y_s, y_r, gs_s, gs_r, mt_s, mt_r, gate):
    Z, X, Y, A, Q, S, G, R, H = k.Z, k.X, k.Y, k.A, k.Q, k.S, k.G, k.R, k.H
    YR, NC, GA, RC, NN = k.YR, k.NC, k.GA, k.RC, k.NN
    z, x, c, y = [lax.axis_index(a) for a in AXES]
    yo = 1 - y

    def group(m, e):
        return (flip(z, m), x, c + e - 2 * c * e, y)

    def plane(dx, dy):
        return (z, lax.rem(x + dx, X), c, flip(y, dy))

    def remote(src, dst, send, recv, where):
        return pltpu.make_async_remote_copy(
            src_ref=src, dst_ref=dst, send_sem=send, recv_sem=recv,
            device_id=where, device_id_type=MESH_ID)

    groups = [(m, e) for m in range(Z) for e in range(2) if (m, e) != (0, 0)]
    planes = [(dx, dy) for dx in range(X) for dy in range(Y) if (dx, dy) != (0, 0)]
    me = z * 2 + c
    pending = []

    cp_flat = pltpu.make_async_copy(logits_flat, ybuf, loc_sem.at[0])
    cp_flat.start()
    cp_own = pltpu.make_async_copy(logits.at[z, :, c], lbuf.at[0, 0], loc_sem.at[1])
    cp_own.start()
    cp_cells = pltpu.make_async_copy(
        own_cells, cells.at[pl.ds(pl.multiple_of((x * Y + y) * R, R), R)], loc_sem.at[2])
    cp_cells.start()
    barrier = pltpu.get_barrier_semaphore()
    for m, e in groups:
        pl.semaphore_signal(barrier, inc=1, device_id=group(m, e), device_id_type=MESH_ID)
    for dx, dy in planes:
        pl.semaphore_signal(barrier, inc=1, device_id=plane(dx, dy), device_id_type=MESH_ID)
    pl.semaphore_wait(barrier, len(groups) + len(planes))

    def rows(bx, by, half):
        return cells.at[pl.ds(pl.multiple_of(((bx * Y + by) * 2 + half) * H, H), H)]

    XN = X - 1

    def cell_copy(slot, src, bx, by, half, where):
        return remote(src, rows(bx, by, half), cl_s.at[slot], cl_r.at[slot], where)

    own_half = [own_cells.at[pl.ds(0, H)], own_cells.at[pl.ds(H, H)]]
    x_first = [cell_copy(d, own_half[0], x, y, 0, plane(d + 1, 0)) for d in range(XN)]
    x_last = [cell_copy(XN + d, own_half[1], x, y, 1, plane(d + 1, 0)) for d in range(XN)]
    y_first = cell_copy(2 * XN, own_half[1], x, y, 1, plane(0, 1))
    y_last = cell_copy(2 * XN + 1, own_half[0], x, y, 0, plane(0, 1))
    for cp in x_first + [y_first]:
        cp.start()

    high = Z // 2
    far = [m for m in range(Z) if m & high and m != high]
    near = [m for m in range(1, Z) if not m & high]
    lg = {(m, e): remote(logits.at[flip(z, m), :, flip(c, e)], lbuf.at[m, e],
                         lg_s.at[m, e], lg_r.at[m, e], group(m, e)) for m, e in groups}

    pending.extend(cp for (m, e), cp in lg.items() if m in [0] + near)

    def sent(ms):
        for m in ms:
            for e in range(2):
                lg[m, e].wait_send()

    def send_logits(ms, es=(0, 1)):
        for m in ms:
            for e in es:
                lg[m, e].start()

    at_end = (z == 0) | (z == Z - 1)
    inside = jnp.logical_not(at_end)
    lg[0, 1].start()

    @pl.when(at_end)
    def _():
        send_logits(near + far)

    @pl.when(inside)
    def _():
        send_logits([high])

    for cp in x_last + [y_last]:
        cp.start()
    pending.extend(x_first + x_last + [y_first, y_last])

    cp_flat.wait()

    def add_exp(i, acc):
        e = jnp.exp(ybuf[i].astype(F32))
        return acc + jnp.sum(e.reshape(YR // 8, 8, S), axis=0)

    acc = lax.fori_loop(0, A * X, add_exp, jnp.zeros((8, S), F32))
    inv_sum = 1.0 / jnp.sum(acc, axis=0, keepdims=True)
    idr = ids[...]
    maskf = mask[...].astype(F32)
    mrow = [jnp.where(idr == s, maskf, 0.0) for s in range(SLIDES)]
    info[0, 0] = jnp.concatenate([inv_sum] + mrow + [jnp.zeros((8 - 1 - SLIDES, S), F32)], axis=0)
    inf = {}
    for m, e in groups:
        inf[m, e] = remote(info.at[0, 0], info.at[m, e], in_s.at[m, e], in_r.at[m, e], group(m, e))
        inf[m, e].start()
        pending.append(inf[m, e])

    W = G // k.NB
    for b in range(k.NB):
        v = jnp.zeros((S, W), F32)
        for j in range(k.NB):
            here = (order[0:1, j:j + 1] == b).astype(F32)
            v = v + here * spatial[:, j * W:(j + 1) * W].astype(F32)
        meas[:, b * W:(b + 1) * W] = v.astype(BF16)
    mcols = jnp.concatenate(mrow + [maskf] + [jnp.zeros((8 - 1 - SLIDES, S), F32)], axis=0).T
    mcol = [mcols[:, s:s + 1] for s in range(SLIDES)]
    wcol = mcols[:, SLIDES:SLIDES + 1]
    meas_sq = jnp.zeros((S, 1), F32)
    for j in range(A):
        v = meas[:, j * GA:(j + 1) * GA].astype(F32)
        v = v * v
        meas_sq = meas_sq + jnp.sum(v, axis=1, keepdims=True)
        for s in range(SLIDES):
            mstat[j, s:s + 1, :] = jnp.sum(mcol[s] * v, axis=0, keepdims=True)
        mstat[j, SLIDES:8, :] = jnp.zeros((8 - SLIDES, GA), F32)
    inv_meas = lax.rsqrt(meas_sq + FLOOR)
    mst = {}
    for m, e in groups:
        mst[m, e] = remote(mstat.at[flip(z, m) * 2 + flip(c, e)], mstat_in.at[m, e],
                           mt_s.at[m, e], mt_r.at[m, e], group(m, e))
        mst[m, e].start()
    pending.extend(mst.values())

    fwd_a, fwd_b = [], []
    for d in range(XN):
        bx = lax.rem(x - (d + 1) + X, X)
        cell_copy(d, own_half[0], bx, y, 0, plane(d + 1, 0)).wait_recv()
        cp = cell_copy(2 * XN + 2 + d, rows(bx, y, 0), bx, y, 0, plane(0, 1))
        cp.start()
        fwd_a.append(cp)
    y_first.wait_recv()
    for d in range(XN):
        cp = cell_copy(3 * XN + 2 + d, rows(x, yo, 1), x, yo, 1, plane(d + 1, 0))
        cp.start()
        fwd_b.append(cp)
    pending.extend(fwd_a + fwd_b)

    cp_own.wait()
    cp_cells.wait()

    def shares_of(m, e, i):
        per = YR // RC
        l = lbuf[m, e, i // per, pl.ds(pl.multiple_of(lax.rem(i, per) * RC, RC), RC), :]
        return jnp.exp(l.astype(F32)) * info[m, e, 0:1, :]

    def t_row(m, i):
        return (m * 2 + i) * S

    def slot(cc):
        return c if cc == 0 else 1 - c

    def wait_cross(m, cc):
        e = slot(cc)
        remote(info.at[0, 0], info.at[m, e], in_s.at[m, e], in_r.at[m, e],
               group(m, e)).wait_recv()
        remote(lbuf.at[0, 0], lbuf.at[m, e], lg_s.at[m, e], lg_r.at[m, e],
               group(m, e)).wait_recv()

    def wait_pair(m):
        for e in range(2):
            if (m, e) != (0, 0):
                inf[m, e].wait_recv()
                lg[m, e].wait_recv()

    def make_shares(m, e, row):
        lane = (m * 2 + e) * S
        if type(e) is not int:
            lane = pl.multiple_of(lane, S)

        def step(i, _):
            sh = shares_of(m, e, i).astype(BF16)
            r0 = pl.multiple_of(i * RC, RC)
            slow[pl.ds(r0, RC), pl.ds(lane, S)] = sh
            slow_t[row:row + S, pl.ds(r0, RC)] = sh.T
            return 0

        lax.fori_loop(0, NC // RC, step, 0)

    def pair_shares(m):
        wait_pair(m)
        for e in range(2):
            make_shares(m, e, t_row(m, e))

    def cross_shares(m, cc):
        make_shares(m, slot(cc), t_row(m, cc))

    ps = [remote(p1.at[m], psib.at[m], ps_s.at[m], ps_r.at[m], group(0, 1)) for m in range(Z)]
    pending.extend(ps)

    def gene_loop(put):
        def step(i, _):
            put(pl.ds(pl.multiple_of(i * NN, NN), NN))
            return 0

        lax.fori_loop(0, G // NN, step, 0)

    def predict_pair(m):
        row = t_row(m, 0)

        def put(lanes):
            r = jnp.dot(slow_t[row:row + 2 * S, :], cells[:, lanes], preferred_element_type=F32)
            pacc[m, :, lanes] = r[:S]
            p1[m, :, lanes] = r[S:].astype(BF16)

        gene_loop(put)
        ps[m].start()

    def predict_cross(m, cc):
        row = t_row(m, cc)

        def part(lanes):
            return jnp.dot(slow_t[row:row + S, :], cells[:, lanes], preferred_element_type=F32)

        @pl.when(c == cc)
        def _():
            def put(lanes):
                pacc[m, :, lanes] = part(lanes)

            gene_loop(put)

        @pl.when(c != cc)
        def _():
            def put(lanes):
                p1[m, :, lanes] = part(lanes).astype(BF16)

            gene_loop(put)
            ps[m].start()

    def level_slot(b, m):
        return sum(Z >> (j + 1) for j in range(b)) + (m >> (b + 1))

    rs = {}
    for b in range(k.LV):
        step_m = 1 << b
        for m in range(0, Z, 2 * step_m):
            sl = level_slot(b, m)
            rs[b, m] = remote(psib.at[m ^ step_m], rs_in.at[sl], rs_s.at[sl], rs_r.at[sl],
                              group(step_m, 0))
    pending.extend(rs.values())

    def piece_sum(m, b):
        ps[m].wait_recv()
        for j in range(b):
            rs[j, m].wait_recv()

        def total(lanes):
            t = pacc[m, :, lanes] + psib[m, :, lanes].astype(F32)
            for j in range(b):
                t = t + rs_in[level_slot(j, m), :, lanes].astype(F32)
            return t
        return total

    def sum_level(b, m):
        total = piece_sum(m, b)
        for j in range(A):
            lanes = slice(j * GA, (j + 1) * GA)
            psib[m, :, lanes] = total(lanes).astype(BF16)

    def far_levels(cc):
        @pl.when(c == cc)
        def _():
            for b in range(top):
                send_level(b, of_level(b, far))

    def send_level(b, ms):
        for m in ms:
            sum_level(b, m)
            rs[b, m ^ (1 << b)].start()

    top = k.LV - 1
    def of_level(b, ms):
        return [m for m in reversed(ms) if m % (2 << b) == 1 << b]

    pair_shares(0)

    @pl.when(at_end)
    def _():
        sent(far)
        send_logits([high])

    @pl.when(inside)
    def _():
        sent([high])
        send_logits(near)

    pair_shares(high)

    @pl.when(inside & (c == 0))
    def _():
        send_logits(far)

    @pl.when(at_end)
    def _():
        for m in far:
            for cc in range(2):
                wait_cross(m, cc)
                cross_shares(m, cc)

    for m in near:
        pair_shares(m)
    for cp in x_last + [y_last] + fwd_a + fwd_b:
        cp.wait_recv()

    @pl.when(at_end)
    def _():
        for cc in range(2):
            for m in far:
                predict_cross(m, cc)
        for cc in range(2):
            far_levels(cc)

    predict_pair(high)
    for b in range(top):
        for m in of_level(b, near):
            predict_pair(m)
        send_level(b, of_level(b, near))
    predict_pair(0)

    @pl.when(inside)
    def _():
        for m in far:
            wait_cross(m, 0)

        @pl.when(c == 1)
        def _():
            send_logits(far, (1, 0))

        for m in far:
            cross_shares(m, 0)
            predict_cross(m, 0)
        far_levels(0)

        @pl.when(c == 0)
        def _():
            sum_level(top, high)

        for m in far:
            wait_cross(m, 1)
            cross_shares(m, 1)
            predict_cross(m, 1)

        @pl.when(c == 0)
        def _():
            rs[top, 0].start()

        far_levels(1)

    @pl.when(at_end | (c == 1))
    def _():
        sum_level(top, high)
        rs[top, 0].start()

    mem_rows = jnp.concatenate(
        [info[m, e, 1:1 + SLIDES, :] for m in range(Z) for e in range(2)], axis=1)
    mem16 = jnp.concatenate([mem_rows, jnp.zeros((16 - SLIDES, A * S), F32)], axis=0).astype(BF16)
    part = lax.dot_general(mem16, slow[...], (((1,), (1,)), ((), ())), preferred_element_type=F32)
    col_tally = jnp.sum(mem_rows, axis=1, keepdims=True)
    gmeas = mstat[me]
    for m, e in groups:
        mst[m, e].wait_recv()
        gmeas = gmeas + mstat_in[m, e]
    packed = [gmeas[s:s + 1] for s in range(SLIDES)] + [jnp.zeros((1, NC - SLIDES * GA), F32)]
    mass_out[...] = jnp.concatenate(
        [part[:SLIDES], jnp.broadcast_to(col_tally, (SLIDES, NC)),
         jnp.concatenate(packed, axis=1), jnp.zeros((1, NC), F32)], axis=0)
    mcp = []
    for i, (dx, dy) in enumerate(planes):
        cp = remote(mass_out, mass_in.at[i], ms_s.at[i], ms_r.at[i], plane(dx, dy))
        cp.start()
        mcp.append(cp)
    pending.extend(mcp)
    for cp in mcp:
        cp.wait_recv()
    msum = mass_out[...]
    for i in range(Q - 1):
        msum = msum + mass_in[i]
    mass = msum[:SLIDES]
    gmeas = jnp.concatenate(
        [msum[6:7, s * GA:(s + 1) * GA] for s in range(SLIDES)], axis=0)
    inv_gmeas = lax.rsqrt(gmeas + FLOOR)
    tally = jnp.maximum(msum[SLIDES:2 * SLIDES, 0:1], 1.0)
    quota = mass / tally
    prior_sum = jnp.sum(jnp.sum(cell_prior[...], axis=0, keepdims=True), axis=1, keepdims=True)
    prior = jnp.concatenate(
        [cell_prior[pl.ds(((z * X + bx) * 2 + c) * (YR // k.PL) + i, 1), :]
         for bx in range(X) for i in range(YR // k.PL)], axis=1) / prior_sum
    kl = jnp.sum(prior * (jnp.log(prior) - jnp.log(quota)), axis=1, keepdims=True)
    rat = prior / quota
    rat_hi = rat.astype(BF16)
    rat_lo = (rat - rat_hi.astype(F32)).astype(BF16)
    ratio_hl[...] = jnp.concatenate(
        [rat_hi, rat_lo, jnp.zeros((16 - 2 * SLIDES, NC), BF16)], axis=0)
    dd = jnp.dot(ratio_hl[...], slow[...], preferred_element_type=F32)
    dd = dd[:SLIDES] + dd[SLIDES:2 * SLIDES]
    dsum = jnp.sum(dd * mem_rows, axis=0, keepdims=True)
    mext[...] = jnp.concatenate(
        [mem_rows, mem_rows, jnp.zeros((16 - 2 * SLIDES, A * S), F32)], axis=0).astype(BF16)
    dcp = {}
    for m in range(Z):
        for e in range(2):
            lane = (m * 2 + e) * S
            dpart[m, e] = jnp.broadcast_to(dsum[:, lane:lane + S], (8, S))
    for m, e in groups:
        cp = remote(dpart.at[m, e], din.at[m, e], d_s.at[m, e], d_r.at[m, e], group(m, e))
        cp.start()
        dcp[m, e] = cp
        pending.append(cp)

    total = piece_sum(0, k.LV)
    pred_sq = jnp.zeros((S, 1), F32)
    pred_meas = jnp.zeros((S, 1), F32)
    lane_id = lax.broadcasted_iota(jnp.int32, (1, GA), 1)
    for j in range(A):
        lanes = slice(j * GA, (j + 1) * GA)
        p = total(lanes)
        pacc[0, :, lanes] = p
        q = meas[:, lanes].astype(F32)
        pq, pp = p * q, p * p
        pred_sq = pred_sq + jnp.sum(pp, axis=1, keepdims=True)
        pred_meas = pred_meas + jnp.sum(pq, axis=1, keepdims=True)
        for s in range(SLIDES):
            stat[j, s:s + 1, :] = jnp.sum(mcol[s] * pq, axis=0, keepdims=True)
            stat[j, 3 + s:4 + s, :] = jnp.sum(mcol[s] * pp, axis=0, keepdims=True)
    inv_pred = lax.rsqrt(pred_sq + FLOOR)
    spot_cos = pred_meas * inv_pred * inv_meas
    spot_sum = jnp.sum(wcol * spot_cos, axis=0, keepdims=True)
    scal = jnp.where(lane_id == 0, spot_sum, 0.0)
    for s in range(SLIDES):
        scal = scal + jnp.where(lane_id == 1 + s, kl[s:s + 1] * (1.0 / Q), 0.0)
    for j in range(A):
        stat[j, 6:8, :] = jnp.concatenate([scal, jnp.zeros((1, GA), F32)], axis=0)

    cps = {}
    for m, e in groups:
        cp = remote(stat.at[flip(z, m) * 2 + flip(c, e)], s1.at[m, e],
                    s1_s.at[m, e], s1_r.at[m, e], group(m, e))
        cp.start()
        cps[m, e] = cp
        pending.append(cp)
    u = stat[me]
    for m, e in groups:
        cps[m, e].wait_recv()
        u = u + s1[m, e]
    ubuf[...] = u
    cps = []
    for i, (dx, dy) in enumerate(planes):
        cp = remote(ubuf, s2.at[i], s2_s.at[i], s2_r.at[i], plane(dx, dy))
        cp.start()
        cps.append(cp)
        pending.append(cp)
    for i, cp in enumerate(cps):
        cp.wait_recv()
        u = u + s2[i]
    share = tally * (1.0 / G)
    a = lax.rsqrt(u[3:6] + FLOOR)
    b = inv_gmeas
    gcos = u[0:3] * a * b
    wall[me] = jnp.concatenate(
        [share * a * b, share * gcos * a * a,
         jnp.sum(share * gcos, axis=0, keepdims=True), u[6:7]], axis=0)
    cps = []
    for m, e in groups:
        cp = remote(wall.at[me], wall.at[me], s3_s.at[m, e], s3_r.at[m, e], group(m, e))
        cp.start()
        cps.append(cp)
        pending.append(cp)
    for (m, e) in groups:
        other = flip(z, m) * 2 + flip(c, e)
        remote(wall.at[other], wall.at[other], s3_s.at[m, e], s3_r.at[m, e], group(m, e)).wait_recv()

    lead = -(wcol * inv_pred * inv_meas)
    back = wcol * spot_cos * inv_pred * inv_pred
    dot1 = jnp.zeros((S, 1), F32)
    gene_total = jnp.zeros((1, GA), F32)
    for j in range(A):
        lanes = slice(j * GA, (j + 1) * GA)
        w = wall[j]
        direct = mcol[0] * w[0:1] + mcol[1] * w[1:2] + mcol[2] * w[2:3]
        damp = mcol[0] * w[3:4] + mcol[1] * w[4:5] + mcol[2] * w[5:6]
        gene_total = gene_total + w[6:7]
        p = pacc[0, :, lanes]
        g = (lead - direct) * meas[:, lanes].astype(F32) + (back + damp) * p
        glow = g.astype(BF16)
        gp[0, 0, :, lanes] = glow
        dot1 = dot1 + jnp.sum(glow.astype(F32) * p, axis=1, keepdims=True)

    gz, gc = {}, {}

    def to_core(m):
        cp = remote(gp.at[m, 0], gp.at[m, 1], gc_s.at[m], gc_r.at[m], group(0, 1))
        cp.start()
        gc[m] = cp
        pending.append(cp)

    def to_plane(m, b):
        t = m ^ (1 << b)
        cp = remote(gp.at[m, 0], gp.at[t, 0], gz_s.at[t], gz_r.at[t], group(1 << b, 0))
        cp.start()
        gz[t] = cp
        pending.append(cp)

    to_core(0)
    gz[high] = remote(gp.at[0, 0], gp.at[high, 0], gz_s.at[high], gz_r.at[high], group(high, 0))

    for b in range(top):
        t = 1 << b
        gz[t] = remote(gp.at[0, 0], gp.at[t, 0], gz_s.at[t], gz_r.at[t], group(t, 0))

    def near_start():
        for b in reversed(range(top)):
            gz[1 << b].start()

    @pl.when(c == 0)
    def _():
        gz[high].start()

    @pl.when(c == 1)
    def _():
        near_start()

    for m, e in groups:
        dcp[m, e].wait_recv()
    dtot = dpart[0, 0]
    for m, e in groups:
        dtot = dtot + din[m, e]
    dot_row = jnp.broadcast_to(dot1, (S, S)).T[0:8] - dtot
    info2[0, 0] = dot_row
    i2 = {}
    for m, e in groups:
        cp = remote(info2.at[0, 0], info2.at[m, e], i2_s.at[m, e], i2_r.at[m, e], group(m, e))
        cp.start()
        i2[m, e] = cp
        pending.append(cp)

    fin = wall[0]
    total_tally = jnp.sum(tally, axis=0, keepdims=True)
    gsum = jnp.sum(gene_total, axis=1, keepdims=True)
    dens = jnp.zeros((1, 1), F32)
    for s in range(SLIDES):
        dens = dens + tally[s:s + 1] * fin[7:8, 1 + s:2 + s]
    lid = lax.broadcasted_iota(jnp.int32, (8, 128), 1)
    out_loss[...] = (jnp.where(lid == 0, fin[7:8, 0:1], 0.0) + jnp.where(lid == 1, gsum, 0.0)
                     + jnp.where(lid == 2, dens, 0.0)) / total_tally

    ycp = {}

    def map_rows(m, es, gpm):
        n = len(es)

        def step(i, _):
            r0 = pl.multiple_of(i * RC, RC)
            low = lax.dot_general(cells[pl.ds(r0, RC), :], gpm(),
                                  (((1,), (1,)), ((), ())), preferred_element_type=F32)
            mx = [mext[:, pl.ds(pl.multiple_of((m * 2 + e) * S, S), S)] for e in es]
            rt = lax.dot_general(ratio_hl[:, pl.ds(r0, RC)], jnp.concatenate(mx, axis=1),
                                 (((0,), (0,)), ((), ())), preferred_element_type=F32)
            low = low - rt
            per = YR // RC
            for i_e, e in enumerate(es):
                sh = shares_of(m, e, i) * float(k.CELLS)
                v = sh * (low[:, i_e * S:(i_e + 1) * S] - info2[m, e, 0:1, :])
                ybuf[(m * 2 + e) * X + i // per,
                     pl.ds(pl.multiple_of(lax.rem(i, per) * RC, RC), RC), :] = v.astype(BF16)
            return 0

        lax.fori_loop(0, NC // RC, step, 0)

    def send_map(m, es):
        for e in es:
            src = ybuf.at[pl.ds((m * 2 + e) * X, X)]
            if m == 0 and type(e) is int and e == 0:
                cp = pltpu.make_async_copy(src, out_map.at[z, :, c], loc_sem.at[3])
                cp.start()
                ycp[0, 0] = cp
            else:
                cp = remote(src, out_map.at[z, :, c], y_s.at[m, e], y_r.at[m, e], group(m, e))
                cp.start()
                pending.append(cp)

    def map_piece(m):
        for e in range(2):
            if (m, e) != (0, 0):
                i2[m, e].wait_recv()
        map_rows(m, [0, 1], lambda: gp[m].reshape(2 * S, G))
        send_map(m, [0, 1])

    gc[0].wait_recv()
    map_piece(0)

    def pass_on(m, b):
        for b2 in reversed(range(b)):
            to_plane(m, b2)
        to_core(m)

    gc[high] = remote(gp.at[high, 0], gp.at[high, 1], gc_s.at[high], gc_r.at[high], group(0, 1))
    pending.append(gc[high])
    for b2 in range(top):
        t = high ^ (1 << b2)
        gz[t] = remote(gp.at[high, 0], gp.at[t, 0], gz_s.at[t], gz_r.at[t], group(1 << b2, 0))
        pending.append(gz[t])

    def high_on():
        gz[high].wait_recv()
        gc[high].start()
        for b2 in reversed(range(top)):
            gz[high ^ (1 << b2)].start()

    @pl.when(c == 0)
    def _():
        gz[high].wait_send()
        pl.semaphore_signal(gate, inc=1, device_id=group(0, 1), device_id_type=MESH_ID)
        near_start()
        high_on()

    @pl.when(c == 1)
    def _():
        pl.semaphore_wait(gate, 1)
        gz[high].start()
        gc[high].wait_recv()

    i2[high, 0].wait_recv()
    i2[high, 1].wait_recv()
    map_rows(high, [c], lambda: gp[high, c])

    @pl.when(c == 1)
    def _():
        high_on()

    @pl.when(c == 0)
    def _():
        gc[high].wait_recv()

    send_map(high, [c])
    map_rows(high, [1 - c], lambda: gp[high, 1 - c])
    send_map(high, [1 - c])
    for b in reversed(range(top)):
        for m in range(1 << b, Z, 2 << b):
            gz[m].wait_recv()
            pass_on(m, b)
    for m in far + near:
        gc[m].wait_recv()

    def slot_of(dx, dy, half):
        return ((dx * Y + dy) - 1) * 2 + half

    def single_rows(dx, dy, half):
        bx = lax.rem(x + dx, X)
        by = flip(y, dy)
        return pl.multiple_of(((bx * Y + by) * 2 + half) * H, H)

    def single_part(dx, dy, half, put):
        r0 = single_rows(dx, dy, half)

        def step(i, _):
            lanes = pl.ds(pl.multiple_of(i * NN, NN), NN)
            v = jnp.dot(slow[pl.ds(r0, H), :], gp[:, :, :, lanes].reshape(A * S, NN),
                        preferred_element_type=F32)
            put(lanes, v)
            return 0

        lax.fori_loop(0, G // NN, step, 0)

    def put_send(slot, extra=()):
        def put(lanes, v):
            for i in extra:
                v = v + grecv[i, :, lanes].astype(F32)
            gsend[slot, :, lanes] = v.astype(BF16)
        return put

    r_m1 = lambda d: d
    r_m2 = lambda d: XN + d
    r_m3 = lambda d: 2 * XN + d
    r_m5 = lambda d: 3 * XN + d
    r_m4, r_m6 = 4 * XN, 4 * XN + 1
    gcp = {}

    def send_single(slot, r_slot, where):
        cp = remote(gsend.at[slot], grecv.at[r_slot], gs_s.at[r_slot], gs_r.at[r_slot], where)
        cp.start()
        gcp[r_slot] = cp
        pending.append(cp)

    for d in range(XN):
        s0, s1_ = slot_of(d + 1, 1, 0), slot_of(d + 1, 1, 1)
        single_part(d + 1, 1, 0, put_send(s0))
        send_single(s0, r_m1(d), plane(d + 1, 0))
        single_part(d + 1, 1, 1, put_send(s1_))
        send_single(s1_, r_m2(d), plane(0, 1))
    for m in far:
        map_piece(m)
    for d in range(XN):
        s0 = slot_of(d + 1, 0, 0)
        single_part(d + 1, 0, 0, put_send(s0))
        send_single(s0, r_m3(d), plane(d + 1, 0))
    s0 = slot_of(0, 1, 1)
    single_part(0, 1, 1, put_send(s0))
    send_single(s0, r_m4, plane(0, 1))

    for m in near:
        map_piece(m)

    for d in range(XN):
        gcp[r_m2(d)].wait_recv()
        s0 = slot_of(d + 1, 0, 1)
        single_part(d + 1, 0, 1, put_send(s0, [r_m2(d)]))
        send_single(s0, r_m5(d), plane(d + 1, 0))
    for d in range(XN):
        gcp[r_m1(d)].wait_recv()
    s0 = slot_of(0, 1, 0)
    single_part(0, 1, 0, put_send(s0, [r_m1(d) for d in range(XN)]))
    send_single(s0, r_m6, plane(0, 1))

    def put_own(half):
        def put(lanes, v):
            own_single[half * H:(half + 1) * H, lanes] = v
        return put

    for half in range(2):
        single_part(0, 0, half, put_own(half))
    halves = [[r_m3(d) for d in range(XN)] + [r_m6], [r_m5(d) for d in range(XN)] + [r_m4]]
    for half in range(2):
        for i in halves[half]:
            gcp[i].wait_recv()

        def step(i, _):
            lanes = pl.ds(pl.multiple_of(i * NN, NN), NN)
            v = own_single[half * H:(half + 1) * H, lanes]
            for i2_ in halves[half]:
                v = v + grecv[i2_, :, lanes].astype(F32)
            own_single[half * H:(half + 1) * H, lanes] = v * float(k.CELLS) ** 0.5
            return 0

        lax.fori_loop(0, G // NN, step, 0)

    cp_single = pltpu.make_async_copy(own_single, out_single, loc_sem.at[4])
    cp_single.start()

    for m, e in groups:
        other = (flip(z, m), slice(None), flip(c, e))
        remote(ybuf.at[pl.ds(0, X)], out_map.at[other[0], :, other[2]], y_s.at[m, e], y_r.at[m, e],
               group(m, e)).wait_recv()
    ycp[0, 0].wait()
    cp_single.wait()
    for cp in pending:
        cp.wait_send()
    for b in range(top):
        gz[1 << b].wait_send()

    @pl.when(c == 1)
    def _():
        gz[high].wait_send()

    @pl.when(at_end)
    def _():
        sent([high])

    @pl.when(inside)
    def _():
        sent(far)


def forward_and_back(k, logits, single_cell, spatial, ids, mask, cell_prior, order):
    Z, X, Y, A, Q, S, G, R, H = k.Z, k.X, k.Y, k.A, k.Q, k.S, k.G, k.R, k.H
    YR, NC, GA, XN = k.YR, k.NC, k.GA, k.X - 1
    vm = pl.BlockSpec(memory_space=pltpu.VMEM)
    hbm = pl.BlockSpec(memory_space=pl.ANY)
    dma = lambda *s: pltpu.SemaphoreType.DMA(s)
    ncl, ngs = 4 * XN + 2, 4 * XN + 2
    scratch = [
        pltpu.VMEM((Z, 2, X, YR, S), BF16),
        pltpu.VMEM((NC, G), BF16),
        pltpu.VMEM((NC, A * S), BF16),
        pltpu.VMEM((A * S, NC), BF16),
        pltpu.VMEM((A * X, YR, S), BF16),
        pltpu.VMEM((Z, 2, 8, S), F32),
        pltpu.VMEM((Z, 2, 8, S), F32),
        pltpu.VMEM((Z, S, G), F32),
        pltpu.VMEM((Z, S, G), BF16),
        pltpu.VMEM((Z, S, G), BF16),
        pltpu.VMEM((Z - 1, S, G), BF16),
        pltpu.VMEM((S, G), BF16),
        pltpu.VMEM((Z, 2, S, G), BF16),
        pltpu.VMEM((2 * (Q - 1), H, G), BF16),
        pltpu.VMEM((ngs, H, G), BF16),
        pltpu.VMEM((8, NC), F32),
        pltpu.VMEM((Q - 1, 8, NC), F32),
        pltpu.VMEM((16, NC), BF16),
        pltpu.VMEM((16, A * S), BF16),
        pltpu.VMEM((Z, 2, 8, S), F32),
        pltpu.VMEM((Z, 2, 8, S), F32),
        pltpu.VMEM((A, 8, GA), F32),
        pltpu.VMEM((Z, 2, 8, GA), F32),
        pltpu.VMEM((A, 8, GA), F32),
        pltpu.VMEM((Z, 2, 8, GA), F32),
        pltpu.VMEM((8, GA), F32),
        pltpu.VMEM((Q - 1, 8, GA), F32),
        pltpu.VMEM((A, 8, GA), F32),
        pltpu.VMEM((R, G), F32),
        dma(6),
        dma(Z, 2), dma(Z, 2),
        dma(ncl), dma(ncl),
        dma(Z, 2), dma(Z, 2),
        dma(Z), dma(Z),
        dma(Z - 1), dma(Z - 1),
        dma(Q - 1), dma(Q - 1),
        dma(Z, 2), dma(Z, 2),
        dma(Z, 2), dma(Z, 2),
        dma(Q - 1), dma(Q - 1),
        dma(Z, 2), dma(Z, 2),
        dma(Z), dma(Z),
        dma(Z), dma(Z),
        dma(Z, 2), dma(Z, 2),
        dma(Z, 2), dma(Z, 2),
        dma(ngs), dma(ngs),
        dma(Z, 2), dma(Z, 2),
        pltpu.SemaphoreType.REGULAR,
    ]
    return pl.pallas_call(
        functools.partial(kernel, k),
        name="mapping",
        out_shape=[
            jax.ShapeDtypeStruct((Z, X, 2, YR, S), BF16),
            jax.ShapeDtypeStruct((R, G), F32),
            jax.ShapeDtypeStruct((8, 128), F32),
        ],
        in_specs=[hbm, hbm, hbm, vm, vm, vm, vm, vm],
        out_specs=[hbm, hbm, vm],
        scratch_shapes=scratch,
        compiler_params=pltpu.CompilerParams(
            collective_id=0, has_side_effects=True, vmem_limit_bytes=64000 * 1024),
        cost_estimate=pl.CostEstimate(
            flops=6 * NC * A * S * G, bytes_accessed=32 << 20, transcendentals=2 * NC * A * S),
    )(logits.reshape(Z, X, 2, YR, S), logits.reshape(A * X, YR, S), single_cell, spatial,
      ids.reshape(1, S), mask.reshape(1, S), cell_prior.reshape(-1, k.PL), order.reshape(1, k.NB))


def body(mesh, map_logits, single_cell, spatial, slide_ids, spot_mask, cell_prior, gene_order):
    cells, spots = map_logits.shape
    k = Sizes(mesh, cells, spatial.shape[1], spots, gene_order.shape[0])
    gmap, gsingle, loss = forward_and_back(
        k, map_logits, single_cell, spatial, slide_ids, spot_mask, cell_prior, gene_order)
    grad_map = gmap.reshape(cells, spots).astype(F32)
    return loss[0, :3], grad_map, gsingle


def solution(mesh):
    k = Sizes(mesh, 1 << 20, 1 << 20, 128, 1)
    fine = Mesh(mesh.devices.reshape(k.Z, k.X, 2, k.Y), AXES)
    in_specs = (P(None, AXES), P(AXES, None), P(AXES, None), P(AXES), P(AXES), P(), P())
    out_specs = (P(), P(None, AXES), P(AXES, None))
    return jax.shard_map(functools.partial(body, mesh), mesh=fine, in_specs=in_specs,
                         out_specs=out_specs, check_vma=False)
```

```python
import functools

import jax
import jax.numpy as jnp
from jax import lax
from jax.experimental import pallas as pl
from jax.experimental.pallas import tpu as pltpu
from jax.sharding import Mesh, PartitionSpec as P

SLIDES = 3
FLOOR = 1e-06
F32 = jnp.float32
BF16 = jnp.bfloat16
AXES = ("z", "x", "c", "y")
MESH_ID = pl.DeviceIdType.MESH


def flip(value, mask):
    bit = 1
    while bit <= mask:
        if mask & bit:
            value = value + (1 - 2 * ((value // bit) % 2)) * bit
        bit *= 2
    return value


class Sizes:
    def __init__(self, mesh, cells, genes, spots, blocks):
        n = mesh.shape["spot"] // 2
        zs = 1
        while zs * zs * 4 <= 2 * n:
            zs *= 2
        self.Z, self.X, self.Y = zs, n // zs, mesh.shape["grp"]
        assert self.Y == 2 and self.Z * self.X == n and self.Z >= 2
        self.LV = self.Z.bit_length() - 1
        self.A = 2 * self.Z
        self.Q = self.X * self.Y
        self.CELLS, self.G, self.S, self.NB = cells, genes, spots, blocks
        self.R = cells // (self.A * self.Q)
        self.H = self.R // 2
        self.YR = self.Y * self.R
        self.NC = self.X * self.YR
        self.GA = genes // self.A
        self.RC = min(256, self.YR)
        self.PL = min(128, self.YR)
        self.NN = min(512, genes)


def kernel(k, logits, logits_flat, own_cells, spatial, ids, mask, cell_prior, order,
           out_map, out_single, out_loss,
           lbuf, cells, slow, slow_t, ybuf, info, info2,
           pacc, p1, psib, rs_in, meas,
           gp, gsend, grecv,
           mass_out, mass_in, ratio_hl, mext, dpart, din,
           mstat, mstat_in, stat, s1, ubuf, s2, wall, own_single,
           loc_sem, lg_s, lg_r, cl_s, cl_r, in_s, in_r, ps_s, ps_r, rs_s, rs_r, ms_s, ms_r,
           d_s, d_r, s1_s, s1_r, s2_s, s2_r, s3_s, s3_r, gz_s, gz_r, gc_s, gc_r, i2_s, i2_r,
           y_s, y_r, gs_s, gs_r, mt_s, mt_r, gate):
    Z, X, Y, A, Q, S, G, R, H = k.Z, k.X, k.Y, k.A, k.Q, k.S, k.G, k.R, k.H
    YR, NC, GA, RC, NN = k.YR, k.NC, k.GA, k.RC, k.NN
    z, x, c, y = [lax.axis_index(a) for a in AXES]
    yo = 1 - y

    def group(m, e):
        return (flip(z, m), x, c + e - 2 * c * e, y)

    def plane(dx, dy):
        return (z, lax.rem(x + dx, X), c, flip(y, dy))

    def remote(src, dst, send, recv, where):
        return pltpu.make_async_remote_copy(
            src_ref=src, dst_ref=dst, send_sem=send, recv_sem=recv,
            device_id=where, device_id_type=MESH_ID)

    groups = [(m, e) for m in range(Z) for e in range(2) if (m, e) != (0, 0)]
    planes = [(dx, dy) for dx in range(X) for dy in range(Y) if (dx, dy) != (0, 0)]
    me = z * 2 + c
    pending = []

    cp_flat = pltpu.make_async_copy(logits_flat, ybuf, loc_sem.at[0])
    cp_flat.start()
    cp_own = pltpu.make_async_copy(logits.at[z, :, c], lbuf.at[0, 0], loc_sem.at[1])
    cp_own.start()
    cp_cells = pltpu.make_async_copy(
        own_cells, cells.at[pl.ds(pl.multiple_of((x * Y + y) * R, R), R)], loc_sem.at[2])
    cp_cells.start()
    barrier = pltpu.get_barrier_semaphore()
    for m, e in groups:
        pl.semaphore_signal(barrier, inc=1, device_id=group(m, e), device_id_type=MESH_ID)
    for dx, dy in planes:
        pl.semaphore_signal(barrier, inc=1, device_id=plane(dx, dy), device_id_type=MESH_ID)
    pl.semaphore_wait(barrier, len(groups) + len(planes))

    def rows(bx, by, half):
        return cells.at[pl.ds(pl.multiple_of(((bx * Y + by) * 2 + half) * H, H), H)]

    XN = X - 1

    def cell_copy(slot, src, bx, by, half, where):
        return remote(src, rows(bx, by, half), cl_s.at[slot], cl_r.at[slot], where)

    own_half = [own_cells.at[pl.ds(0, H)], own_cells.at[pl.ds(H, H)]]
    x_first = [cell_copy(d, own_half[0], x, y, 0, plane(d + 1, 0)) for d in range(XN)]
    x_last = [cell_copy(XN + d, own_half[1], x, y, 1, plane(d + 1, 0)) for d in range(XN)]
    y_first = cell_copy(2 * XN, own_half[1], x, y, 1, plane(0, 1))
    y_last = cell_copy(2 * XN + 1, own_half[0], x, y, 0, plane(0, 1))
    for cp in x_first + [y_first]:
        cp.start()

    high = Z // 2
    far = [m for m in range(Z) if m & high and m != high]
    near = [m for m in range(1, Z) if not m & high]
    lg = {(m, e): remote(logits.at[flip(z, m), :, flip(c, e)], lbuf.at[m, e],
                         lg_s.at[m, e], lg_r.at[m, e], group(m, e)) for m, e in groups}

    pending.extend(cp for (m, e), cp in lg.items() if m in [0] + near)

    def sent(ms):
        for m in ms:
            for e in range(2):
                lg[m, e].wait_send()

    def send_logits(ms, es=(0, 1)):
        for m in ms:
            for e in es:
                lg[m, e].start()

    at_end = (z == 0) | (z == Z - 1)
    inside = jnp.logical_not(at_end)
    lg[0, 1].start()

    @pl.when(at_end)
    def _():
        send_logits(near + far)

    @pl.when(inside)
    def _():
        send_logits([high])

    for cp in x_last + [y_last]:
        cp.start()
    pending.extend(x_first + x_last + [y_first, y_last])

    cp_flat.wait()

    def add_exp(i, acc):
        e = jnp.exp(ybuf[i].astype(F32))
        return acc + jnp.sum(e.reshape(YR // 8, 8, S), axis=0)

    acc = lax.fori_loop(0, A * X, add_exp, jnp.zeros((8, S), F32))
    inv_sum = 1.0 / jnp.sum(acc, axis=0, keepdims=True)
    idr = ids[...]
    maskf = mask[...].astype(F32)
    mrow = [jnp.where(idr == s, maskf, 0.0) for s in range(SLIDES)]
    info[0, 0] = jnp.concatenate([inv_sum] + mrow + [jnp.zeros((8 - 1 - SLIDES, S), F32)], axis=0)
    inf = {}
    for m, e in groups:
        inf[m, e] = remote(info.at[0, 0], info.at[m, e], in_s.at[m, e], in_r.at[m, e], group(m, e))
        inf[m, e].start()
        pending.append(inf[m, e])

    W = G // k.NB
    for b in range(k.NB):
        v = jnp.zeros((S, W), F32)
        for j in range(k.NB):
            here = (order[0:1, j:j + 1] == b).astype(F32)
            v = v + here * spatial[:, j * W:(j + 1) * W].astype(F32)
        meas[:, b * W:(b + 1) * W] = v.astype(BF16)
    mcols = jnp.concatenate(mrow + [maskf] + [jnp.zeros((8 - 1 - SLIDES, S), F32)], axis=0).T
    mcol = [mcols[:, s:s + 1] for s in range(SLIDES)]
    wcol = mcols[:, SLIDES:SLIDES + 1]
    meas_sq = jnp.zeros((S, 1), F32)
    for j in range(A):
        v = meas[:, j * GA:(j + 1) * GA].astype(F32)
        v = v * v
        meas_sq = meas_sq + jnp.sum(v, axis=1, keepdims=True)
        for s in range(SLIDES):
            mstat[j, s:s + 1, :] = jnp.sum(mcol[s] * v, axis=0, keepdims=True)
        mstat[j, SLIDES:8, :] = jnp.zeros((8 - SLIDES, GA), F32)
    inv_meas = lax.rsqrt(meas_sq + FLOOR)
    mst = {}
    for m, e in groups:
        mst[m, e] = remote(mstat.at[flip(z, m) * 2 + flip(c, e)], mstat_in.at[m, e],
                           mt_s.at[m, e], mt_r.at[m, e], group(m, e))
        mst[m, e].start()
    pending.extend(mst.values())

    fwd_a, fwd_b = [], []
    for d in range(XN):
        bx = lax.rem(x - (d + 1) + X, X)
        cell_copy(d, own_half[0], bx, y, 0, plane(d + 1, 0)).wait_recv()
        cp = cell_copy(2 * XN + 2 + d, rows(bx, y, 0), bx, y, 0, plane(0, 1))
        cp.start()
        fwd_a.append(cp)
    y_first.wait_recv()
    for d in range(XN):
        cp = cell_copy(3 * XN + 2 + d, rows(x, yo, 1), x, yo, 1, plane(d + 1, 0))
        cp.start()
        fwd_b.append(cp)
    pending.extend(fwd_a + fwd_b)

    cp_own.wait()
    cp_cells.wait()

    def shares_of(m, e, i):
        per = YR // RC
        l = lbuf[m, e, i // per, pl.ds(pl.multiple_of(lax.rem(i, per) * RC, RC), RC), :]
        return jnp.exp(l.astype(F32)) * info[m, e, 0:1, :]

    def t_row(m, i):
        return (m * 2 + i) * S

    def slot(cc):
        return c if cc == 0 else 1 - c

    def wait_cross(m, cc):
        e = slot(cc)
        remote(info.at[0, 0], info.at[m, e], in_s.at[m, e], in_r.at[m, e],
               group(m, e)).wait_recv()
        remote(lbuf.at[0, 0], lbuf.at[m, e], lg_s.at[m, e], lg_r.at[m, e],
               group(m, e)).wait_recv()

    def wait_pair(m):
        for e in range(2):
            if (m, e) != (0, 0):
                inf[m, e].wait_recv()
                lg[m, e].wait_recv()

    def make_shares(m, e, row):
        lane = (m * 2 + e) * S
        if type(e) is not int:
            lane = pl.multiple_of(lane, S)

        def step(i, _):
            sh = shares_of(m, e, i).astype(BF16)
            r0 = pl.multiple_of(i * RC, RC)
            slow[pl.ds(r0, RC), pl.ds(lane, S)] = sh
            slow_t[row:row + S, pl.ds(r0, RC)] = sh.T
            return 0

        lax.fori_loop(0, NC // RC, step, 0)

    def pair_shares(m):
        wait_pair(m)
        for e in range(2):
            make_shares(m, e, t_row(m, e))

    def cross_shares(m, cc):
        make_shares(m, slot(cc), t_row(m, cc))

    ps = [remote(p1.at[m], psib.at[m], ps_s.at[m], ps_r.at[m], group(0, 1)) for m in range(Z)]
    pending.extend(ps)

    def gene_loop(put):
        def step(i, _):
            put(pl.ds(pl.multiple_of(i * NN, NN), NN))
            return 0

        lax.fori_loop(0, G // NN, step, 0)

    def predict_pair(m):
        row = t_row(m, 0)

        def put(lanes):
            r = jnp.dot(slow_t[row:row + 2 * S, :], cells[:, lanes], preferred_element_type=F32)
            pacc[m, :, lanes] = r[:S]
            p1[m, :, lanes] = r[S:].astype(BF16)

        gene_loop(put)
        ps[m].start()

    def predict_cross(m, cc):
        row = t_row(m, cc)

        def part(lanes):
            return jnp.dot(slow_t[row:row + S, :], cells[:, lanes], preferred_element_type=F32)

        @pl.when(c == cc)
        def _():
            def put(lanes):
                pacc[m, :, lanes] = part(lanes)

            gene_loop(put)

        @pl.when(c != cc)
        def _():
            def put(lanes):
                p1[m, :, lanes] = part(lanes).astype(BF16)

            gene_loop(put)
            ps[m].start()

    def level_slot(b, m):
        return sum(Z >> (j + 1) for j in range(b)) + (m >> (b + 1))

    rs = {}
    for b in range(k.LV):
        step_m = 1 << b
        for m in range(0, Z, 2 * step_m):
            sl = level_slot(b, m)
            rs[b, m] = remote(psib.at[m ^ step_m], rs_in.at[sl], rs_s.at[sl], rs_r.at[sl],
                              group(step_m, 0))
    pending.extend(rs.values())

    def piece_sum(m, b):
        ps[m].wait_recv()
        for j in range(b):
            rs[j, m].wait_recv()

        def total(lanes):
            t = pacc[m, :, lanes] + psib[m, :, lanes].astype(F32)
            for j in range(b):
                t = t + rs_in[level_slot(j, m), :, lanes].astype(F32)
            return t
        return total

    def sum_level(b, m):
        total = piece_sum(m, b)
        for j in range(A):
            lanes = slice(j * GA, (j + 1) * GA)
            psib[m, :, lanes] = total(lanes).astype(BF16)

    def far_levels(cc):
        @pl.when(c == cc)
        def _():
            for b in range(top):
                send_level(b, of_level(b, far))

    def send_level(b, ms):
        for m in ms:
            sum_level(b, m)
            rs[b, m ^ (1 << b)].start()

    top = k.LV - 1
    def of_level(b, ms):
        return [m for m in reversed(ms) if m % (2 << b) == 1 << b]

    pair_shares(0)

    @pl.when(at_end)
    def _():
        sent(far)
        send_logits([high])

    @pl.when(inside)
    def _():
        sent([high])
        send_logits(near)

    pair_shares(high)

    @pl.when(inside & (c == 0))
    def _():
        send_logits(far, (1, 0))

    @pl.when(at_end)
    def _():
        for m in far:
            for cc in range(2):
                wait_cross(m, cc)
                cross_shares(m, cc)

    for m in near:
        pair_shares(m)
    for cp in x_last + [y_last] + fwd_a + fwd_b:
        cp.wait_recv()

    @pl.when(at_end)
    def _():
        for cc in range(2):
            for m in far:
                predict_cross(m, cc)
        for cc in range(2):
            far_levels(cc)

    predict_pair(high)
    for b in range(top):
        for m in of_level(b, near):
            predict_pair(m)
        send_level(b, of_level(b, near))
    @pl.when(at_end)
    def _():
        predict_pair(0)

    @pl.when(inside)
    def _():
        for m in far:
            wait_cross(m, 0)

        @pl.when(c == 1)
        def _():
            send_logits(far, (1, 0))

        for m in far:
            cross_shares(m, 0)
            predict_cross(m, 0)
        far_levels(0)
        predict_pair(0)

        @pl.when(c == 0)
        def _():
            sum_level(top, high)

        for m in far:
            wait_cross(m, 1)
            cross_shares(m, 1)
            predict_cross(m, 1)

        @pl.when(c == 0)
        def _():
            rs[top, 0].start()

        far_levels(1)

    @pl.when(at_end | (c == 1))
    def _():
        sum_level(top, high)
        rs[top, 0].start()

    mem_rows = jnp.concatenate(
        [info[m, e, 1:1 + SLIDES, :] for m in range(Z) for e in range(2)], axis=1)
    mem16 = jnp.concatenate([mem_rows, jnp.zeros((16 - SLIDES, A * S), F32)], axis=0).astype(BF16)
    part = lax.dot_general(mem16, slow[...], (((1,), (1,)), ((), ())), preferred_element_type=F32)
    col_tally = jnp.sum(mem_rows, axis=1, keepdims=True)
    gmeas = mstat[me]
    for m, e in groups:
        mst[m, e].wait_recv()
        gmeas = gmeas + mstat_in[m, e]
    packed = [gmeas[s:s + 1] for s in range(SLIDES)] + [jnp.zeros((1, NC - SLIDES * GA), F32)]
    mass_out[...] = jnp.concatenate(
        [part[:SLIDES], jnp.broadcast_to(col_tally, (SLIDES, NC)),
         jnp.concatenate(packed, axis=1), jnp.zeros((1, NC), F32)], axis=0)
    mcp = []
    for i, (dx, dy) in enumerate(planes):
        cp = remote(mass_out, mass_in.at[i], ms_s.at[i], ms_r.at[i], plane(dx, dy))
        cp.start()
        mcp.append(cp)
    pending.extend(mcp)
    for cp in mcp:
        cp.wait_recv()
    msum = mass_out[...]
    for i in range(Q - 1):
        msum = msum + mass_in[i]
    mass = msum[:SLIDES]
    gmeas = jnp.concatenate(
        [msum[6:7, s * GA:(s + 1) * GA] for s in range(SLIDES)], axis=0)
    inv_gmeas = lax.rsqrt(gmeas + FLOOR)
    tally = jnp.maximum(msum[SLIDES:2 * SLIDES, 0:1], 1.0)
    quota = mass / tally
    prior_sum = jnp.sum(jnp.sum(cell_prior[...], axis=0, keepdims=True), axis=1, keepdims=True)
    prior = jnp.concatenate(
        [cell_prior[pl.ds(((z * X + bx) * 2 + c) * (YR // k.PL) + i, 1), :]
         for bx in range(X) for i in range(YR // k.PL)], axis=1) / prior_sum
    kl = jnp.sum(prior * (jnp.log(prior) - jnp.log(quota)), axis=1, keepdims=True)
    rat = prior / quota
    rat_hi = rat.astype(BF16)
    rat_lo = (rat - rat_hi.astype(F32)).astype(BF16)
    ratio_hl[...] = jnp.concatenate(
        [rat_hi, rat_lo, jnp.zeros((16 - 2 * SLIDES, NC), BF16)], axis=0)
    dd = jnp.dot(ratio_hl[...], slow[...], preferred_element_type=F32)
    dd = dd[:SLIDES] + dd[SLIDES:2 * SLIDES]
    dsum = jnp.sum(dd * mem_rows, axis=0, keepdims=True)
    mext[...] = jnp.concatenate(
        [mem_rows, mem_rows, jnp.zeros((16 - 2 * SLIDES, A * S), F32)], axis=0).astype(BF16)
    dcp = {}
    for m in range(Z):
        for e in range(2):
            lane = (m * 2 + e) * S
            dpart[m, e] = jnp.broadcast_to(dsum[:, lane:lane + S], (8, S))
    for m, e in groups:
        cp = remote(dpart.at[m, e], din.at[m, e], d_s.at[m, e], d_r.at[m, e], group(m, e))
        cp.start()
        dcp[m, e] = cp
        pending.append(cp)

    total = piece_sum(0, k.LV)
    pred_sq = jnp.zeros((S, 1), F32)
    pred_meas = jnp.zeros((S, 1), F32)
    lane_id = lax.broadcasted_iota(jnp.int32, (1, GA), 1)
    for j in range(A):
        lanes = slice(j * GA, (j + 1) * GA)
        p = total(lanes)
        pacc[0, :, lanes] = p
        q = meas[:, lanes].astype(F32)
        pq, pp = p * q, p * p
        pred_sq = pred_sq + jnp.sum(pp, axis=1, keepdims=True)
        pred_meas = pred_meas + jnp.sum(pq, axis=1, keepdims=True)
        for s in range(SLIDES):
            stat[j, s:s + 1, :] = jnp.sum(mcol[s] * pq, axis=0, keepdims=True)
            stat[j, 3 + s:4 + s, :] = jnp.sum(mcol[s] * pp, axis=0, keepdims=True)
    inv_pred = lax.rsqrt(pred_sq + FLOOR)
    spot_cos = pred_meas * inv_pred * inv_meas
    spot_sum = jnp.sum(wcol * spot_cos, axis=0, keepdims=True)
    scal = jnp.where(lane_id == 0, spot_sum, 0.0)
    for s in range(SLIDES):
        scal = scal + jnp.where(lane_id == 1 + s, kl[s:s + 1] * (1.0 / Q), 0.0)
    for j in range(A):
        stat[j, 6:8, :] = jnp.concatenate([scal, jnp.zeros((1, GA), F32)], axis=0)

    cps = {}
    for m, e in groups:
        cp = remote(stat.at[flip(z, m) * 2 + flip(c, e)], s1.at[m, e],
                    s1_s.at[m, e], s1_r.at[m, e], group(m, e))
        cp.start()
        cps[m, e] = cp
        pending.append(cp)
    u = stat[me]
    for m, e in groups:
        cps[m, e].wait_recv()
        u = u + s1[m, e]
    ubuf[...] = u
    cps = []
    for i, (dx, dy) in enumerate(planes):
        cp = remote(ubuf, s2.at[i], s2_s.at[i], s2_r.at[i], plane(dx, dy))
        cp.start()
        cps.append(cp)
        pending.append(cp)
    for i, cp in enumerate(cps):
        cp.wait_recv()
        u = u + s2[i]
    share = tally * (1.0 / G)
    a = lax.rsqrt(u[3:6] + FLOOR)
    b = inv_gmeas
    gcos = u[0:3] * a * b
    wall[me] = jnp.concatenate(
        [share * a * b, share * gcos * a * a,
         jnp.sum(share * gcos, axis=0, keepdims=True), u[6:7]], axis=0)
    cps = []
    for m, e in groups:
        cp = remote(wall.at[me], wall.at[me], s3_s.at[m, e], s3_r.at[m, e], group(m, e))
        cp.start()
        cps.append(cp)
        pending.append(cp)
    for (m, e) in groups:
        other = flip(z, m) * 2 + flip(c, e)
        remote(wall.at[other], wall.at[other], s3_s.at[m, e], s3_r.at[m, e], group(m, e)).wait_recv()

    lead = -(wcol * inv_pred * inv_meas)
    back = wcol * spot_cos * inv_pred * inv_pred
    dot1 = jnp.zeros((S, 1), F32)
    gene_total = jnp.zeros((1, GA), F32)
    for j in range(A):
        lanes = slice(j * GA, (j + 1) * GA)
        w = wall[j]
        direct = mcol[0] * w[0:1] + mcol[1] * w[1:2] + mcol[2] * w[2:3]
        damp = mcol[0] * w[3:4] + mcol[1] * w[4:5] + mcol[2] * w[5:6]
        gene_total = gene_total + w[6:7]
        p = pacc[0, :, lanes]
        g = (lead - direct) * meas[:, lanes].astype(F32) + (back + damp) * p
        glow = g.astype(BF16)
        gp[0, 0, :, lanes] = glow
        dot1 = dot1 + jnp.sum(glow.astype(F32) * p, axis=1, keepdims=True)

    gz, gc = {}, {}

    def to_core(m):
        cp = remote(gp.at[m, 0], gp.at[m, 1], gc_s.at[m], gc_r.at[m], group(0, 1))
        cp.start()
        gc[m] = cp
        pending.append(cp)

    def to_plane(m, b):
        t = m ^ (1 << b)
        cp = remote(gp.at[m, 0], gp.at[t, 0], gz_s.at[t], gz_r.at[t], group(1 << b, 0))
        cp.start()
        gz[t] = cp
        pending.append(cp)

    to_core(0)
    gz[high] = remote(gp.at[0, 0], gp.at[high, 0], gz_s.at[high], gz_r.at[high], group(high, 0))

    for b in range(top):
        t = 1 << b
        gz[t] = remote(gp.at[0, 0], gp.at[t, 0], gz_s.at[t], gz_r.at[t], group(t, 0))

    def near_start():
        for b in reversed(range(top)):
            gz[1 << b].start()

    @pl.when(c == 0)
    def _():
        gz[high].start()

    @pl.when(c == 1)
    def _():
        near_start()

    for m, e in groups:
        dcp[m, e].wait_recv()
    dtot = dpart[0, 0]
    for m, e in groups:
        dtot = dtot + din[m, e]
    dot_row = jnp.broadcast_to(dot1, (S, S)).T[0:8] - dtot
    info2[0, 0] = dot_row
    i2 = {}
    for m, e in groups:
        cp = remote(info2.at[0, 0], info2.at[m, e], i2_s.at[m, e], i2_r.at[m, e], group(m, e))
        cp.start()
        i2[m, e] = cp
        pending.append(cp)

    fin = wall[0]
    total_tally = jnp.sum(tally, axis=0, keepdims=True)
    gsum = jnp.sum(gene_total, axis=1, keepdims=True)
    dens = jnp.zeros((1, 1), F32)
    for s in range(SLIDES):
        dens = dens + tally[s:s + 1] * fin[7:8, 1 + s:2 + s]
    lid = lax.broadcasted_iota(jnp.int32, (8, 128), 1)
    out_loss[...] = (jnp.where(lid == 0, fin[7:8, 0:1], 0.0) + jnp.where(lid == 1, gsum, 0.0)
                     + jnp.where(lid == 2, dens, 0.0)) / total_tally

    ycp = {}

    def map_rows(m, es, gpm):
        n = len(es)

        def step(i, _):
            r0 = pl.multiple_of(i * RC, RC)
            low = lax.dot_general(cells[pl.ds(r0, RC), :], gpm(),
                                  (((1,), (1,)), ((), ())), preferred_element_type=F32)
            mx = [mext[:, pl.ds(pl.multiple_of((m * 2 + e) * S, S), S)] for e in es]
            rt = lax.dot_general(ratio_hl[:, pl.ds(r0, RC)], jnp.concatenate(mx, axis=1),
                                 (((0,), (0,)), ((), ())), preferred_element_type=F32)
            low = low - rt
            per = YR // RC
            for i_e, e in enumerate(es):
                sh = shares_of(m, e, i) * float(k.CELLS)
                v = sh * (low[:, i_e * S:(i_e + 1) * S] - info2[m, e, 0:1, :])
                ybuf[(m * 2 + e) * X + i // per,
                     pl.ds(pl.multiple_of(lax.rem(i, per) * RC, RC), RC), :] = v.astype(BF16)
            return 0

        lax.fori_loop(0, NC // RC, step, 0)

    def map_copies(m, es):
        cps = []
        for e in es:
            src = ybuf.at[pl.ds((m * 2 + e) * X, X)]
            if m == 0 and type(e) is int and e == 0:
                cps.append(pltpu.make_async_copy(src, out_map.at[z, :, c], loc_sem.at[3]))
                ycp[0, 0] = cps[-1]
            else:
                cps.append(remote(src, out_map.at[z, :, c], y_s.at[m, e], y_r.at[m, e],
                                  group(m, e)))
                pending.append(cps[-1])
        return cps

    def send_map(m, es):
        for cp in map_copies(m, es):
            cp.start()

    def map_piece(m):
        for e in range(2):
            if (m, e) != (0, 0):
                i2[m, e].wait_recv()
        map_rows(m, [0, 1], lambda: gp[m].reshape(2 * S, G))
        send_map(m, [0, 1])

    gc[0].wait_recv()
    map_piece(0)

    def pass_on(m, b):
        for b2 in reversed(range(b)):
            to_plane(m, b2)
        to_core(m)

    gc[high] = remote(gp.at[high, 0], gp.at[high, 1], gc_s.at[high], gc_r.at[high], group(0, 1))
    pending.append(gc[high])
    for b2 in range(top):
        t = high ^ (1 << b2)
        gz[t] = remote(gp.at[high, 0], gp.at[t, 0], gz_s.at[t], gz_r.at[t], group(1 << b2, 0))
        pending.append(gz[t])

    def high_on():
        gz[high].wait_recv()
        gc[high].start()
        for b2 in reversed(range(top)):
            gz[high ^ (1 << b2)].start()

    @pl.when(c == 0)
    def _():
        gz[high].wait_send()
        pl.semaphore_signal(gate, inc=1, device_id=group(0, 1), device_id_type=MESH_ID)
        near_start()
        high_on()

    @pl.when(c == 1)
    def _():
        pl.semaphore_wait(gate, 1)
        gz[high].start()
        gc[high].wait_recv()

    i2[high, 0].wait_recv()
    i2[high, 1].wait_recv()
    map_rows(high, [c], lambda: gp[high, c])

    @pl.when(c == 1)
    def _():
        high_on()

    @pl.when(c == 0)
    def _():
        gc[high].wait_recv()

    own_core = map_copies(high, [c])

    @pl.when(at_end)
    def _():
        own_core[0].start()

    map_rows(high, [1 - c], lambda: gp[high, 1 - c])

    @pl.when(inside)
    def _():
        own_core[0].start()

    send_map(high, [1 - c])
    for b in reversed(range(top)):
        for m in range(1 << b, Z, 2 << b):
            gz[m].wait_recv()
            pass_on(m, b)
    def slot_of(dx, dy, half):
        return ((dx * Y + dy) - 1) * 2 + half

    def single_rows(dx, dy, half):
        bx = lax.rem(x + dx, X)
        by = flip(y, dy)
        return pl.multiple_of(((bx * Y + by) * 2 + half) * H, H)

    def single_part(dx, dy, half, put, m0=0, m1=Z):
        r0 = single_rows(dx, dy, half)
        n = (m1 - m0) * 2 * S

        def step(i, _):
            lanes = pl.ds(pl.multiple_of(i * NN, NN), NN)
            v = jnp.dot(slow[pl.ds(r0, H), m0 * 2 * S:m1 * 2 * S],
                        gp[pl.ds(m0, m1 - m0), :, :, lanes].reshape(n, NN), preferred_element_type=F32)
            put(lanes, v)
            return 0

        lax.fori_loop(0, G // NN, step, 0)

    def put_send(slot, extra=()):
        def put(lanes, v):
            for i in extra:
                v = v + grecv[i, :, lanes].astype(F32)
            gsend[slot, :, lanes] = v.astype(BF16)
        return put

    def put_own(half):
        def put(lanes, v):
            own_single[half * H:(half + 1) * H, lanes] = v
        return put

    def put_rest(sl, half):
        def put(lanes, v):
            v = v + own_single[half * H:(half + 1) * H, lanes]
            gsend[sl, :, lanes] = v.astype(BF16)
        return put

    r_m1 = lambda d: d
    r_m2 = lambda d: XN + d
    r_m3 = lambda d: 2 * XN + d
    r_m5 = lambda d: 3 * XN + d
    r_m4, r_m6 = 4 * XN, 4 * XN + 1
    gcp = {}

    def send_single(slot, r_slot, where):
        cp = remote(gsend.at[slot], grecv.at[r_slot], gs_s.at[r_slot], gs_r.at[r_slot], where)
        cp.start()
        gcp[r_slot] = cp
        pending.append(cp)

    for m in range(1, Z - 1):
        if m != high:
            gc[m].wait_recv()
    for half in range(2):
        single_part(1, 1, half, put_own(half), 0, Z - 1)
    if Z > 2:
        gc[Z - 1].wait_recv()
    for d in range(XN):
        for half in range(2):
            sl = slot_of(d + 1, 1, half)
            if d == 0:
                single_part(1, 1, half, put_rest(sl, half), Z - 1, Z)
            else:
                single_part(d + 1, 1, half, put_send(sl))
            if half == 0:
                send_single(sl, r_m1(d), plane(d + 1, 0))
            else:
                send_single(sl, r_m2(d), plane(0, 1))
    for m in far:
        map_piece(m)
    for d in range(XN):
        s0 = slot_of(d + 1, 0, 0)
        single_part(d + 1, 0, 0, put_send(s0))
        send_single(s0, r_m3(d), plane(d + 1, 0))
    s0 = slot_of(0, 1, 1)
    single_part(0, 1, 1, put_send(s0))
    send_single(s0, r_m4, plane(0, 1))

    for m in near:
        map_piece(m)

    for d in range(XN):
        gcp[r_m2(d)].wait_recv()
        s0 = slot_of(d + 1, 0, 1)
        single_part(d + 1, 0, 1, put_send(s0, [r_m2(d)]))
        send_single(s0, r_m5(d), plane(d + 1, 0))
    for d in range(XN):
        gcp[r_m1(d)].wait_recv()
    s0 = slot_of(0, 1, 0)
    single_part(0, 1, 0, put_send(s0, [r_m1(d) for d in range(XN)]))
    send_single(s0, r_m6, plane(0, 1))

    for half in range(2):
        single_part(0, 0, half, put_own(half))
    cp_single = []
    halves = [[r_m3(d) for d in range(XN)] + [r_m6], [r_m5(d) for d in range(XN)] + [r_m4]]
    for half in range(2):
        for i in halves[half]:
            gcp[i].wait_recv()

        def step(i, _):
            lanes = pl.ds(pl.multiple_of(i * NN, NN), NN)
            v = own_single[half * H:(half + 1) * H, lanes]
            for i2_ in halves[half]:
                v = v + grecv[i2_, :, lanes].astype(F32)
            own_single[half * H:(half + 1) * H, lanes] = v * float(k.CELLS) ** 0.5
            return 0

        lax.fori_loop(0, G // NN, step, 0)
        rows_h = pl.ds(half * H, H)
        cp_single.append(pltpu.make_async_copy(
            own_single.at[rows_h], out_single.at[rows_h], loc_sem.at[4 + half]))
        cp_single[half].start()

    for m, e in groups:
        other = (flip(z, m), slice(None), flip(c, e))
        remote(ybuf.at[pl.ds(0, X)], out_map.at[other[0], :, other[2]], y_s.at[m, e], y_r.at[m, e],
               group(m, e)).wait_recv()
    ycp[0, 0].wait()
    for cp in cp_single:
        cp.wait()
    for cp in pending:
        cp.wait_send()
    for b in range(top):
        gz[1 << b].wait_send()

    @pl.when(c == 1)
    def _():
        gz[high].wait_send()

    @pl.when(at_end)
    def _():
        sent([high])

    @pl.when(inside)
    def _():
        sent(far)


def forward_and_back(k, logits, single_cell, spatial, ids, mask, cell_prior, order):
    Z, X, Y, A, Q, S, G, R, H = k.Z, k.X, k.Y, k.A, k.Q, k.S, k.G, k.R, k.H
    YR, NC, GA, XN = k.YR, k.NC, k.GA, k.X - 1
    vm = pl.BlockSpec(memory_space=pltpu.VMEM)
    hbm = pl.BlockSpec(memory_space=pl.ANY)
    dma = lambda *s: pltpu.SemaphoreType.DMA(s)
    ncl, ngs = 4 * XN + 2, 4 * XN + 2
    scratch = [
        pltpu.VMEM((Z, 2, X, YR, S), BF16),
        pltpu.VMEM((NC, G), BF16),
        pltpu.VMEM((NC, A * S), BF16),
        pltpu.VMEM((A * S, NC), BF16),
        pltpu.VMEM((A * X, YR, S), BF16),
        pltpu.VMEM((Z, 2, 8, S), F32),
        pltpu.VMEM((Z, 2, 8, S), F32),
        pltpu.VMEM((Z, S, G), F32),
        pltpu.VMEM((Z, S, G), BF16),
        pltpu.VMEM((Z, S, G), BF16),
        pltpu.VMEM((Z - 1, S, G), BF16),
        pltpu.VMEM((S, G), BF16),
        pltpu.VMEM((Z, 2, S, G), BF16),
        pltpu.VMEM((2 * (Q - 1), H, G), BF16),
        pltpu.VMEM((ngs, H, G), BF16),
        pltpu.VMEM((8, NC), F32),
        pltpu.VMEM((Q - 1, 8, NC), F32),
        pltpu.VMEM((16, NC), BF16),
        pltpu.VMEM((16, A * S), BF16),
        pltpu.VMEM((Z, 2, 8, S), F32),
        pltpu.VMEM((Z, 2, 8, S), F32),
        pltpu.VMEM((A, 8, GA), F32),
        pltpu.VMEM((Z, 2, 8, GA), F32),
        pltpu.VMEM((A, 8, GA), F32),
        pltpu.VMEM((Z, 2, 8, GA), F32),
        pltpu.VMEM((8, GA), F32),
        pltpu.VMEM((Q - 1, 8, GA), F32),
        pltpu.VMEM((A, 8, GA), F32),
        pltpu.VMEM((R, G), F32),
        dma(6),
        dma(Z, 2), dma(Z, 2),
        dma(ncl), dma(ncl),
        dma(Z, 2), dma(Z, 2),
        dma(Z), dma(Z),
        dma(Z - 1), dma(Z - 1),
        dma(Q - 1), dma(Q - 1),
        dma(Z, 2), dma(Z, 2),
        dma(Z, 2), dma(Z, 2),
        dma(Q - 1), dma(Q - 1),
        dma(Z, 2), dma(Z, 2),
        dma(Z), dma(Z),
        dma(Z), dma(Z),
        dma(Z, 2), dma(Z, 2),
        dma(Z, 2), dma(Z, 2),
        dma(ngs), dma(ngs),
        dma(Z, 2), dma(Z, 2),
        pltpu.SemaphoreType.REGULAR,
    ]
    return pl.pallas_call(
        functools.partial(kernel, k),
        name="mapping",
        out_shape=[
            jax.ShapeDtypeStruct((Z, X, 2, YR, S), BF16),
            jax.ShapeDtypeStruct((R, G), F32),
            jax.ShapeDtypeStruct((8, 128), F32),
        ],
        in_specs=[hbm, hbm, hbm, vm, vm, vm, vm, vm],
        out_specs=[hbm, hbm, vm],
        scratch_shapes=scratch,
        compiler_params=pltpu.CompilerParams(
            collective_id=0, has_side_effects=True, vmem_limit_bytes=64000 * 1024),
        cost_estimate=pl.CostEstimate(
            flops=6 * NC * A * S * G, bytes_accessed=32 << 20, transcendentals=2 * NC * A * S),
    )(logits.reshape(Z, X, 2, YR, S), logits.reshape(A * X, YR, S), single_cell, spatial,
      ids.reshape(1, S), mask.reshape(1, S), cell_prior.reshape(-1, k.PL), order.reshape(1, k.NB))


def body(mesh, map_logits, single_cell, spatial, slide_ids, spot_mask, cell_prior, gene_order):
    cells, spots = map_logits.shape
    k = Sizes(mesh, cells, spatial.shape[1], spots, gene_order.shape[0])
    gmap, gsingle, loss = forward_and_back(
        k, map_logits, single_cell, spatial, slide_ids, spot_mask, cell_prior, gene_order)
    grad_map = gmap.reshape(cells, spots).astype(F32)
    return loss[0, :3], grad_map, gsingle


def solution(mesh):
    k = Sizes(mesh, 1 << 20, 1 << 20, 128, 1)
    fine = Mesh(mesh.devices.reshape(k.Z, k.X, 2, k.Y), AXES)
    in_specs = (P(None, AXES), P(AXES, None), P(AXES, None), P(AXES), P(AXES), P(), P())
    out_specs = (P(), P(None, AXES), P(AXES, None))
    return jax.shard_map(functools.partial(body, mesh), mesh=fine, in_specs=in_specs,
                         out_specs=out_specs, check_vma=False)
```

```python
import functools

import jax
import jax.numpy as jnp
from jax import lax
from jax.experimental import pallas as pl
from jax.experimental.pallas import tpu as pltpu
from jax.sharding import Mesh, PartitionSpec as P

SLIDES = 3
HALVES = 2
FLOOR = 1e-06
F32 = jnp.float32
BF16 = jnp.bfloat16
AXES = ("z", "x", "c", "y")
MESH_ID = pl.DeviceIdType.MESH


def flip(value, mask):
    bit = 1
    while bit <= mask:
        if mask & bit:
            value = value + (1 - 2 * ((value // bit) % 2)) * bit
        bit *= 2
    return value


class Sizes:
    def __init__(self, mesh, cells, genes, spots, blocks):
        n = mesh.shape["spot"] // 2
        zs = 1
        while zs * zs * 4 <= 2 * n:
            zs *= 2
        self.Z, self.X, self.Y = zs, n // zs, mesh.shape["grp"]
        assert self.Y == 2 and self.Z * self.X == n and self.Z >= 2
        self.LV = self.Z.bit_length() - 1
        self.A = 2 * self.Z
        self.Q = self.X * self.Y
        self.CELLS, self.G, self.S, self.NB = cells, genes, spots, blocks
        self.R = cells // (self.A * self.Q)
        self.H = self.R // 2
        self.YR = self.Y * self.R
        self.NC = self.X * self.YR
        self.GA = genes // self.A
        self.RC = min(256, self.YR)
        self.PL = min(128, self.YR)
        self.NN = min(512, genes)


def kernel(k, logits, logits_flat, own_cells, spatial, ids, mask, cell_prior, order,
           out_map, out_single, out_loss,
           lbuf, cells, slow, slow_t, ybuf, info, info2,
           pacc, p1, psib, rs_in, meas,
           gp, gsend, grecv,
           mass_out, mass_in, ratio_hl, mext, dpart, din,
           mstat, mstat_in, stat, s1, ubuf, s2, wall, own_single,
           loc_sem, lg_s, lg_r, cl_s, cl_r, in_s, in_r, ps_s, ps_r, rs_s, rs_r, ms_s, ms_r,
           d_s, d_r, s1_s, s1_r, s2_s, s2_r, s3_s, s3_r, gz_s, gz_r, gc_s, gc_r, i2_s, i2_r,
           y_s, y_r, gs_s, gs_r, mt_s, mt_r, gate):
    Z, X, Y, A, Q, S, G, R, H = k.Z, k.X, k.Y, k.A, k.Q, k.S, k.G, k.R, k.H
    YR, NC, GA, RC, NN = k.YR, k.NC, k.GA, k.RC, k.NN
    z, x, c, y = [lax.axis_index(a) for a in AXES]
    yo = 1 - y

    def group(m, e):
        return (flip(z, m), x, c + e - 2 * c * e, y)

    def plane(dx, dy):
        return (z, lax.rem(x + dx, X), c, flip(y, dy))

    def remote(src, dst, send, recv, where):
        return pltpu.make_async_remote_copy(
            src_ref=src, dst_ref=dst, send_sem=send, recv_sem=recv,
            device_id=where, device_id_type=MESH_ID)

    groups = [(m, e) for m in reversed(range(Z)) for e in (1, 0) if (m, e) != (0, 0)]
    planes = [(dx, dy) for dx in reversed(range(X)) for dy in (1, 0) if (dx, dy) != (0, 0)]
    me = z * 2 + c
    pending = []

    cp_flat = pltpu.make_async_copy(logits_flat, ybuf, loc_sem.at[0])
    cp_flat.start()
    cp_own = pltpu.make_async_copy(logits.at[z, :, c], lbuf.at[0, 0], loc_sem.at[1])
    cp_own.start()
    cp_cells = pltpu.make_async_copy(
        own_cells, cells.at[pl.ds(pl.multiple_of((x * Y + y) * R, R), R)], loc_sem.at[2])
    cp_cells.start()
    barrier = pltpu.get_barrier_semaphore()
    for m, e in groups:
        pl.semaphore_signal(barrier, inc=1, device_id=group(m, e), device_id_type=MESH_ID)
    for dx, dy in planes:
        pl.semaphore_signal(barrier, inc=1, device_id=plane(dx, dy), device_id_type=MESH_ID)
    pl.semaphore_wait(barrier, len(groups) + len(planes))

    def rows(bx, by, half):
        return cells.at[pl.ds(pl.multiple_of(((bx * Y + by) * 2 + half) * H, H), H)]

    XN = X - 1

    def cell_copy(slot, src, bx, by, half, where):
        return remote(src, rows(bx, by, half), cl_s.at[slot], cl_r.at[slot], where)

    own_half = [own_cells.at[pl.ds(0, H)], own_cells.at[pl.ds(H, H)]]
    x_first = [cell_copy(d, own_half[0], x, y, 0, plane(d + 1, 0)) for d in range(XN)]
    x_last = [cell_copy(XN + d, own_half[1], x, y, 1, plane(d + 1, 0)) for d in range(XN)]
    y_first = cell_copy(2 * XN, own_half[1], x, y, 1, plane(0, 1))
    y_last = cell_copy(2 * XN + 1, own_half[0], x, y, 0, plane(0, 1))
    for cp in x_first + [y_first]:
        cp.start()

    high = Z // 2
    far = [m for m in range(Z) if m & high and m != high]
    near = [m for m in range(1, Z) if not m & high]
    lg = {(m, e): remote(logits.at[flip(z, m), :, flip(c, e)], lbuf.at[m, e],
                         lg_s.at[m, e], lg_r.at[m, e], group(m, e)) for m, e in groups}

    pending.extend(cp for (m, e), cp in lg.items() if m in [0] + near)

    def sent(ms):
        for m in ms:
            for e in range(2):
                lg[m, e].wait_send()

    def send_logits(ms, es=(0, 1)):
        for m in ms:
            for e in es:
                lg[m, e].start()

    at_end = (z == 0) | (z == Z - 1)
    inside = jnp.logical_not(at_end)
    lg[0, 1].start()

    @pl.when(at_end)
    def _():
        send_logits(near + far)

    @pl.when(inside)
    def _():
        send_logits([high])

    for cp in x_last + [y_last]:
        cp.start()
    pending.extend(x_first + x_last + [y_first, y_last])

    cp_flat.wait()

    def add_exp(i, acc):
        e = jnp.exp(ybuf[i].astype(F32))
        return acc + jnp.sum(e.reshape(YR // 8, 8, S), axis=0)

    acc = lax.fori_loop(0, A * X, add_exp, jnp.zeros((8, S), F32))
    inv_sum = 1.0 / jnp.sum(acc, axis=0, keepdims=True)
    idr = ids[...]
    maskf = mask[...].astype(F32)
    mrow = [jnp.where(idr == s, maskf, 0.0) for s in range(SLIDES)]
    info[0, 0] = jnp.concatenate([inv_sum] + mrow + [jnp.zeros((8 - 1 - SLIDES, S), F32)], axis=0)
    inf = {}
    for m, e in groups:
        inf[m, e] = remote(info.at[0, 0], info.at[m, e], in_s.at[m, e], in_r.at[m, e], group(m, e))
        inf[m, e].start()
        pending.append(inf[m, e])

    W = G // k.NB
    for b in range(k.NB):
        v = jnp.zeros((S, W), F32)
        for j in range(k.NB):
            here = (order[0:1, j:j + 1] == b).astype(F32)
            v = v + here * spatial[:, j * W:(j + 1) * W].astype(F32)
        meas[:, b * W:(b + 1) * W] = v.astype(BF16)
    mcols = jnp.concatenate(mrow + [maskf] + [jnp.zeros((8 - 1 - SLIDES, S), F32)], axis=0).T
    mcol = [mcols[:, s:s + 1] for s in range(SLIDES)]
    wcol = mcols[:, SLIDES:SLIDES + 1]
    meas_sq = jnp.zeros((S, 1), F32)
    for j in range(A):
        v = meas[:, j * GA:(j + 1) * GA].astype(F32)
        v = v * v
        meas_sq = meas_sq + jnp.sum(v, axis=1, keepdims=True)
        for s in range(SLIDES):
            mstat[j, s:s + 1, :] = jnp.sum(mcol[s] * v, axis=0, keepdims=True)
        mstat[j, SLIDES:8, :] = jnp.zeros((8 - SLIDES, GA), F32)
    inv_meas = lax.rsqrt(meas_sq + FLOOR)
    mst = {}
    for m, e in groups:
        mst[m, e] = remote(mstat.at[flip(z, m) * 2 + flip(c, e)], mstat_in.at[m, e],
                           mt_s.at[m, e], mt_r.at[m, e], group(m, e))
        mst[m, e].start()
    pending.extend(mst.values())

    fwd_a, fwd_b = [], []
    for d in range(XN):
        bx = lax.rem(x - (d + 1) + X, X)
        cell_copy(d, own_half[0], bx, y, 0, plane(d + 1, 0)).wait_recv()
        cp = cell_copy(2 * XN + 2 + d, rows(bx, y, 0), bx, y, 0, plane(0, 1))
        cp.start()
        fwd_a.append(cp)
    y_first.wait_recv()
    for d in range(XN):
        cp = cell_copy(3 * XN + 2 + d, rows(x, yo, 1), x, yo, 1, plane(d + 1, 0))
        cp.start()
        fwd_b.append(cp)
    pending.extend(fwd_a + fwd_b)

    cp_own.wait()
    cp_cells.wait()

    def shares_of(m, e, i):
        per = YR // RC
        l = lbuf[m, e, i // per, pl.ds(pl.multiple_of(lax.rem(i, per) * RC, RC), RC), :]
        return jnp.exp(l.astype(F32)) * info[m, e, 0:1, :]

    def t_row(m, i):
        return (m * 2 + i) * S

    def slot(cc):
        return c if cc == 0 else 1 - c

    def wait_cross(m, cc):
        e = slot(cc)
        remote(info.at[0, 0], info.at[m, e], in_s.at[m, e], in_r.at[m, e],
               group(m, e)).wait_recv()
        remote(lbuf.at[0, 0], lbuf.at[m, e], lg_s.at[m, e], lg_r.at[m, e],
               group(m, e)).wait_recv()

    def wait_pair(m):
        for e in range(2):
            if (m, e) != (0, 0):
                inf[m, e].wait_recv()
                lg[m, e].wait_recv()

    def make_shares(m, e, row):
        lane = (m * 2 + e) * S
        if type(e) is not int:
            lane = pl.multiple_of(lane, S)

        def step(i, _):
            sh = shares_of(m, e, i).astype(BF16)
            r0 = pl.multiple_of(i * RC, RC)
            slow[pl.ds(r0, RC), pl.ds(lane, S)] = sh
            slow_t[row:row + S, pl.ds(r0, RC)] = sh.T
            return 0

        lax.fori_loop(0, NC // RC, step, 0)

    def pair_shares(m):
        wait_pair(m)
        for e in range(2):
            make_shares(m, e, t_row(m, e))

    def cross_shares(m, cc):
        make_shares(m, slot(cc), t_row(m, cc))

    gene_part = [pl.ds(h * (G // HALVES), G // HALVES) for h in range(HALVES)]

    class Parts:
        def __init__(self, make):
            self.cps = [make(h) for h in range(HALVES)]

        def start(self):
            for cp in self.cps:
                cp.start()

        def wait_send(self):
            for cp in self.cps:
                cp.wait_send()

    def sibling_part(m):
        return Parts(lambda h: remote(
            p1.at[m, :, gene_part[h]], psib.at[m, :, gene_part[h]], ps_s.at[m, h], ps_r.at[m, h],
            group(0, 1)))

    ps = [sibling_part(m) for m in range(Z)]
    pending.extend(ps)

    def gene_loop(put, h=0, parts=1):
        n = G // NN // parts

        def step(i, _):
            put(pl.ds(pl.multiple_of(i * NN, NN), NN))
            return 0

        lax.fori_loop(h * n, (h + 1) * n, step, 0)

    def predict_pair(m):
        row = t_row(m, 0)

        def put(lanes):
            r = jnp.dot(slow_t[row:row + 2 * S, :], cells[:, lanes], preferred_element_type=F32)
            pacc[m, :, lanes] = r[:S]
            p1[m, :, lanes] = r[S:].astype(BF16)

        gene_loop(put)
        ps[m].start()

    def predict_cross(m, cc):
        row = t_row(m, cc)

        def part(lanes):
            return jnp.dot(slow_t[row:row + S, :], cells[:, lanes], preferred_element_type=F32)

        @pl.when(c == cc)
        def _():
            def put(lanes):
                pacc[m, :, lanes] = part(lanes)

            gene_loop(put)

        @pl.when(c != cc)
        def _():
            def put(lanes):
                p1[m, :, lanes] = part(lanes).astype(BF16)

            for h in range(HALVES):
                gene_loop(put, h, HALVES)
                ps[m].cps[h].start()

    def level_slot(b, m):
        return sum(Z >> (j + 1) for j in range(b)) + (m >> (b + 1))

    def level_part(b, m):
        sl, step_m = level_slot(b, m), 1 << b
        return Parts(lambda h: remote(
            psib.at[m ^ step_m, :, gene_part[h]], rs_in.at[sl, :, gene_part[h]],
            rs_s.at[sl, h], rs_r.at[sl, h], group(step_m, 0)))

    rs = {(b, m): level_part(b, m) for b in range(k.LV) for m in range(0, Z, 2 << b)}
    pending.extend(rs.values())

    def piece_sum(m, b, h):
        ps[m].cps[h].wait_recv()
        for j in range(b):
            rs[j, m].cps[h].wait_recv()

        def total(lanes):
            t = pacc[m, :, lanes] + psib[m, :, lanes].astype(F32)
            for j in range(b):
                t = t + rs_in[level_slot(j, m), :, lanes].astype(F32)
            return t
        return total

    per_part = A // HALVES

    def sum_level(b, m, send=True):
        for h in range(HALVES):
            total = piece_sum(m, b, h)
            for j in range(h * per_part, (h + 1) * per_part):
                lanes = slice(j * GA, (j + 1) * GA)
                psib[m, :, lanes] = total(lanes).astype(BF16)
            if send:
                rs[b, m ^ (1 << b)].cps[h].start()

    def far_levels(cc):
        @pl.when(c == cc)
        def _():
            for b in range(top):
                send_level(b, of_level(b, far))

    def send_level(b, ms):
        for m in ms:
            sum_level(b, m)

    top = k.LV - 1
    def of_level(b, ms):
        return [m for m in reversed(ms) if m % (2 << b) == 1 << b]

    pair_shares(0)

    @pl.when(at_end)
    def _():
        sent(far)
        send_logits([high])

    @pl.when(inside)
    def _():
        sent([high])
        send_logits(near)

    pair_shares(high)

    @pl.when(inside & (c == 0))
    def _():
        send_logits(far, (1, 0))

    @pl.when(at_end)
    def _():
        for m in far:
            for cc in range(2):
                wait_cross(m, cc)
                cross_shares(m, cc)

    for m in near:
        pair_shares(m)
    for cp in x_last + [y_last] + fwd_a + fwd_b:
        cp.wait_recv()

    @pl.when(at_end)
    def _():
        for cc in range(2):
            for m in far:
                predict_cross(m, cc)
        for cc in range(2):
            far_levels(cc)

    predict_pair(high)
    for b in range(top):
        for m in of_level(b, near):
            predict_pair(m)
        send_level(b, of_level(b, near))
    @pl.when(at_end)
    def _():
        predict_pair(0)

    @pl.when(inside)
    def _():
        for m in far:
            wait_cross(m, 0)

        @pl.when(c == 1)
        def _():
            send_logits(far, (1, 0))

        for m in far:
            cross_shares(m, 0)
            predict_cross(m, 0)
        far_levels(0)
        predict_pair(0)

        @pl.when(c == 0)
        def _():
            sum_level(top, high, False)

        for m in far:
            wait_cross(m, 1)

        @pl.when(c == 0)
        def _():
            rs[top, 0].start()

        for m in far:
            cross_shares(m, 1)
            predict_cross(m, 1)

        far_levels(1)

    @pl.when(at_end | (c == 1))
    def _():
        sum_level(top, high)

    mem_rows = jnp.concatenate(
        [info[m, e, 1:1 + SLIDES, :] for m in range(Z) for e in range(2)], axis=1)
    mem16 = jnp.concatenate([mem_rows, jnp.zeros((16 - SLIDES, A * S), F32)], axis=0).astype(BF16)
    part = lax.dot_general(mem16, slow[...], (((1,), (1,)), ((), ())), preferred_element_type=F32)
    col_tally = jnp.sum(mem_rows, axis=1, keepdims=True)
    gmeas = mstat[me]
    for m, e in groups:
        mst[m, e].wait_recv()
        gmeas = gmeas + mstat_in[m, e]
    packed = [gmeas[s:s + 1] for s in range(SLIDES)] + [jnp.zeros((1, NC - SLIDES * GA), F32)]
    mass_out[...] = jnp.concatenate(
        [part[:SLIDES], jnp.broadcast_to(col_tally, (SLIDES, NC)),
         jnp.concatenate(packed, axis=1), jnp.zeros((1, NC), F32)], axis=0)
    mcp = []
    for i, (dx, dy) in enumerate(planes):
        cp = remote(mass_out, mass_in.at[i], ms_s.at[i], ms_r.at[i], plane(dx, dy))
        cp.start()
        mcp.append(cp)
    pending.extend(mcp)
    for cp in mcp:
        cp.wait_recv()
    msum = mass_out[...]
    for i in range(Q - 1):
        msum = msum + mass_in[i]
    mass = msum[:SLIDES]
    gmeas = jnp.concatenate(
        [msum[6:7, s * GA:(s + 1) * GA] for s in range(SLIDES)], axis=0)
    inv_gmeas = lax.rsqrt(gmeas + FLOOR)
    tally = jnp.maximum(msum[SLIDES:2 * SLIDES, 0:1], 1.0)
    quota = mass / tally
    prior_sum = jnp.sum(jnp.sum(cell_prior[...], axis=0, keepdims=True), axis=1, keepdims=True)
    prior = jnp.concatenate(
        [cell_prior[pl.ds(((z * X + bx) * 2 + c) * (YR // k.PL) + i, 1), :]
         for bx in range(X) for i in range(YR // k.PL)], axis=1) / prior_sum
    kl = jnp.sum(prior * (jnp.log(prior) - jnp.log(quota)), axis=1, keepdims=True)
    rat = prior / quota
    rat_hi = rat.astype(BF16)
    rat_lo = (rat - rat_hi.astype(F32)).astype(BF16)
    ratio_hl[...] = jnp.concatenate(
        [rat_hi, rat_lo, jnp.zeros((16 - 2 * SLIDES, NC), BF16)], axis=0)
    dd = jnp.dot(ratio_hl[...], slow[...], preferred_element_type=F32)
    dd = dd[:SLIDES] + dd[SLIDES:2 * SLIDES]
    dsum = jnp.sum(dd * mem_rows, axis=0, keepdims=True)
    mext[...] = jnp.concatenate(
        [mem_rows, mem_rows, jnp.zeros((16 - 2 * SLIDES, A * S), F32)], axis=0).astype(BF16)
    dcp = {}
    for m in range(Z):
        for e in range(2):
            lane = (m * 2 + e) * S
            dpart[m, e] = jnp.broadcast_to(dsum[:, lane:lane + S], (8, S))
    for m, e in groups:
        cp = remote(dpart.at[m, e], din.at[m, e], d_s.at[m, e], d_r.at[m, e], group(m, e))
        cp.start()
        dcp[m, e] = cp
        pending.append(cp)

    pred_sq = jnp.zeros((S, 1), F32)
    pred_meas = jnp.zeros((S, 1), F32)
    lane_id = lax.broadcasted_iota(jnp.int32, (1, GA), 1)
    for j in range(A):
        lanes = slice(j * GA, (j + 1) * GA)
        if j % per_part == 0:
            total = piece_sum(0, k.LV, j // per_part)
        p = total(lanes)
        pacc[0, :, lanes] = p
        q = meas[:, lanes].astype(F32)
        pq, pp = p * q, p * p
        pred_sq = pred_sq + jnp.sum(pp, axis=1, keepdims=True)
        pred_meas = pred_meas + jnp.sum(pq, axis=1, keepdims=True)
        for s in range(SLIDES):
            stat[j, s:s + 1, :] = jnp.sum(mcol[s] * pq, axis=0, keepdims=True)
            stat[j, 3 + s:4 + s, :] = jnp.sum(mcol[s] * pp, axis=0, keepdims=True)
    inv_pred = lax.rsqrt(pred_sq + FLOOR)
    spot_cos = pred_meas * inv_pred * inv_meas
    spot_sum = jnp.sum(wcol * spot_cos, axis=0, keepdims=True)
    scal = jnp.where(lane_id == 0, spot_sum, 0.0)
    for s in range(SLIDES):
        scal = scal + jnp.where(lane_id == 1 + s, kl[s:s + 1] * (1.0 / Q), 0.0)
    for j in range(A):
        stat[j, 6:8, :] = jnp.concatenate([scal, jnp.zeros((1, GA), F32)], axis=0)

    cps = {}
    for m, e in groups:
        cp = remote(stat.at[flip(z, m) * 2 + flip(c, e)], s1.at[m, e],
                    s1_s.at[m, e], s1_r.at[m, e], group(m, e))
        cp.start()
        cps[m, e] = cp
        pending.append(cp)
    u = stat[me]
    for m, e in groups:
        cps[m, e].wait_recv()
        u = u + s1[m, e]
    ubuf[...] = u
    cps = []
    for i, (dx, dy) in enumerate(planes):
        cp = remote(ubuf, s2.at[i], s2_s.at[i], s2_r.at[i], plane(dx, dy))
        cp.start()
        cps.append(cp)
        pending.append(cp)
    for i, cp in enumerate(cps):
        cp.wait_recv()
        u = u + s2[i]
    share = tally * (1.0 / G)
    a = lax.rsqrt(u[3:6] + FLOOR)
    b = inv_gmeas
    gcos = u[0:3] * a * b
    wall[me] = jnp.concatenate(
        [share * a * b, share * gcos * a * a,
         jnp.sum(share * gcos, axis=0, keepdims=True), u[6:7]], axis=0)
    cps = []
    for m, e in groups:
        cp = remote(wall.at[me], wall.at[me], s3_s.at[m, e], s3_r.at[m, e], group(m, e))
        cp.start()
        cps.append(cp)
        pending.append(cp)
    for (m, e) in groups:
        other = flip(z, m) * 2 + flip(c, e)
        remote(wall.at[other], wall.at[other], s3_s.at[m, e], s3_r.at[m, e], group(m, e)).wait_recv()

    lead = -(wcol * inv_pred * inv_meas)
    back = wcol * spot_cos * inv_pred * inv_pred
    dot1 = jnp.zeros((S, 1), F32)
    gene_total = jnp.zeros((1, GA), F32)
    for j in range(A):
        lanes = slice(j * GA, (j + 1) * GA)
        w = wall[j]
        direct = mcol[0] * w[0:1] + mcol[1] * w[1:2] + mcol[2] * w[2:3]
        damp = mcol[0] * w[3:4] + mcol[1] * w[4:5] + mcol[2] * w[5:6]
        gene_total = gene_total + w[6:7]
        p = pacc[0, :, lanes]
        g = (lead - direct) * meas[:, lanes].astype(F32) + (back + damp) * p
        glow = g.astype(BF16)
        gp[0, 0, :, lanes] = glow
        dot1 = dot1 + jnp.sum(glow.astype(F32) * p, axis=1, keepdims=True)

    gz, gc = {}, {}

    def to_core(m):
        cp = remote(gp.at[m, 0], gp.at[m, 1], gc_s.at[m], gc_r.at[m], group(0, 1))
        cp.start()
        gc[m] = cp
        pending.append(cp)

    def to_plane(m, b):
        t = m ^ (1 << b)
        cp = remote(gp.at[m, 0], gp.at[t, 0], gz_s.at[t], gz_r.at[t], group(1 << b, 0))
        cp.start()
        gz[t] = cp
        pending.append(cp)

    to_core(0)
    gz[high] = remote(gp.at[0, 0], gp.at[high, 0], gz_s.at[high], gz_r.at[high], group(high, 0))

    for b in range(top):
        t = 1 << b
        gz[t] = remote(gp.at[0, 0], gp.at[t, 0], gz_s.at[t], gz_r.at[t], group(t, 0))

    def near_start():
        for b in reversed(range(top)):
            gz[1 << b].start()

    @pl.when(c == 0)
    def _():
        gz[high].start()

    @pl.when(c == 1)
    def _():
        near_start()

    for m, e in groups:
        dcp[m, e].wait_recv()
    dtot = dpart[0, 0]
    for m, e in groups:
        dtot = dtot + din[m, e]
    dot_row = jnp.broadcast_to(dot1, (S, S)).T[0:8] - dtot
    info2[0, 0] = dot_row
    i2 = {}
    for m, e in groups:
        cp = remote(info2.at[0, 0], info2.at[m, e], i2_s.at[m, e], i2_r.at[m, e], group(m, e))
        cp.start()
        i2[m, e] = cp
        pending.append(cp)

    fin = wall[0]
    total_tally = jnp.sum(tally, axis=0, keepdims=True)
    gsum = jnp.sum(gene_total, axis=1, keepdims=True)
    dens = jnp.zeros((1, 1), F32)
    for s in range(SLIDES):
        dens = dens + tally[s:s + 1] * fin[7:8, 1 + s:2 + s]
    lid = lax.broadcasted_iota(jnp.int32, (8, 128), 1)
    out_loss[...] = (jnp.where(lid == 0, fin[7:8, 0:1], 0.0) + jnp.where(lid == 1, gsum, 0.0)
                     + jnp.where(lid == 2, dens, 0.0)) / total_tally

    ycp = {}

    def map_rows(m, es, gpm):
        n = len(es)

        def step(i, _):
            r0 = pl.multiple_of(i * RC, RC)
            low = lax.dot_general(cells[pl.ds(r0, RC), :], gpm(),
                                  (((1,), (1,)), ((), ())), preferred_element_type=F32)
            mx = [mext[:, pl.ds(pl.multiple_of((m * 2 + e) * S, S), S)] for e in es]
            rt = lax.dot_general(ratio_hl[:, pl.ds(r0, RC)], jnp.concatenate(mx, axis=1),
                                 (((0,), (0,)), ((), ())), preferred_element_type=F32)
            low = low - rt
            per = YR // RC
            for i_e, e in enumerate(es):
                sh = shares_of(m, e, i) * float(k.CELLS)
                v = sh * (low[:, i_e * S:(i_e + 1) * S] - info2[m, e, 0:1, :])
                ybuf[(m * 2 + e) * X + i // per,
                     pl.ds(pl.multiple_of(lax.rem(i, per) * RC, RC), RC), :] = v.astype(BF16)
            return 0

        lax.fori_loop(0, NC // RC, step, 0)

    def map_copies(m, es):
        cps = []
        for e in es:
            src = ybuf.at[pl.ds((m * 2 + e) * X, X)]
            if m == 0 and type(e) is int and e == 0:
                cps.append(pltpu.make_async_copy(src, out_map.at[z, :, c], loc_sem.at[3]))
                ycp[0, 0] = cps[-1]
            else:
                cps.append(remote(src, out_map.at[z, :, c], y_s.at[m, e], y_r.at[m, e],
                                  group(m, e)))
                pending.append(cps[-1])
        return cps

    def send_map(m, es):
        for cp in map_copies(m, es):
            cp.start()

    def map_piece(m):
        for e in range(2):
            if (m, e) != (0, 0):
                i2[m, e].wait_recv()
        map_rows(m, [0, 1], lambda: gp[m].reshape(2 * S, G))
        send_map(m, [0, 1])

    gc[0].wait_recv()
    map_piece(0)

    def pass_on(m, b):
        for b2 in reversed(range(b)):
            to_plane(m, b2)
        to_core(m)

    gc[high] = remote(gp.at[high, 0], gp.at[high, 1], gc_s.at[high], gc_r.at[high], group(0, 1))
    pending.append(gc[high])
    for b2 in range(top):
        t = high ^ (1 << b2)
        gz[t] = remote(gp.at[high, 0], gp.at[t, 0], gz_s.at[t], gz_r.at[t], group(1 << b2, 0))
        pending.append(gz[t])

    def high_on():
        gz[high].wait_recv()
        gc[high].start()
        for b2 in reversed(range(top)):
            gz[high ^ (1 << b2)].start()

    @pl.when(c == 0)
    def _():
        gz[high].wait_send()
        pl.semaphore_signal(gate, inc=1, device_id=group(0, 1), device_id_type=MESH_ID)
        near_start()
        high_on()

    @pl.when(c == 1)
    def _():
        pl.semaphore_wait(gate, 1)
        gz[high].start()
        gc[high].wait_recv()

    i2[high, 0].wait_recv()
    i2[high, 1].wait_recv()
    map_rows(high, [c], lambda: gp[high, c])

    @pl.when(c == 1)
    def _():
        high_on()

    @pl.when(c == 0)
    def _():
        gc[high].wait_recv()

    own_core = map_copies(high, [c])

    @pl.when(at_end)
    def _():
        own_core[0].start()

    map_rows(high, [1 - c], lambda: gp[high, 1 - c])

    @pl.when(inside)
    def _():
        own_core[0].start()

    send_map(high, [1 - c])
    for b in reversed(range(top)):
        for m in range(1 << b, Z, 2 << b):
            gz[m].wait_recv()
            pass_on(m, b)
    def slot_of(dx, dy, half):
        return ((dx * Y + dy) - 1) * 2 + half

    def single_rows(dx, dy, half):
        bx = lax.rem(x + dx, X)
        by = flip(y, dy)
        return pl.multiple_of(((bx * Y + by) * 2 + half) * H, H)

    def single_part(dx, dy, half, put, m0=0, m1=Z):
        r0 = single_rows(dx, dy, half)
        n = (m1 - m0) * 2 * S

        def step(i, _):
            lanes = pl.ds(pl.multiple_of(i * NN, NN), NN)
            v = jnp.dot(slow[pl.ds(r0, H), m0 * 2 * S:m1 * 2 * S],
                        gp[pl.ds(m0, m1 - m0), :, :, lanes].reshape(n, NN), preferred_element_type=F32)
            put(lanes, v)
            return 0

        lax.fori_loop(0, G // NN, step, 0)

    def put_send(slot, extra=()):
        def put(lanes, v):
            for i in extra:
                v = v + grecv[i, :, lanes].astype(F32)
            gsend[slot, :, lanes] = v.astype(BF16)
        return put

    def put_own(half):
        def put(lanes, v):
            own_single[half * H:(half + 1) * H, lanes] = v
        return put

    def put_rest(sl, half):
        def put(lanes, v):
            v = v + own_single[half * H:(half + 1) * H, lanes]
            gsend[sl, :, lanes] = v.astype(BF16)
        return put

    r_m1 = lambda d: d
    r_m2 = lambda d: XN + d
    r_m3 = lambda d: 2 * XN + d
    r_m5 = lambda d: 3 * XN + d
    r_m4, r_m6 = 4 * XN, 4 * XN + 1
    gcp = {}

    def send_single(slot, r_slot, where):
        cp = remote(gsend.at[slot], grecv.at[r_slot], gs_s.at[r_slot], gs_r.at[r_slot], where)
        cp.start()
        gcp[r_slot] = cp
        pending.append(cp)

    for m in range(1, Z - 1):
        if m != high:
            gc[m].wait_recv()
    for half in range(2):
        single_part(1, 1, half, put_own(half), 0, Z - 1)
    if Z > 2:
        gc[Z - 1].wait_recv()
    for d in range(XN):
        for half in range(2):
            sl = slot_of(d + 1, 1, half)
            if d == 0:
                single_part(1, 1, half, put_rest(sl, half), Z - 1, Z)
            else:
                single_part(d + 1, 1, half, put_send(sl))
            if half == 0:
                send_single(sl, r_m1(d), plane(d + 1, 0))
            else:
                send_single(sl, r_m2(d), plane(0, 1))
    for m in far:
        map_piece(m)
    for d in range(XN):
        s0 = slot_of(d + 1, 0, 0)
        single_part(d + 1, 0, 0, put_send(s0))
        send_single(s0, r_m3(d), plane(d + 1, 0))
    s0 = slot_of(0, 1, 1)
    single_part(0, 1, 1, put_send(s0))
    send_single(s0, r_m4, plane(0, 1))

    for m in near:
        map_piece(m)

    for d in range(XN):
        gcp[r_m2(d)].wait_recv()
        s0 = slot_of(d + 1, 0, 1)
        single_part(d + 1, 0, 1, put_send(s0, [r_m2(d)]))
        send_single(s0, r_m5(d), plane(d + 1, 0))
    for d in range(XN):
        gcp[r_m1(d)].wait_recv()
    s0 = slot_of(0, 1, 0)
    single_part(0, 1, 0, put_send(s0, [r_m1(d) for d in range(XN)]))
    send_single(s0, r_m6, plane(0, 1))

    for half in range(2):
        single_part(0, 0, half, put_own(half))
    cp_single = []
    halves = [[r_m3(d) for d in range(XN)] + [r_m6], [r_m5(d) for d in range(XN)] + [r_m4]]
    for half in range(2):
        for i in halves[half]:
            gcp[i].wait_recv()

        def step(i, _):
            lanes = pl.ds(pl.multiple_of(i * NN, NN), NN)
            v = own_single[half * H:(half + 1) * H, lanes]
            for i2_ in halves[half]:
                v = v + grecv[i2_, :, lanes].astype(F32)
            own_single[half * H:(half + 1) * H, lanes] = v * float(k.CELLS) ** 0.5
            return 0

        lax.fori_loop(0, G // NN, step, 0)
        rows_h = pl.ds(half * H, H)
        cp_single.append(pltpu.make_async_copy(
            own_single.at[rows_h], out_single.at[rows_h], loc_sem.at[4 + half]))
        cp_single[half].start()

    for m, e in groups:
        other = (flip(z, m), slice(None), flip(c, e))
        remote(ybuf.at[pl.ds(0, X)], out_map.at[other[0], :, other[2]], y_s.at[m, e], y_r.at[m, e],
               group(m, e)).wait_recv()
    ycp[0, 0].wait()
    for cp in cp_single:
        cp.wait()
    for cp in pending:
        cp.wait_send()
    for b in range(top):
        gz[1 << b].wait_send()

    @pl.when(c == 1)
    def _():
        gz[high].wait_send()

    @pl.when(at_end)
    def _():
        sent([high])

    @pl.when(inside)
    def _():
        sent(far)


def forward_and_back(k, logits, single_cell, spatial, ids, mask, cell_prior, order):
    Z, X, Y, A, Q, S, G, R, H = k.Z, k.X, k.Y, k.A, k.Q, k.S, k.G, k.R, k.H
    YR, NC, GA, XN = k.YR, k.NC, k.GA, k.X - 1
    vm = pl.BlockSpec(memory_space=pltpu.VMEM)
    hbm = pl.BlockSpec(memory_space=pl.ANY)
    dma = lambda *s: pltpu.SemaphoreType.DMA(s)
    ncl, ngs = 4 * XN + 2, 4 * XN + 2
    scratch = [
        pltpu.VMEM((Z, 2, X, YR, S), BF16),
        pltpu.VMEM((NC, G), BF16),
        pltpu.VMEM((NC, A * S), BF16),
        pltpu.VMEM((A * S, NC), BF16),
        pltpu.VMEM((A * X, YR, S), BF16),
        pltpu.VMEM((Z, 2, 8, S), F32),
        pltpu.VMEM((Z, 2, 8, S), F32),
        pltpu.VMEM((Z, S, G), F32),
        pltpu.VMEM((Z, S, G), BF16),
        pltpu.VMEM((Z, S, G), BF16),
        pltpu.VMEM((Z - 1, S, G), BF16),
        pltpu.VMEM((S, G), BF16),
        pltpu.VMEM((Z, 2, S, G), BF16),
        pltpu.VMEM((2 * (Q - 1), H, G), BF16),
        pltpu.VMEM((ngs, H, G), BF16),
        pltpu.VMEM((8, NC), F32),
        pltpu.VMEM((Q - 1, 8, NC), F32),
        pltpu.VMEM((16, NC), BF16),
        pltpu.VMEM((16, A * S), BF16),
        pltpu.VMEM((Z, 2, 8, S), F32),
        pltpu.VMEM((Z, 2, 8, S), F32),
        pltpu.VMEM((A, 8, GA), F32),
        pltpu.VMEM((Z, 2, 8, GA), F32),
        pltpu.VMEM((A, 8, GA), F32),
        pltpu.VMEM((Z, 2, 8, GA), F32),
        pltpu.VMEM((8, GA), F32),
        pltpu.VMEM((Q - 1, 8, GA), F32),
        pltpu.VMEM((A, 8, GA), F32),
        pltpu.VMEM((R, G), F32),
        dma(6),
        dma(Z, 2), dma(Z, 2),
        dma(ncl), dma(ncl),
        dma(Z, 2), dma(Z, 2),
        dma(Z, HALVES), dma(Z, HALVES),
        dma(Z - 1, HALVES), dma(Z - 1, HALVES),
        dma(Q - 1), dma(Q - 1),
        dma(Z, 2), dma(Z, 2),
        dma(Z, 2), dma(Z, 2),
        dma(Q - 1), dma(Q - 1),
        dma(Z, 2), dma(Z, 2),
        dma(Z), dma(Z),
        dma(Z), dma(Z),
        dma(Z, 2), dma(Z, 2),
        dma(Z, 2), dma(Z, 2),
        dma(ngs), dma(ngs),
        dma(Z, 2), dma(Z, 2),
        pltpu.SemaphoreType.REGULAR,
    ]
    return pl.pallas_call(
        functools.partial(kernel, k),
        name="mapping",
        out_shape=[
            jax.ShapeDtypeStruct((Z, X, 2, YR, S), BF16),
            jax.ShapeDtypeStruct((R, G), F32),
            jax.ShapeDtypeStruct((8, 128), F32),
        ],
        in_specs=[hbm, hbm, hbm, vm, vm, vm, vm, vm],
        out_specs=[hbm, hbm, vm],
        scratch_shapes=scratch,
        compiler_params=pltpu.CompilerParams(
            collective_id=0, has_side_effects=True, vmem_limit_bytes=64000 * 1024),
        cost_estimate=pl.CostEstimate(
            flops=6 * NC * A * S * G, bytes_accessed=32 << 20, transcendentals=2 * NC * A * S),
    )(logits.reshape(Z, X, 2, YR, S), logits.reshape(A * X, YR, S), single_cell, spatial,
      ids.reshape(1, S), mask.reshape(1, S), cell_prior.reshape(-1, k.PL), order.reshape(1, k.NB))


def body(mesh, map_logits, single_cell, spatial, slide_ids, spot_mask, cell_prior, gene_order):
    cells, spots = map_logits.shape
    k = Sizes(mesh, cells, spatial.shape[1], spots, gene_order.shape[0])
    gmap, gsingle, loss = forward_and_back(
        k, map_logits, single_cell, spatial, slide_ids, spot_mask, cell_prior, gene_order)
    grad_map = gmap.reshape(cells, spots).astype(F32)
    return loss[0, :3], grad_map, gsingle


def solution(mesh):
    k = Sizes(mesh, 1 << 20, 1 << 20, 128, 1)
    fine = Mesh(mesh.devices.reshape(k.Z, k.X, 2, k.Y), AXES)
    in_specs = (P(None, AXES), P(AXES, None), P(AXES, None), P(AXES), P(AXES), P(), P())
    out_specs = (P(), P(None, AXES), P(AXES, None))
    return jax.shard_map(functools.partial(body, mesh), mesh=fine, in_specs=in_specs,
                         out_specs=out_specs, check_vma=False)
```

```python
import functools

import jax
import jax.numpy as jnp
from jax import lax
from jax.experimental import pallas as pl
from jax.experimental.pallas import tpu as pltpu
from jax.sharding import Mesh, PartitionSpec as P

SLIDES = 3
HALVES = 2
FLOOR = 1e-06
F32 = jnp.float32
BF16 = jnp.bfloat16
AXES = ("z", "x", "c", "y")
MESH_ID = pl.DeviceIdType.MESH


def flip(value, mask):
    bit = 1
    while bit <= mask:
        if mask & bit:
            value = value + (1 - 2 * ((value // bit) % 2)) * bit
        bit *= 2
    return value


class Sizes:
    def __init__(self, mesh, cells, genes, spots, blocks):
        n = mesh.shape["spot"] // 2
        zs = 1
        while zs * zs * 4 <= 2 * n:
            zs *= 2
        self.Z, self.X, self.Y = zs, n // zs, mesh.shape["grp"]
        assert self.Y == 2 and self.Z * self.X == n and self.Z >= 2
        self.LV = self.Z.bit_length() - 1
        self.A = 2 * self.Z
        self.Q = self.X * self.Y
        self.CELLS, self.G, self.S, self.NB = cells, genes, spots, blocks
        self.R = cells // (self.A * self.Q)
        self.H = self.R // 2
        self.YR = self.Y * self.R
        self.NC = self.X * self.YR
        self.GA = genes // self.A
        self.RC = min(256, self.YR)
        self.PL = min(128, self.YR)
        self.PLANE = 2 * self.Q == self.A
        self.NN = min(512, genes)


def kernel(k, logits, logits_flat, own_cells, spatial, ids, mask, cell_prior, order,
           out_map, out_single, out_loss,
           lbuf, cells, slow, slow_t, ybuf, info, info2,
           pacc, p1, psib, rs_in, meas,
           gp, gsend, grecv,
           mass_out, mass_in, ratio_hl, mext, dpart, din,
           mstat, mstat_in, gm_out, gm_in, stat, s1, ubuf, s2, wall, own_single,
           loc_sem, lg_s, lg_r, cl_s, cl_r, in_s, in_r, ps_s, ps_r, rs_s, rs_r, ms_s, ms_r,
           d_s, d_r, s1_s, s1_r, s2_s, s2_r, s3_s, s3_r, gz_s, gz_r, gc_s, gc_r, i2_s, i2_r,
           y_s, y_r, gs_s, gs_r, mt_s, mt_r, gate, gm_s, gm_r):
    Z, X, Y, A, Q, S, G, R, H = k.Z, k.X, k.Y, k.A, k.Q, k.S, k.G, k.R, k.H
    YR, NC, GA, RC, NN = k.YR, k.NC, k.GA, k.RC, k.NN
    z, x, c, y = [lax.axis_index(a) for a in AXES]
    yo = 1 - y

    def group(m, e):
        return (flip(z, m), x, c + e - 2 * c * e, y)

    def plane(dx, dy):
        return (z, lax.rem(x + dx, X), c, flip(y, dy))

    def remote(src, dst, send, recv, where):
        return pltpu.make_async_remote_copy(
            src_ref=src, dst_ref=dst, send_sem=send, recv_sem=recv,
            device_id=where, device_id_type=MESH_ID)

    groups = [(m, e) for m in reversed(range(Z)) for e in (1, 0) if (m, e) != (0, 0)]
    planes = [(dx, dy) for dx in reversed(range(X)) for dy in (1, 0) if (dx, dy) != (0, 0)]
    me = z * 2 + c

    def part_of(dx, dy, e):
        return (lax.rem(x + dx, X) * Y + flip(y, dy)) * 2 + c + e - 2 * c * e

    if k.PLANE:
        mine = part_of(0, 0, 0)
        sharers = [(dx * Y + dy, e, part_of(dx, dy, e),
                    (z, lax.rem(x + dx, X), c + e - 2 * c * e, flip(y, dy)))
                   for dx in reversed(range(X)) for dy in (1, 0) for e in (1, 0)
                   if (dx, dy, e) != (0, 0, 0)]
        others = [(m - 1, group(m, 0)) for m in reversed(range(1, Z))]
    else:
        mine = me
        sharers = [(m, e, flip(z, m) * 2 + flip(c, e), group(m, e)) for m, e in groups]
        others = [(i, plane(dx, dy)) for i, (dx, dy) in enumerate(planes)]

    def tree_sum(first, parts):
        v = [first] + list(parts)
        while len(v) > 1:
            v = [v[i] + v[i + 1] if i + 1 < len(v) else v[i] for i in range(0, len(v), 2)]
        return v[0]

    pending = []

    cp_flat = pltpu.make_async_copy(logits_flat, ybuf, loc_sem.at[0])
    cp_flat.start()
    cp_own = pltpu.make_async_copy(logits.at[z, :, c], lbuf.at[0, 0], loc_sem.at[1])
    cp_own.start()
    cp_cells = pltpu.make_async_copy(
        own_cells, cells.at[pl.ds(pl.multiple_of((x * Y + y) * R, R), R)], loc_sem.at[2])
    cp_cells.start()
    barrier = pltpu.get_barrier_semaphore()
    for m, e in groups:
        pl.semaphore_signal(barrier, inc=1, device_id=group(m, e), device_id_type=MESH_ID)
    for dx, dy in planes:
        pl.semaphore_signal(barrier, inc=1, device_id=plane(dx, dy), device_id_type=MESH_ID)
    greeted = len(groups) + len(planes)
    if k.PLANE:
        for dx, dy in planes:
            pl.semaphore_signal(barrier, inc=1, device_id=(*plane(dx, dy)[:2], 1 - c, flip(y, dy)),
                                device_id_type=MESH_ID)
        greeted += len(planes)
    pl.semaphore_wait(barrier, greeted)

    def rows(bx, by, half):
        return cells.at[pl.ds(pl.multiple_of(((bx * Y + by) * 2 + half) * H, H), H)]

    XN = X - 1

    def cell_copy(slot, src, bx, by, half, where):
        return remote(src, rows(bx, by, half), cl_s.at[slot], cl_r.at[slot], where)

    own_half = [own_cells.at[pl.ds(0, H)], own_cells.at[pl.ds(H, H)]]
    x_first = [cell_copy(d, own_half[0], x, y, 0, plane(d + 1, 0)) for d in range(XN)]
    x_last = [cell_copy(XN + d, own_half[1], x, y, 1, plane(d + 1, 0)) for d in range(XN)]
    y_first = cell_copy(2 * XN, own_half[1], x, y, 1, plane(0, 1))
    y_last = cell_copy(2 * XN + 1, own_half[0], x, y, 0, plane(0, 1))
    for cp in x_first + [y_first]:
        cp.start()

    high = Z // 2
    far = [m for m in range(Z) if m & high and m != high]
    near = [m for m in range(1, Z) if not m & high]
    lg = {(m, e): remote(logits.at[flip(z, m), :, flip(c, e)], lbuf.at[m, e],
                         lg_s.at[m, e], lg_r.at[m, e], group(m, e)) for m, e in groups}

    pending.extend(cp for (m, e), cp in lg.items() if m in [0] + near)

    def sent(ms):
        for m in ms:
            for e in range(2):
                lg[m, e].wait_send()

    def send_logits(ms, es=(0, 1)):
        for m in ms:
            for e in es:
                lg[m, e].start()

    at_end = (z == 0) | (z == Z - 1)
    inside = jnp.logical_not(at_end)
    lg[0, 1].start()

    @pl.when(at_end)
    def _():
        send_logits(near + far)

    @pl.when(inside)
    def _():
        send_logits([high])

    for cp in x_last + [y_last]:
        cp.start()
    pending.extend(x_first + x_last + [y_first, y_last])

    cp_flat.wait()

    def add_exp(i, acc):
        e = jnp.exp(ybuf[i].astype(F32))
        return acc + jnp.sum(e.reshape(YR // 8, 8, S), axis=0)

    acc = lax.fori_loop(0, A * X, add_exp, jnp.zeros((8, S), F32))
    inv_sum = 1.0 / jnp.sum(acc, axis=0, keepdims=True)
    idr = ids[...]
    maskf = mask[...].astype(F32)
    mrow = [jnp.where(idr == s, maskf, 0.0) for s in range(SLIDES)]
    info[0, 0] = jnp.concatenate([inv_sum] + mrow + [jnp.zeros((8 - 1 - SLIDES, S), F32)], axis=0)
    inf = {}
    for m, e in groups:
        inf[m, e] = remote(info.at[0, 0], info.at[m, e], in_s.at[m, e], in_r.at[m, e], group(m, e))
        inf[m, e].start()
        pending.append(inf[m, e])

    W = G // k.NB
    for b in range(k.NB):
        v = jnp.zeros((S, W), F32)
        for j in range(k.NB):
            here = (order[0:1, j:j + 1] == b).astype(F32)
            v = v + here * spatial[:, j * W:(j + 1) * W].astype(F32)
        meas[:, b * W:(b + 1) * W] = v.astype(BF16)
    mcols = jnp.concatenate(mrow + [maskf] + [jnp.zeros((8 - 1 - SLIDES, S), F32)], axis=0).T
    mcol = [mcols[:, s:s + 1] for s in range(SLIDES)]
    wcol = mcols[:, SLIDES:SLIDES + 1]
    meas_sq = jnp.zeros((S, 1), F32)
    for j in range(A):
        v = meas[:, j * GA:(j + 1) * GA].astype(F32)
        v = v * v
        meas_sq = meas_sq + jnp.sum(v, axis=1, keepdims=True)
        for s in range(SLIDES):
            mstat[j, s:s + 1, :] = jnp.sum(mcol[s] * v, axis=0, keepdims=True)
        mstat[j, SLIDES:8, :] = jnp.zeros((8 - SLIDES, GA), F32)
    inv_meas = lax.rsqrt(meas_sq + FLOOR)
    mst = {}
    for i, e, part, where in sharers:
        mst[i, e] = remote(mstat.at[part], mstat_in.at[i, e], mt_s.at[i, e], mt_r.at[i, e], where)
        mst[i, e].start()
    pending.extend(mst.values())

    fwd_a, fwd_b = [], []
    for d in range(XN):
        bx = lax.rem(x - (d + 1) + X, X)
        cell_copy(d, own_half[0], bx, y, 0, plane(d + 1, 0)).wait_recv()
        cp = cell_copy(2 * XN + 2 + d, rows(bx, y, 0), bx, y, 0, plane(0, 1))
        cp.start()
        fwd_a.append(cp)
    y_first.wait_recv()
    for d in range(XN):
        cp = cell_copy(3 * XN + 2 + d, rows(x, yo, 1), x, yo, 1, plane(d + 1, 0))
        cp.start()
        fwd_b.append(cp)
    pending.extend(fwd_a + fwd_b)

    cp_own.wait()
    cp_cells.wait()

    def shares_of(m, e, i):
        per = YR // RC
        l = lbuf[m, e, i // per, pl.ds(pl.multiple_of(lax.rem(i, per) * RC, RC), RC), :]
        return jnp.exp(l.astype(F32)) * info[m, e, 0:1, :]

    def t_row(m, i):
        return (m * 2 + i) * S

    def slot(cc):
        return c if cc == 0 else 1 - c

    def wait_cross(m, cc):
        e = slot(cc)
        remote(info.at[0, 0], info.at[m, e], in_s.at[m, e], in_r.at[m, e],
               group(m, e)).wait_recv()
        remote(lbuf.at[0, 0], lbuf.at[m, e], lg_s.at[m, e], lg_r.at[m, e],
               group(m, e)).wait_recv()

    def wait_pair(m):
        for e in range(2):
            if (m, e) != (0, 0):
                inf[m, e].wait_recv()
                lg[m, e].wait_recv()

    def make_shares(m, e, row):
        lane = (m * 2 + e) * S
        if type(e) is not int:
            lane = pl.multiple_of(lane, S)

        def step(i, _):
            sh = shares_of(m, e, i).astype(BF16)
            r0 = pl.multiple_of(i * RC, RC)
            slow[pl.ds(r0, RC), pl.ds(lane, S)] = sh
            slow_t[row:row + S, pl.ds(r0, RC)] = sh.T
            return 0

        lax.fori_loop(0, NC // RC, step, 0)

    def pair_shares(m):
        wait_pair(m)
        for e in range(2):
            make_shares(m, e, t_row(m, e))

    def cross_shares(m, cc):
        make_shares(m, slot(cc), t_row(m, cc))

    gene_part = [pl.ds(h * (G // HALVES), G // HALVES) for h in range(HALVES)]

    class Parts:
        def __init__(self, make):
            self.cps = [make(h) for h in range(HALVES)]

        def start(self):
            for cp in self.cps:
                cp.start()

        def wait_send(self):
            for cp in self.cps:
                cp.wait_send()

    def sibling_part(m):
        return Parts(lambda h: remote(
            p1.at[m, :, gene_part[h]], psib.at[m, :, gene_part[h]], ps_s.at[m, h], ps_r.at[m, h],
            group(0, 1)))

    ps = [sibling_part(m) for m in range(Z)]
    pending.extend(ps)

    def gene_loop(put, h=0, parts=1):
        n = G // NN // parts

        def step(i, _):
            put(pl.ds(pl.multiple_of(i * NN, NN), NN))
            return 0

        lax.fori_loop(h * n, (h + 1) * n, step, 0)

    def predict_pair(m):
        row = t_row(m, 0)

        def put(lanes):
            r = jnp.dot(slow_t[row:row + 2 * S, :], cells[:, lanes], preferred_element_type=F32)
            pacc[m, :, lanes] = r[:S]
            p1[m, :, lanes] = r[S:].astype(BF16)

        gene_loop(put)
        ps[m].start()

    def predict_cross(m, cc):
        row = t_row(m, cc)

        def part(lanes):
            return jnp.dot(slow_t[row:row + S, :], cells[:, lanes], preferred_element_type=F32)

        @pl.when(c == cc)
        def _():
            def put(lanes):
                pacc[m, :, lanes] = part(lanes)

            gene_loop(put)

        @pl.when(c != cc)
        def _():
            def put(lanes):
                p1[m, :, lanes] = part(lanes).astype(BF16)

            for h in range(HALVES):
                gene_loop(put, h, HALVES)
                ps[m].cps[h].start()

    def level_slot(b, m):
        return sum(Z >> (j + 1) for j in range(b)) + (m >> (b + 1))

    def level_part(b, m):
        sl, step_m = level_slot(b, m), 1 << b
        return Parts(lambda h: remote(
            psib.at[m ^ step_m, :, gene_part[h]], rs_in.at[sl, :, gene_part[h]],
            rs_s.at[sl, h], rs_r.at[sl, h], group(step_m, 0)))

    rs = {(b, m): level_part(b, m) for b in range(k.LV) for m in range(0, Z, 2 << b)}
    pending.extend(rs.values())

    def piece_sum(m, b, h):
        ps[m].cps[h].wait_recv()
        for j in range(b):
            rs[j, m].cps[h].wait_recv()

        def total(lanes):
            t = pacc[m, :, lanes] + psib[m, :, lanes].astype(F32)
            for j in range(b):
                t = t + rs_in[level_slot(j, m), :, lanes].astype(F32)
            return t
        return total

    per_part = A // HALVES

    def sum_level(b, m, send=True):
        for h in range(HALVES):
            total = piece_sum(m, b, h)
            for j in range(h * per_part, (h + 1) * per_part):
                lanes = slice(j * GA, (j + 1) * GA)
                psib[m, :, lanes] = total(lanes).astype(BF16)
            if send:
                rs[b, m ^ (1 << b)].cps[h].start()

    def far_levels(cc):
        @pl.when(c == cc)
        def _():
            for b in range(top):
                send_level(b, of_level(b, far))

    def send_level(b, ms):
        for m in ms:
            sum_level(b, m)

    top = k.LV - 1
    def of_level(b, ms):
        return [m for m in reversed(ms) if m % (2 << b) == 1 << b]

    pair_shares(0)

    @pl.when(at_end)
    def _():
        sent(far)
        send_logits([high])

    @pl.when(inside)
    def _():
        sent([high])
        send_logits(near)

    pair_shares(high)

    @pl.when(inside & (c == 0))
    def _():
        send_logits(far, (1, 0))

    @pl.when(at_end)
    def _():
        for m in far:
            for cc in range(2):
                wait_cross(m, cc)
                cross_shares(m, cc)

    for m in near:
        pair_shares(m)
    for cp in x_last + [y_last] + fwd_a + fwd_b:
        cp.wait_recv()

    @pl.when(at_end)
    def _():
        for cc in range(2):
            for m in far:
                predict_cross(m, cc)
        for cc in range(2):
            far_levels(cc)

    predict_pair(high)
    for b in range(top):
        for m in of_level(b, near):
            predict_pair(m)
        send_level(b, of_level(b, near))
    @pl.when(at_end)
    def _():
        predict_pair(0)

    @pl.when(inside)
    def _():
        for m in far:
            wait_cross(m, 0)

        @pl.when(c == 1)
        def _():
            send_logits(far, (1, 0))

        for m in far:
            cross_shares(m, 0)
            predict_cross(m, 0)
        far_levels(0)
        predict_pair(0)

        @pl.when(c == 0)
        def _():
            sum_level(top, high, False)

        for m in far:
            wait_cross(m, 1)

        @pl.when(c == 0)
        def _():
            rs[top, 0].start()

        for m in far:
            cross_shares(m, 1)
            predict_cross(m, 1)

        far_levels(1)

    @pl.when(at_end | (c == 1))
    def _():
        sum_level(top, high)

    mem_rows = jnp.concatenate(
        [info[m, e, 1:1 + SLIDES, :] for m in range(Z) for e in range(2)], axis=1)
    mem16 = jnp.concatenate([mem_rows, jnp.zeros((16 - SLIDES, A * S), F32)], axis=0).astype(BF16)
    part_mass = lax.dot_general(mem16, slow[...], (((1,), (1,)), ((), ())), preferred_element_type=F32)
    col_tally = jnp.sum(mem_rows, axis=1, keepdims=True)
    gmeas = mstat[mine]
    for i, e, part, where in sharers:
        mst[i, e].wait_recv()
        gmeas = gmeas + mstat_in[i, e]
    packed = [gmeas[s:s + 1] for s in range(SLIDES)] + [jnp.zeros((1, NC - SLIDES * GA), F32)]
    mass_out[...] = jnp.concatenate(
        [part_mass[:SLIDES], jnp.broadcast_to(col_tally, (SLIDES, NC)),
         jnp.concatenate(packed, axis=1), jnp.zeros((1, NC), F32)], axis=0)
    gmc = []
    if k.PLANE:
        gm_out[...] = gmeas
        for i, where in others:
            gmc.append(remote(gm_out, gm_in.at[i], gm_s.at[i], gm_r.at[i], where))
            gmc[-1].start()
        pending.extend(gmc)
    mcp = []
    for i, (dx, dy) in enumerate(planes):
        cp = remote(mass_out, mass_in.at[i], ms_s.at[i], ms_r.at[i], plane(dx, dy))
        cp.start()
        mcp.append(cp)
    pending.extend(mcp)
    for cp in mcp:
        cp.wait_recv()
    msum = mass_out[...]
    for i in range(Q - 1):
        msum = msum + mass_in[i]
    mass = msum[:SLIDES]
    gmeas = jnp.concatenate(
        [msum[6:7, s * GA:(s + 1) * GA] for s in range(SLIDES)], axis=0)
    inv_gmeas = lax.rsqrt(gmeas + FLOOR)
    tally = jnp.maximum(msum[SLIDES:2 * SLIDES, 0:1], 1.0)
    quota = mass / tally
    prior_sum = jnp.sum(jnp.sum(cell_prior[...], axis=0, keepdims=True), axis=1, keepdims=True)
    prior = jnp.concatenate(
        [cell_prior[pl.ds(((z * X + bx) * 2 + c) * (YR // k.PL) + i, 1), :]
         for bx in range(X) for i in range(YR // k.PL)], axis=1) / prior_sum
    kl = jnp.sum(prior * (jnp.log(prior) - jnp.log(quota)), axis=1, keepdims=True)
    rat = prior / quota
    rat_hi = rat.astype(BF16)
    rat_lo = (rat - rat_hi.astype(F32)).astype(BF16)
    ratio_hl[...] = jnp.concatenate(
        [rat_hi, rat_lo, jnp.zeros((16 - 2 * SLIDES, NC), BF16)], axis=0)
    dd = jnp.dot(ratio_hl[...], slow[...], preferred_element_type=F32)
    dd = dd[:SLIDES] + dd[SLIDES:2 * SLIDES]
    dsum = jnp.sum(dd * mem_rows, axis=0, keepdims=True)
    mext[...] = jnp.concatenate(
        [mem_rows, mem_rows, jnp.zeros((16 - 2 * SLIDES, A * S), F32)], axis=0).astype(BF16)
    dcp = {}
    for m in range(Z):
        for e in range(2):
            lane = (m * 2 + e) * S
            dpart[m, e] = jnp.broadcast_to(dsum[:, lane:lane + S], (8, S))
    for m, e in groups:
        cp = remote(dpart.at[m, e], din.at[m, e], d_s.at[m, e], d_r.at[m, e], group(m, e))
        cp.start()
        dcp[m, e] = cp
        pending.append(cp)

    pred_sq = jnp.zeros((S, 1), F32)
    pred_meas = jnp.zeros((S, 1), F32)
    lane_id = lax.broadcasted_iota(jnp.int32, (1, GA), 1)
    for j in range(A):
        lanes = slice(j * GA, (j + 1) * GA)
        if j % per_part == 0:
            total = piece_sum(0, k.LV, j // per_part)
        p = total(lanes)
        pacc[0, :, lanes] = p
        q = meas[:, lanes].astype(F32)
        pq, pp = p * q, p * p
        pred_sq = pred_sq + jnp.sum(pp, axis=1, keepdims=True)
        pred_meas = pred_meas + jnp.sum(pq, axis=1, keepdims=True)
        for s in range(SLIDES):
            stat[j, s:s + 1, :] = jnp.sum(mcol[s] * pq, axis=0, keepdims=True)
            stat[j, 3 + s:4 + s, :] = jnp.sum(mcol[s] * pp, axis=0, keepdims=True)
    inv_pred = lax.rsqrt(pred_sq + FLOOR)
    spot_cos = pred_meas * inv_pred * inv_meas
    spot_sum = jnp.sum(wcol * spot_cos, axis=0, keepdims=True)
    scal = jnp.where(lane_id == 0, spot_sum, 0.0)
    for s in range(SLIDES):
        scal = scal + jnp.where(lane_id == 1 + s, kl[s:s + 1] * (1.0 / Q), 0.0)
    for j in range(A):
        stat[j, 6:8, :] = jnp.concatenate([scal, jnp.zeros((1, GA), F32)], axis=0)

    cps = []
    for i, e, part, where in sharers:
        cp = remote(stat.at[part], s1.at[i, e], s1_s.at[i, e], s1_r.at[i, e], where)
        cp.start()
        cps.append(cp)
    pending.extend(cps)
    u = stat[mine]
    for (i, e, part, where), cp in zip(sharers, cps):
        cp.wait_recv()
        u = u + s1[i, e]
    ubuf[...] = u
    cps = []
    for i, where in others:
        cp = remote(ubuf, s2.at[i], s2_s.at[i], s2_r.at[i], where)
        cp.start()
        cps.append(cp)
    pending.extend(cps)
    for cp in cps + gmc:
        cp.wait_recv()
    u = tree_sum(u, [s2[i] for i in range(len(others))])
    if k.PLANE:
        gmeas = tree_sum(gm_out[...], [gm_in[i] for i in range(len(others))])[:SLIDES]
        inv_gmeas = lax.rsqrt(gmeas + FLOOR)
    share = tally * (1.0 / G)
    a = lax.rsqrt(u[3:6] + FLOOR)
    b = inv_gmeas
    gcos = u[0:3] * a * b
    wall[mine] = jnp.concatenate(
        [share * a * b, share * gcos * a * a,
         jnp.sum(share * gcos, axis=0, keepdims=True), u[6:7]], axis=0)
    cps = []
    for i, e, part, where in sharers:
        cp = remote(wall.at[mine], wall.at[mine], s3_s.at[i, e], s3_r.at[i, e], where)
        cp.start()
        cps.append(cp)
    pending.extend(cps)
    for i, e, part, where in sharers:
        remote(wall.at[part], wall.at[part], s3_s.at[i, e], s3_r.at[i, e], where).wait_recv()

    lead = -(wcol * inv_pred * inv_meas)
    back = wcol * spot_cos * inv_pred * inv_pred
    dot1 = jnp.zeros((S, 1), F32)
    gene_total = jnp.zeros((1, GA), F32)
    for j in range(A):
        lanes = slice(j * GA, (j + 1) * GA)
        w = wall[j]
        direct = mcol[0] * w[0:1] + mcol[1] * w[1:2] + mcol[2] * w[2:3]
        damp = mcol[0] * w[3:4] + mcol[1] * w[4:5] + mcol[2] * w[5:6]
        gene_total = gene_total + w[6:7]
        p = pacc[0, :, lanes]
        g = (lead - direct) * meas[:, lanes].astype(F32) + (back + damp) * p
        glow = g.astype(BF16)
        gp[0, 0, :, lanes] = glow
        dot1 = dot1 + jnp.sum(glow.astype(F32) * p, axis=1, keepdims=True)

    gz, gc = {}, {}

    def to_core(m):
        cp = remote(gp.at[m, 0], gp.at[m, 1], gc_s.at[m], gc_r.at[m], group(0, 1))
        cp.start()
        gc[m] = cp
        pending.append(cp)

    def to_plane(m, b):
        t = m ^ (1 << b)
        cp = remote(gp.at[m, 0], gp.at[t, 0], gz_s.at[t], gz_r.at[t], group(1 << b, 0))
        cp.start()
        gz[t] = cp
        pending.append(cp)

    to_core(0)
    gz[high] = remote(gp.at[0, 0], gp.at[high, 0], gz_s.at[high], gz_r.at[high], group(high, 0))

    for b in range(top):
        t = 1 << b
        gz[t] = remote(gp.at[0, 0], gp.at[t, 0], gz_s.at[t], gz_r.at[t], group(t, 0))

    def near_start():
        for b in reversed(range(top)):
            gz[1 << b].start()

    @pl.when(c == 0)
    def _():
        gz[high].start()

    @pl.when(c == 1)
    def _():
        near_start()

    for m, e in groups:
        dcp[m, e].wait_recv()
    dtot = dpart[0, 0]
    for m, e in groups:
        dtot = dtot + din[m, e]
    dot_row = jnp.broadcast_to(dot1, (S, S)).T[0:8] - dtot
    info2[0, 0] = dot_row
    i2 = {}
    for m, e in groups:
        cp = remote(info2.at[0, 0], info2.at[m, e], i2_s.at[m, e], i2_r.at[m, e], group(m, e))
        cp.start()
        i2[m, e] = cp
        pending.append(cp)

    fin = wall[0]
    total_tally = jnp.sum(tally, axis=0, keepdims=True)
    gsum = jnp.sum(gene_total, axis=1, keepdims=True)
    dens = jnp.zeros((1, 1), F32)
    for s in range(SLIDES):
        dens = dens + tally[s:s + 1] * fin[7:8, 1 + s:2 + s]
    lid = lax.broadcasted_iota(jnp.int32, (8, 128), 1)
    out_loss[...] = (jnp.where(lid == 0, fin[7:8, 0:1], 0.0) + jnp.where(lid == 1, gsum, 0.0)
                     + jnp.where(lid == 2, dens, 0.0)) / total_tally

    ycp = {}

    def map_rows(m, es, gpm):
        n = len(es)

        def step(i, _):
            r0 = pl.multiple_of(i * RC, RC)
            low = lax.dot_general(cells[pl.ds(r0, RC), :], gpm(),
                                  (((1,), (1,)), ((), ())), preferred_element_type=F32)
            mx = [mext[:, pl.ds(pl.multiple_of((m * 2 + e) * S, S), S)] for e in es]
            rt = lax.dot_general(ratio_hl[:, pl.ds(r0, RC)], jnp.concatenate(mx, axis=1),
                                 (((0,), (0,)), ((), ())), preferred_element_type=F32)
            low = low - rt
            per = YR // RC
            for i_e, e in enumerate(es):
                sh = shares_of(m, e, i) * float(k.CELLS)
                v = sh * (low[:, i_e * S:(i_e + 1) * S] - info2[m, e, 0:1, :])
                ybuf[(m * 2 + e) * X + i // per,
                     pl.ds(pl.multiple_of(lax.rem(i, per) * RC, RC), RC), :] = v.astype(BF16)
            return 0

        lax.fori_loop(0, NC // RC, step, 0)

    def map_copies(m, es):
        cps = []
        for e in es:
            src = ybuf.at[pl.ds((m * 2 + e) * X, X)]
            if m == 0 and type(e) is int and e == 0:
                cps.append(pltpu.make_async_copy(src, out_map.at[z, :, c], loc_sem.at[3]))
                ycp[0, 0] = cps[-1]
            else:
                cps.append(remote(src, out_map.at[z, :, c], y_s.at[m, e], y_r.at[m, e],
                                  group(m, e)))
                pending.append(cps[-1])
        return cps

    def send_map(m, es):
        for cp in map_copies(m, es):
            cp.start()

    def map_piece(m):
        for e in range(2):
            if (m, e) != (0, 0):
                i2[m, e].wait_recv()
        map_rows(m, [0, 1], lambda: gp[m].reshape(2 * S, G))
        send_map(m, [0, 1])

    gc[0].wait_recv()
    map_piece(0)

    def pass_on(m, b):
        for b2 in reversed(range(b)):
            to_plane(m, b2)
        to_core(m)

    gc[high] = remote(gp.at[high, 0], gp.at[high, 1], gc_s.at[high], gc_r.at[high], group(0, 1))
    pending.append(gc[high])
    for b2 in range(top):
        t = high ^ (1 << b2)
        gz[t] = remote(gp.at[high, 0], gp.at[t, 0], gz_s.at[t], gz_r.at[t], group(1 << b2, 0))
        pending.append(gz[t])

    def high_on():
        gz[high].wait_recv()
        gc[high].start()
        for b2 in reversed(range(top)):
            gz[high ^ (1 << b2)].start()

    @pl.when(c == 0)
    def _():
        gz[high].wait_send()
        pl.semaphore_signal(gate, inc=1, device_id=group(0, 1), device_id_type=MESH_ID)
        near_start()
        high_on()

    @pl.when(c == 1)
    def _():
        pl.semaphore_wait(gate, 1)
        gz[high].start()
        gc[high].wait_recv()

    i2[high, 0].wait_recv()
    i2[high, 1].wait_recv()
    map_rows(high, [c], lambda: gp[high, c])

    @pl.when(c == 1)
    def _():
        high_on()

    @pl.when(c == 0)
    def _():
        gc[high].wait_recv()

    own_core = map_copies(high, [c])

    @pl.when(at_end)
    def _():
        own_core[0].start()

    map_rows(high, [1 - c], lambda: gp[high, 1 - c])

    @pl.when(inside)
    def _():
        own_core[0].start()

    send_map(high, [1 - c])
    for b in reversed(range(top)):
        for m in range(1 << b, Z, 2 << b):
            gz[m].wait_recv()
            pass_on(m, b)
    def slot_of(dx, dy, half):
        return ((dx * Y + dy) - 1) * 2 + half

    def single_rows(dx, dy, half):
        bx = lax.rem(x + dx, X)
        by = flip(y, dy)
        return pl.multiple_of(((bx * Y + by) * 2 + half) * H, H)

    def single_part(dx, dy, half, put, m0=0, m1=Z):
        r0 = single_rows(dx, dy, half)
        n = (m1 - m0) * 2 * S

        def step(i, _):
            lanes = pl.ds(pl.multiple_of(i * NN, NN), NN)
            v = jnp.dot(slow[pl.ds(r0, H), m0 * 2 * S:m1 * 2 * S],
                        gp[pl.ds(m0, m1 - m0), :, :, lanes].reshape(n, NN), preferred_element_type=F32)
            put(lanes, v)
            return 0

        lax.fori_loop(0, G // NN, step, 0)

    def put_send(slot, extra=()):
        def put(lanes, v):
            for i in extra:
                v = v + grecv[i, :, lanes].astype(F32)
            gsend[slot, :, lanes] = v.astype(BF16)
        return put

    def put_own(half):
        def put(lanes, v):
            own_single[half * H:(half + 1) * H, lanes] = v
        return put

    def put_rest(sl, half):
        def put(lanes, v):
            v = v + own_single[half * H:(half + 1) * H, lanes]
            gsend[sl, :, lanes] = v.astype(BF16)
        return put

    r_m1 = lambda d: d
    r_m2 = lambda d: XN + d
    r_m3 = lambda d: 2 * XN + d
    r_m5 = lambda d: 3 * XN + d
    r_m4, r_m6 = 4 * XN, 4 * XN + 1
    gcp = {}

    def send_single(slot, r_slot, where):
        cp = remote(gsend.at[slot], grecv.at[r_slot], gs_s.at[r_slot], gs_r.at[r_slot], where)
        cp.start()
        gcp[r_slot] = cp
        pending.append(cp)

    for m in range(1, Z - 1):
        if m != high:
            gc[m].wait_recv()
    for half in range(2):
        single_part(1, 1, half, put_own(half), 0, Z - 1)
    if Z > 2:
        gc[Z - 1].wait_recv()
    for d in range(XN):
        for half in range(2):
            sl = slot_of(d + 1, 1, half)
            if d == 0:
                single_part(1, 1, half, put_rest(sl, half), Z - 1, Z)
            else:
                single_part(d + 1, 1, half, put_send(sl))
            if half == 0:
                send_single(sl, r_m1(d), plane(d + 1, 0))
            else:
                send_single(sl, r_m2(d), plane(0, 1))
    for m in far:
        map_piece(m)
    for d in range(XN):
        s0 = slot_of(d + 1, 0, 0)
        single_part(d + 1, 0, 0, put_send(s0))
        send_single(s0, r_m3(d), plane(d + 1, 0))
    s0 = slot_of(0, 1, 1)
    single_part(0, 1, 1, put_send(s0))
    send_single(s0, r_m4, plane(0, 1))

    for m in near:
        map_piece(m)

    for d in range(XN):
        gcp[r_m2(d)].wait_recv()
        s0 = slot_of(d + 1, 0, 1)
        single_part(d + 1, 0, 1, put_send(s0, [r_m2(d)]))
        send_single(s0, r_m5(d), plane(d + 1, 0))
    for d in range(XN):
        gcp[r_m1(d)].wait_recv()
    s0 = slot_of(0, 1, 0)
    single_part(0, 1, 0, put_send(s0, [r_m1(d) for d in range(XN)]))
    send_single(s0, r_m6, plane(0, 1))

    for half in range(2):
        single_part(0, 0, half, put_own(half))
    cp_single = []
    halves = [[r_m3(d) for d in range(XN)] + [r_m6], [r_m5(d) for d in range(XN)] + [r_m4]]
    for half in range(2):
        for i in halves[half]:
            gcp[i].wait_recv()

        def step(i, _):
            lanes = pl.ds(pl.multiple_of(i * NN, NN), NN)
            v = own_single[half * H:(half + 1) * H, lanes]
            for i2_ in halves[half]:
                v = v + grecv[i2_, :, lanes].astype(F32)
            own_single[half * H:(half + 1) * H, lanes] = v * float(k.CELLS) ** 0.5
            return 0

        lax.fori_loop(0, G // NN, step, 0)
        rows_h = pl.ds(half * H, H)
        cp_single.append(pltpu.make_async_copy(
            own_single.at[rows_h], out_single.at[rows_h], loc_sem.at[4 + half]))
        cp_single[half].start()

    for m, e in groups:
        other = (flip(z, m), slice(None), flip(c, e))
        remote(ybuf.at[pl.ds(0, X)], out_map.at[other[0], :, other[2]], y_s.at[m, e], y_r.at[m, e],
               group(m, e)).wait_recv()
    ycp[0, 0].wait()
    for cp in cp_single:
        cp.wait()
    for cp in pending:
        cp.wait_send()
    for b in range(top):
        gz[1 << b].wait_send()

    @pl.when(c == 1)
    def _():
        gz[high].wait_send()

    @pl.when(at_end)
    def _():
        sent([high])

    @pl.when(inside)
    def _():
        sent(far)


def forward_and_back(k, logits, single_cell, spatial, ids, mask, cell_prior, order):
    Z, X, Y, A, Q, S, G, R, H = k.Z, k.X, k.Y, k.A, k.Q, k.S, k.G, k.R, k.H
    YR, NC, GA, XN = k.YR, k.NC, k.GA, k.X - 1
    vm = pl.BlockSpec(memory_space=pltpu.VMEM)
    hbm = pl.BlockSpec(memory_space=pl.ANY)
    dma = lambda *s: pltpu.SemaphoreType.DMA(s)
    ncl, ngs = 4 * XN + 2, 4 * XN + 2
    scratch = [
        pltpu.VMEM((Z, 2, X, YR, S), BF16),
        pltpu.VMEM((NC, G), BF16),
        pltpu.VMEM((NC, A * S), BF16),
        pltpu.VMEM((A * S, NC), BF16),
        pltpu.VMEM((A * X, YR, S), BF16),
        pltpu.VMEM((Z, 2, 8, S), F32),
        pltpu.VMEM((Z, 2, 8, S), F32),
        pltpu.VMEM((Z, S, G), F32),
        pltpu.VMEM((Z, S, G), BF16),
        pltpu.VMEM((Z, S, G), BF16),
        pltpu.VMEM((Z - 1, S, G), BF16),
        pltpu.VMEM((S, G), BF16),
        pltpu.VMEM((Z, 2, S, G), BF16),
        pltpu.VMEM((2 * (Q - 1), H, G), BF16),
        pltpu.VMEM((ngs, H, G), BF16),
        pltpu.VMEM((8, NC), F32),
        pltpu.VMEM((Q - 1, 8, NC), F32),
        pltpu.VMEM((16, NC), BF16),
        pltpu.VMEM((16, A * S), BF16),
        pltpu.VMEM((Z, 2, 8, S), F32),
        pltpu.VMEM((Z, 2, 8, S), F32),
        pltpu.VMEM((A, 8, GA), F32),
        pltpu.VMEM((Z, 2, 8, GA), F32),
        pltpu.VMEM((8, GA), F32),
        pltpu.VMEM((Q - 1, 8, GA), F32),
        pltpu.VMEM((A, 8, GA), F32),
        pltpu.VMEM((Z, 2, 8, GA), F32),
        pltpu.VMEM((8, GA), F32),
        pltpu.VMEM((Q - 1, 8, GA), F32),
        pltpu.VMEM((A, 8, GA), F32),
        pltpu.VMEM((R, G), F32),
        dma(6),
        dma(Z, 2), dma(Z, 2),
        dma(ncl), dma(ncl),
        dma(Z, 2), dma(Z, 2),
        dma(Z, HALVES), dma(Z, HALVES),
        dma(Z - 1, HALVES), dma(Z - 1, HALVES),
        dma(Q - 1), dma(Q - 1),
        dma(Z, 2), dma(Z, 2),
        dma(Z, 2), dma(Z, 2),
        dma(Q - 1), dma(Q - 1),
        dma(Z, 2), dma(Z, 2),
        dma(Z), dma(Z),
        dma(Z), dma(Z),
        dma(Z, 2), dma(Z, 2),
        dma(Z, 2), dma(Z, 2),
        dma(ngs), dma(ngs),
        dma(Z, 2), dma(Z, 2),
        pltpu.SemaphoreType.REGULAR,
        dma(Q - 1), dma(Q - 1),
    ]
    return pl.pallas_call(
        functools.partial(kernel, k),
        name="mapping",
        out_shape=[
            jax.ShapeDtypeStruct((Z, X, 2, YR, S), BF16),
            jax.ShapeDtypeStruct((R, G), F32),
            jax.ShapeDtypeStruct((8, 128), F32),
        ],
        in_specs=[hbm, hbm, hbm, vm, vm, vm, vm, vm],
        out_specs=[hbm, hbm, vm],
        scratch_shapes=scratch,
        compiler_params=pltpu.CompilerParams(
            collective_id=0, has_side_effects=True, vmem_limit_bytes=64000 * 1024),
        cost_estimate=pl.CostEstimate(
            flops=6 * NC * A * S * G, bytes_accessed=32 << 20, transcendentals=2 * NC * A * S),
    )(logits.reshape(Z, X, 2, YR, S), logits.reshape(A * X, YR, S), single_cell, spatial,
      ids.reshape(1, S), mask.reshape(1, S), cell_prior.reshape(-1, k.PL), order.reshape(1, k.NB))


def body(mesh, map_logits, single_cell, spatial, slide_ids, spot_mask, cell_prior, gene_order):
    cells, spots = map_logits.shape
    k = Sizes(mesh, cells, spatial.shape[1], spots, gene_order.shape[0])
    gmap, gsingle, loss = forward_and_back(
        k, map_logits, single_cell, spatial, slide_ids, spot_mask, cell_prior, gene_order)
    grad_map = gmap.reshape(cells, spots).astype(F32)
    return loss[0, :3], grad_map, gsingle


def solution(mesh):
    k = Sizes(mesh, 1 << 20, 1 << 20, 128, 1)
    fine = Mesh(mesh.devices.reshape(k.Z, k.X, 2, k.Y), AXES)
    in_specs = (P(None, AXES), P(AXES, None), P(AXES, None), P(AXES), P(AXES), P(), P())
    out_specs = (P(), P(None, AXES), P(AXES, None))
    return jax.shard_map(functools.partial(body, mesh), mesh=fine, in_specs=in_specs,
                         out_specs=out_specs, check_vma=False)
```

```python
import functools

import jax
import jax.numpy as jnp
from jax import lax
from jax.experimental import pallas as pl
from jax.experimental.pallas import tpu as pltpu
from jax.sharding import Mesh, PartitionSpec as P

SLIDES = 3
HALVES = 2
FLOOR = 1e-06
F32 = jnp.float32
BF16 = jnp.bfloat16
AXES = ("z", "x", "c", "y")
MESH_ID = pl.DeviceIdType.MESH


def flip(value, mask):
    bit = 1
    while bit <= mask:
        if mask & bit:
            value = value + (1 - 2 * ((value // bit) % 2)) * bit
        bit *= 2
    return value


class Sizes:
    def __init__(self, mesh, cells, genes, spots, blocks):
        n = mesh.shape["spot"] // 2
        zs = 1
        while zs * zs * 4 <= 2 * n:
            zs *= 2
        self.Z, self.X, self.Y = zs, n // zs, mesh.shape["grp"]
        assert self.Y == 2 and self.Z * self.X == n and self.Z >= 2
        self.LV = self.Z.bit_length() - 1
        self.A = 2 * self.Z
        self.Q = self.X * self.Y
        self.CELLS, self.G, self.S, self.NB = cells, genes, spots, blocks
        self.R = cells // (self.A * self.Q)
        self.H = self.R // 2
        self.YR = self.Y * self.R
        self.NC = self.X * self.YR
        self.GA = genes // self.A
        self.RC = min(256, self.YR)
        self.PL = min(128, self.YR)
        self.PLANE = 2 * self.Q == self.A
        self.NN = min(512, genes)


def kernel(k, logits, logits_flat, own_cells, spatial, ids, mask, cell_prior, order,
           out_map, out_single, out_loss,
           lbuf, cells, slow, slow_t, ybuf, info, info2,
           pacc, p1, psib, rs_in, meas,
           gp, gsend, grecv,
           mass_out, mass_in, ratio_hl, mext, dpart, din,
           mstat, mstat_in, gm_out, gm_in, stat, s1, ubuf, s2, wall, own_single,
           loc_sem, lg_s, lg_r, cl_s, cl_r, in_s, in_r, ps_s, ps_r, rs_s, rs_r, ms_s, ms_r,
           d_s, d_r, s1_s, s1_r, s2_s, s2_r, s3_s, s3_r, gz_s, gz_r, gc_s, gc_r, i2_s, i2_r,
           y_s, y_r, gs_s, gs_r, mt_s, mt_r, gate, gm_s, gm_r):
    Z, X, Y, A, Q, S, G, R, H = k.Z, k.X, k.Y, k.A, k.Q, k.S, k.G, k.R, k.H
    YR, NC, GA, RC, NN = k.YR, k.NC, k.GA, k.RC, k.NN
    z, x, c, y = [lax.axis_index(a) for a in AXES]
    yo = 1 - y

    def group(m, e):
        return (flip(z, m), x, c + e - 2 * c * e, y)

    def plane(dx, dy):
        return (z, lax.rem(x + dx, X), c, flip(y, dy))

    def remote(src, dst, send, recv, where):
        return pltpu.make_async_remote_copy(
            src_ref=src, dst_ref=dst, send_sem=send, recv_sem=recv,
            device_id=where, device_id_type=MESH_ID)

    groups = [(m, e) for m in reversed(range(Z)) for e in (1, 0) if (m, e) != (0, 0)]
    planes = [(dx, dy) for dx in reversed(range(X)) for dy in (1, 0) if (dx, dy) != (0, 0)]
    me = z * 2 + c

    def part_of(dx, dy, e):
        return (lax.rem(x + dx, X) * Y + flip(y, dy)) * 2 + c + e - 2 * c * e

    if k.PLANE:
        mine = part_of(0, 0, 0)
        sharers = [(dx * Y + dy, e, part_of(dx, dy, e),
                    (z, lax.rem(x + dx, X), c + e - 2 * c * e, flip(y, dy)))
                   for dx in reversed(range(X)) for dy in (1, 0) for e in (1, 0)
                   if (dx, dy, e) != (0, 0, 0)]
        others = [(m - 1, group(m, 0)) for m in reversed(range(1, Z))]
    else:
        mine = me
        sharers = [(m, e, flip(z, m) * 2 + flip(c, e), group(m, e)) for m, e in groups]
        others = [(i, plane(dx, dy)) for i, (dx, dy) in enumerate(planes)]

    def tree_sum(first, parts):
        v = [first] + list(parts)
        while len(v) > 1:
            v = [v[i] + v[i + 1] if i + 1 < len(v) else v[i] for i in range(0, len(v), 2)]
        return v[0]

    pending = []

    cp_flat = pltpu.make_async_copy(logits_flat, ybuf, loc_sem.at[0])
    cp_flat.start()
    cp_own = pltpu.make_async_copy(logits.at[z, :, c], lbuf.at[0, 0], loc_sem.at[1])
    cp_own.start()
    cp_cells = pltpu.make_async_copy(
        own_cells, cells.at[pl.ds(pl.multiple_of((x * Y + y) * R, R), R)], loc_sem.at[2])
    cp_cells.start()
    barrier = pltpu.get_barrier_semaphore()
    for m, e in groups:
        pl.semaphore_signal(barrier, inc=1, device_id=group(m, e), device_id_type=MESH_ID)
    for dx, dy in planes:
        pl.semaphore_signal(barrier, inc=1, device_id=plane(dx, dy), device_id_type=MESH_ID)
    greeted = len(groups) + len(planes)
    if k.PLANE:
        for dx, dy in planes:
            pl.semaphore_signal(barrier, inc=1, device_id=(*plane(dx, dy)[:2], 1 - c, flip(y, dy)),
                                device_id_type=MESH_ID)
        greeted += len(planes)
    pl.semaphore_wait(barrier, greeted)

    def rows(bx, by, half):
        return cells.at[pl.ds(pl.multiple_of(((bx * Y + by) * 2 + half) * H, H), H)]

    XN = X - 1

    def cell_copy(slot, src, bx, by, half, where):
        return remote(src, rows(bx, by, half), cl_s.at[slot], cl_r.at[slot], where)

    own_half = [own_cells.at[pl.ds(0, H)], own_cells.at[pl.ds(H, H)]]
    x_first = [cell_copy(d, own_half[0], x, y, 0, plane(d + 1, 0)) for d in range(XN)]
    x_last = [cell_copy(XN + d, own_half[1], x, y, 1, plane(d + 1, 0)) for d in range(XN)]
    y_first = cell_copy(2 * XN, own_half[1], x, y, 1, plane(0, 1))
    y_last = cell_copy(2 * XN + 1, own_half[0], x, y, 0, plane(0, 1))
    for cp in x_first + [y_first]:
        cp.start()

    high = Z // 2
    far = [m for m in range(Z) if m & high and m != high]
    near = [m for m in range(1, Z) if not m & high]
    lg = {(m, e): remote(logits.at[flip(z, m), :, flip(c, e)], lbuf.at[m, e],
                         lg_s.at[m, e], lg_r.at[m, e], group(m, e)) for m, e in groups}

    pending.extend(cp for (m, e), cp in lg.items() if m in [0] + near)

    def sent(ms):
        for m in ms:
            for e in range(2):
                lg[m, e].wait_send()

    def send_logits(ms, es=(0, 1)):
        for m in ms:
            for e in es:
                lg[m, e].start()

    at_end = (z == 0) | (z == Z - 1)
    inside = jnp.logical_not(at_end)
    lg[0, 1].start()

    @pl.when(at_end)
    def _():
        send_logits(near + far)

    @pl.when(inside)
    def _():
        send_logits([high])

    for cp in x_last + [y_last]:
        cp.start()
    pending.extend(x_first + x_last + [y_first, y_last])

    cp_flat.wait()

    def add_exp(i, acc):
        e = jnp.exp(ybuf[i].astype(F32))
        return acc + jnp.sum(e.reshape(YR // 8, 8, S), axis=0)

    acc = lax.fori_loop(0, A * X, add_exp, jnp.zeros((8, S), F32))
    inv_sum = 1.0 / jnp.sum(acc, axis=0, keepdims=True)
    idr = ids[...]
    maskf = mask[...].astype(F32)
    mrow = [jnp.where(idr == s, maskf, 0.0) for s in range(SLIDES)]
    info[0, 0] = jnp.concatenate([inv_sum] + mrow + [jnp.zeros((8 - 1 - SLIDES, S), F32)], axis=0)
    inf = {}
    for m, e in groups:
        inf[m, e] = remote(info.at[0, 0], info.at[m, e], in_s.at[m, e], in_r.at[m, e], group(m, e))
        inf[m, e].start()
        pending.append(inf[m, e])

    W = G // k.NB
    for b in range(k.NB):
        v = jnp.zeros((S, W), F32)
        for j in range(k.NB):
            here = (order[0:1, j:j + 1] == b).astype(F32)
            v = v + here * spatial[:, j * W:(j + 1) * W].astype(F32)
        meas[:, b * W:(b + 1) * W] = v.astype(BF16)
    mcols = jnp.concatenate(mrow + [maskf] + [jnp.zeros((8 - 1 - SLIDES, S), F32)], axis=0).T
    mcol = [mcols[:, s:s + 1] for s in range(SLIDES)]
    wcol = mcols[:, SLIDES:SLIDES + 1]
    meas_sq = jnp.zeros((S, 1), F32)
    for j in range(A):
        v = meas[:, j * GA:(j + 1) * GA].astype(F32)
        v = v * v
        meas_sq = meas_sq + jnp.sum(v, axis=1, keepdims=True)
        for s in range(SLIDES):
            mstat[j, s:s + 1, :] = jnp.sum(mcol[s] * v, axis=0, keepdims=True)
        mstat[j, SLIDES:8, :] = jnp.zeros((8 - SLIDES, GA), F32)
    inv_meas = lax.rsqrt(meas_sq + FLOOR)
    mst = {}
    for i, e, part, where in sharers:
        mst[i, e] = remote(mstat.at[part], mstat_in.at[i, e], mt_s.at[i, e], mt_r.at[i, e], where)
        mst[i, e].start()
    pending.extend(mst.values())

    fwd_a, fwd_b = [], []
    for d in range(XN):
        bx = lax.rem(x - (d + 1) + X, X)
        cell_copy(d, own_half[0], bx, y, 0, plane(d + 1, 0)).wait_recv()
        cp = cell_copy(2 * XN + 2 + d, rows(bx, y, 0), bx, y, 0, plane(0, 1))
        cp.start()
        fwd_a.append(cp)
    y_first.wait_recv()
    for d in range(XN):
        cp = cell_copy(3 * XN + 2 + d, rows(x, yo, 1), x, yo, 1, plane(d + 1, 0))
        cp.start()
        fwd_b.append(cp)
    pending.extend(fwd_a + fwd_b)

    cp_own.wait()
    cp_cells.wait()

    def shares_of(m, e, i):
        per = YR // RC
        l = lbuf[m, e, i // per, pl.ds(pl.multiple_of(lax.rem(i, per) * RC, RC), RC), :]
        return jnp.exp(l.astype(F32)) * info[m, e, 0:1, :]

    def t_row(m, i):
        return (m * 2 + i) * S

    def slot(cc):
        return c if cc == 0 else 1 - c

    def wait_cross(m, cc):
        e = slot(cc)
        remote(info.at[0, 0], info.at[m, e], in_s.at[m, e], in_r.at[m, e],
               group(m, e)).wait_recv()
        remote(lbuf.at[0, 0], lbuf.at[m, e], lg_s.at[m, e], lg_r.at[m, e],
               group(m, e)).wait_recv()

    def wait_pair(m):
        for e in range(2):
            if (m, e) != (0, 0):
                inf[m, e].wait_recv()
                lg[m, e].wait_recv()

    def make_shares(m, e, row):
        lane = (m * 2 + e) * S
        if type(e) is not int:
            lane = pl.multiple_of(lane, S)

        def step(i, _):
            sh = shares_of(m, e, i).astype(BF16)
            r0 = pl.multiple_of(i * RC, RC)
            slow[pl.ds(r0, RC), pl.ds(lane, S)] = sh
            slow_t[row:row + S, pl.ds(r0, RC)] = sh.T
            return 0

        lax.fori_loop(0, NC // RC, step, 0)

    def pair_shares(m):
        wait_pair(m)
        for e in range(2):
            make_shares(m, e, t_row(m, e))

    def cross_shares(m, cc):
        make_shares(m, slot(cc), t_row(m, cc))

    gene_part = [pl.ds(h * (G // HALVES), G // HALVES) for h in range(HALVES)]

    class Parts:
        def __init__(self, make):
            self.cps = [make(h) for h in range(HALVES)]

        def start(self):
            for cp in self.cps:
                cp.start()

        def wait_send(self):
            for cp in self.cps:
                cp.wait_send()

    def sibling_part(m):
        return Parts(lambda h: remote(
            p1.at[m, :, gene_part[h]], psib.at[m, :, gene_part[h]], ps_s.at[m, h], ps_r.at[m, h],
            group(0, 1)))

    ps = [sibling_part(m) for m in range(Z)]
    pending.extend(ps)

    def gene_loop(put, h=0, parts=1):
        n = G // NN // parts

        def step(i, _):
            put(pl.ds(pl.multiple_of(i * NN, NN), NN))
            return 0

        lax.fori_loop(h * n, (h + 1) * n, step, 0)

    def predict_pair(m):
        row = t_row(m, 0)

        def put(lanes):
            r = jnp.dot(slow_t[row:row + 2 * S, :], cells[:, lanes], preferred_element_type=F32)
            pacc[m, :, lanes] = r[:S]
            p1[m, :, lanes] = r[S:].astype(BF16)

        gene_loop(put)
        ps[m].start()

    def predict_cross(m, cc):
        row = t_row(m, cc)

        def part(lanes):
            return jnp.dot(slow_t[row:row + S, :], cells[:, lanes], preferred_element_type=F32)

        @pl.when(c == cc)
        def _():
            def put(lanes):
                pacc[m, :, lanes] = part(lanes)

            gene_loop(put)

        @pl.when(c != cc)
        def _():
            def put(lanes):
                p1[m, :, lanes] = part(lanes).astype(BF16)

            for h in range(HALVES):
                gene_loop(put, h, HALVES)
                ps[m].cps[h].start()

    def level_slot(b, m):
        return sum(Z >> (j + 1) for j in range(b)) + (m >> (b + 1))

    def level_part(b, m):
        sl, step_m = level_slot(b, m), 1 << b
        return Parts(lambda h: remote(
            psib.at[m ^ step_m, :, gene_part[h]], rs_in.at[sl, :, gene_part[h]],
            rs_s.at[sl, h], rs_r.at[sl, h], group(step_m, 0)))

    rs = {(b, m): level_part(b, m) for b in range(k.LV) for m in range(0, Z, 2 << b)}
    pending.extend(rs.values())

    def piece_sum(m, b, h):
        ps[m].cps[h].wait_recv()
        for j in range(b):
            rs[j, m].cps[h].wait_recv()

        def total(lanes):
            t = pacc[m, :, lanes] + psib[m, :, lanes].astype(F32)
            for j in range(b):
                t = t + rs_in[level_slot(j, m), :, lanes].astype(F32)
            return t
        return total

    per_part = A // HALVES

    def sum_level(b, m, send=True):
        for h in range(HALVES):
            total = piece_sum(m, b, h)
            for j in range(h * per_part, (h + 1) * per_part):
                lanes = slice(j * GA, (j + 1) * GA)
                psib[m, :, lanes] = total(lanes).astype(BF16)
            if send:
                rs[b, m ^ (1 << b)].cps[h].start()

    def far_levels(cc):
        @pl.when(c == cc)
        def _():
            for b in range(top):
                send_level(b, of_level(b, far))

    def send_level(b, ms):
        for m in ms:
            sum_level(b, m)

    top = k.LV - 1
    def of_level(b, ms):
        return [m for m in reversed(ms) if m % (2 << b) == 1 << b]

    pair_shares(0)

    @pl.when(at_end)
    def _():
        sent(far)
        send_logits([high])

    @pl.when(inside)
    def _():
        sent([high])
        send_logits(near)

    pair_shares(high)

    @pl.when(inside & (c == 0))
    def _():
        send_logits(far, (1, 0))

    @pl.when(at_end)
    def _():
        for m in far:
            for cc in range(2):
                wait_cross(m, cc)
                cross_shares(m, cc)

    for m in near:
        pair_shares(m)
    for cp in x_last + [y_last] + fwd_a + fwd_b:
        cp.wait_recv()

    @pl.when(at_end)
    def _():
        for cc in range(2):
            for m in far:
                predict_cross(m, cc)
        for cc in range(2):
            far_levels(cc)

    predict_pair(high)
    for b in range(top):
        for m in of_level(b, near):
            predict_pair(m)
        send_level(b, of_level(b, near))
    @pl.when(at_end)
    def _():
        predict_pair(0)

    @pl.when(inside)
    def _():
        for m in far:
            wait_cross(m, 0)

        @pl.when(c == 1)
        def _():
            send_logits(far, (1, 0))

        for m in far:
            cross_shares(m, 0)
            predict_cross(m, 0)
        far_levels(0)
        predict_pair(0)

        @pl.when(c == 0)
        def _():
            sum_level(top, high, False)

        for m in far:
            wait_cross(m, 1)
            cross_shares(m, 1)
            predict_cross(m, 1)

        @pl.when(c == 0)
        def _():
            rs[top, 0].start()

        far_levels(1)

    @pl.when(at_end | (c == 1))
    def _():
        sum_level(top, high)

    mem_rows = jnp.concatenate(
        [info[m, e, 1:1 + SLIDES, :] for m in range(Z) for e in range(2)], axis=1)
    mem16 = jnp.concatenate([mem_rows, jnp.zeros((16 - SLIDES, A * S), F32)], axis=0).astype(BF16)
    part_mass = lax.dot_general(mem16, slow[...], (((1,), (1,)), ((), ())), preferred_element_type=F32)
    col_tally = jnp.sum(mem_rows, axis=1, keepdims=True)
    gmeas = mstat[mine]
    for i, e, part, where in sharers:
        mst[i, e].wait_recv()
        gmeas = gmeas + mstat_in[i, e]
    packed = [gmeas[s:s + 1] for s in range(SLIDES)] + [jnp.zeros((1, NC - SLIDES * GA), F32)]
    mass_out[...] = jnp.concatenate(
        [part_mass[:SLIDES], jnp.broadcast_to(col_tally, (SLIDES, NC)),
         jnp.concatenate(packed, axis=1), jnp.zeros((1, NC), F32)], axis=0)
    gmc = []
    if k.PLANE:
        gm_out[...] = gmeas
        for i, where in others:
            gmc.append(remote(gm_out, gm_in.at[i], gm_s.at[i], gm_r.at[i], where))
            gmc[-1].start()
        pending.extend(gmc)
    mcp = []
    for i, (dx, dy) in enumerate(planes):
        cp = remote(mass_out, mass_in.at[i], ms_s.at[i], ms_r.at[i], plane(dx, dy))
        cp.start()
        mcp.append(cp)
    pending.extend(mcp)
    for cp in mcp:
        cp.wait_recv()
    msum = mass_out[...]
    for i in range(Q - 1):
        msum = msum + mass_in[i]
    mass = msum[:SLIDES]
    gmeas = jnp.concatenate(
        [msum[6:7, s * GA:(s + 1) * GA] for s in range(SLIDES)], axis=0)
    inv_gmeas = lax.rsqrt(gmeas + FLOOR)
    tally = jnp.maximum(msum[SLIDES:2 * SLIDES, 0:1], 1.0)
    quota = mass / tally
    prior_sum = jnp.sum(jnp.sum(cell_prior[...], axis=0, keepdims=True), axis=1, keepdims=True)
    prior = jnp.concatenate(
        [cell_prior[pl.ds(((z * X + bx) * 2 + c) * (YR // k.PL) + i, 1), :]
         for bx in range(X) for i in range(YR // k.PL)], axis=1) / prior_sum
    kl = jnp.sum(prior * (jnp.log(prior) - jnp.log(quota)), axis=1, keepdims=True)
    rat = prior / quota
    rat_hi = rat.astype(BF16)
    rat_lo = (rat - rat_hi.astype(F32)).astype(BF16)
    ratio_hl[...] = jnp.concatenate(
        [rat_hi, rat_lo, jnp.zeros((16 - 2 * SLIDES, NC), BF16)], axis=0)
    dd = jnp.dot(ratio_hl[...], slow[...], preferred_element_type=F32)
    dd = dd[:SLIDES] + dd[SLIDES:2 * SLIDES]
    dsum = jnp.sum(dd * mem_rows, axis=0, keepdims=True)
    mext[...] = jnp.concatenate(
        [mem_rows, mem_rows, jnp.zeros((16 - 2 * SLIDES, A * S), F32)], axis=0).astype(BF16)
    dcp = {}
    for m in range(Z):
        for e in range(2):
            lane = (m * 2 + e) * S
            dpart[m, e] = jnp.broadcast_to(dsum[:, lane:lane + S], (8, S))
    for m, e in groups:
        cp = remote(dpart.at[m, e], din.at[m, e], d_s.at[m, e], d_r.at[m, e], group(m, e))
        cp.start()
        dcp[m, e] = cp
        pending.append(cp)

    pred_sq = jnp.zeros((S, 1), F32)
    pred_meas = jnp.zeros((S, 1), F32)
    lane_id = lax.broadcasted_iota(jnp.int32, (1, GA), 1)
    for j in range(A):
        lanes = slice(j * GA, (j + 1) * GA)
        if j % per_part == 0:
            total = piece_sum(0, k.LV, j // per_part)
        p = total(lanes)
        pacc[0, :, lanes] = p
        q = meas[:, lanes].astype(F32)
        pq, pp = p * q, p * p
        pred_sq = pred_sq + jnp.sum(pp, axis=1, keepdims=True)
        pred_meas = pred_meas + jnp.sum(pq, axis=1, keepdims=True)
        for s in range(SLIDES):
            stat[j, s:s + 1, :] = jnp.sum(mcol[s] * pq, axis=0, keepdims=True)
            stat[j, 3 + s:4 + s, :] = jnp.sum(mcol[s] * pp, axis=0, keepdims=True)
    inv_pred = lax.rsqrt(pred_sq + FLOOR)
    spot_cos = pred_meas * inv_pred * inv_meas
    spot_sum = jnp.sum(wcol * spot_cos, axis=0, keepdims=True)
    scal = jnp.where(lane_id == 0, spot_sum, 0.0)
    for s in range(SLIDES):
        scal = scal + jnp.where(lane_id == 1 + s, kl[s:s + 1] * (1.0 / Q), 0.0)
    for j in range(A):
        stat[j, 6:8, :] = jnp.concatenate([scal, jnp.zeros((1, GA), F32)], axis=0)

    cps = []
    for i, e, part, where in sharers:
        cp = remote(stat.at[part], s1.at[i, e], s1_s.at[i, e], s1_r.at[i, e], where)
        cp.start()
        cps.append(cp)
    pending.extend(cps)
    u = stat[mine]
    for (i, e, part, where), cp in zip(sharers, cps):
        cp.wait_recv()
        u = u + s1[i, e]
    ubuf[...] = u
    cps = []
    for i, where in others:
        cp = remote(ubuf, s2.at[i], s2_s.at[i], s2_r.at[i], where)
        cp.start()
        cps.append(cp)
    pending.extend(cps)
    for cp in cps + gmc:
        cp.wait_recv()
    u = tree_sum(u, [s2[i] for i in range(len(others))])
    if k.PLANE:
        gmeas = tree_sum(gm_out[...], [gm_in[i] for i in range(len(others))])[:SLIDES]
        inv_gmeas = lax.rsqrt(gmeas + FLOOR)
    share = tally * (1.0 / G)
    a = lax.rsqrt(u[3:6] + FLOOR)
    b = inv_gmeas
    gcos = u[0:3] * a * b
    wall[mine] = jnp.concatenate(
        [share * a * b, share * gcos * a * a,
         jnp.sum(share * gcos, axis=0, keepdims=True), u[6:7]], axis=0)
    cps = []
    for i, e, part, where in sharers:
        cp = remote(wall.at[mine], wall.at[mine], s3_s.at[i, e], s3_r.at[i, e], where)
        cp.start()
        cps.append(cp)
    pending.extend(cps)
    for i, e, part, where in sharers:
        remote(wall.at[part], wall.at[part], s3_s.at[i, e], s3_r.at[i, e], where).wait_recv()

    lead = -(wcol * inv_pred * inv_meas)
    back = wcol * spot_cos * inv_pred * inv_pred
    dot1 = jnp.zeros((S, 1), F32)
    gene_total = jnp.zeros((1, GA), F32)
    for j in range(A):
        lanes = slice(j * GA, (j + 1) * GA)
        w = wall[j]
        direct = mcol[0] * w[0:1] + mcol[1] * w[1:2] + mcol[2] * w[2:3]
        damp = mcol[0] * w[3:4] + mcol[1] * w[4:5] + mcol[2] * w[5:6]
        gene_total = gene_total + w[6:7]
        p = pacc[0, :, lanes]
        g = (lead - direct) * meas[:, lanes].astype(F32) + (back + damp) * p
        glow = g.astype(BF16)
        gp[0, 0, :, lanes] = glow
        dot1 = dot1 + jnp.sum(glow.astype(F32) * p, axis=1, keepdims=True)

    gz, gc = {}, {}

    def to_core(m):
        cp = remote(gp.at[m, 0], gp.at[m, 1], gc_s.at[m], gc_r.at[m], group(0, 1))
        cp.start()
        gc[m] = cp
        pending.append(cp)

    def to_plane(m, b):
        t = m ^ (1 << b)
        cp = remote(gp.at[m, 0], gp.at[t, 0], gz_s.at[t], gz_r.at[t], group(1 << b, 0))
        cp.start()
        gz[t] = cp
        pending.append(cp)

    to_core(0)
    gz[high] = remote(gp.at[0, 0], gp.at[high, 0], gz_s.at[high], gz_r.at[high], group(high, 0))

    for b in range(top):
        t = 1 << b
        gz[t] = remote(gp.at[0, 0], gp.at[t, 0], gz_s.at[t], gz_r.at[t], group(t, 0))

    def near_start():
        for b in reversed(range(top)):
            gz[1 << b].start()

    @pl.when(c == 0)
    def _():
        gz[high].start()

    @pl.when(c == 1)
    def _():
        near_start()

    for m, e in groups:
        dcp[m, e].wait_recv()
    dtot = dpart[0, 0]
    for m, e in groups:
        dtot = dtot + din[m, e]
    dot_row = jnp.broadcast_to(dot1, (S, S)).T[0:8] - dtot
    info2[0, 0] = dot_row
    i2 = {}
    for m, e in groups:
        cp = remote(info2.at[0, 0], info2.at[m, e], i2_s.at[m, e], i2_r.at[m, e], group(m, e))
        cp.start()
        i2[m, e] = cp
        pending.append(cp)

    fin = wall[0]
    total_tally = jnp.sum(tally, axis=0, keepdims=True)
    gsum = jnp.sum(gene_total, axis=1, keepdims=True)
    dens = jnp.zeros((1, 1), F32)
    for s in range(SLIDES):
        dens = dens + tally[s:s + 1] * fin[7:8, 1 + s:2 + s]
    lid = lax.broadcasted_iota(jnp.int32, (8, 128), 1)
    out_loss[...] = (jnp.where(lid == 0, fin[7:8, 0:1], 0.0) + jnp.where(lid == 1, gsum, 0.0)
                     + jnp.where(lid == 2, dens, 0.0)) / total_tally

    ycp = {}

    def map_rows(m, es, gpm):
        n = len(es)

        def step(i, _):
            r0 = pl.multiple_of(i * RC, RC)
            low = lax.dot_general(cells[pl.ds(r0, RC), :], gpm(),
                                  (((1,), (1,)), ((), ())), preferred_element_type=F32)
            mx = [mext[:, pl.ds(pl.multiple_of((m * 2 + e) * S, S), S)] for e in es]
            rt = lax.dot_general(ratio_hl[:, pl.ds(r0, RC)], jnp.concatenate(mx, axis=1),
                                 (((0,), (0,)), ((), ())), preferred_element_type=F32)
            low = low - rt
            per = YR // RC
            for i_e, e in enumerate(es):
                sh = shares_of(m, e, i) * float(k.CELLS)
                v = sh * (low[:, i_e * S:(i_e + 1) * S] - info2[m, e, 0:1, :])
                ybuf[(m * 2 + e) * X + i // per,
                     pl.ds(pl.multiple_of(lax.rem(i, per) * RC, RC), RC), :] = v.astype(BF16)
            return 0

        lax.fori_loop(0, NC // RC, step, 0)

    def map_copies(m, es):
        cps = []
        for e in es:
            src = ybuf.at[pl.ds((m * 2 + e) * X, X)]
            if m == 0 and type(e) is int and e == 0:
                cps.append(pltpu.make_async_copy(src, out_map.at[z, :, c], loc_sem.at[3]))
                ycp[0, 0] = cps[-1]
            else:
                cps.append(remote(src, out_map.at[z, :, c], y_s.at[m, e], y_r.at[m, e],
                                  group(m, e)))
                pending.append(cps[-1])
        return cps

    def send_map(m, es):
        for cp in map_copies(m, es):
            cp.start()

    def map_piece(m):
        for e in range(2):
            if (m, e) != (0, 0):
                i2[m, e].wait_recv()
        map_rows(m, [0, 1], lambda: gp[m].reshape(2 * S, G))
        send_map(m, [0, 1])

    gc[0].wait_recv()
    map_piece(0)

    def pass_on(m, b):
        for b2 in reversed(range(b)):
            to_plane(m, b2)
        to_core(m)

    gc[high] = remote(gp.at[high, 0], gp.at[high, 1], gc_s.at[high], gc_r.at[high], group(0, 1))
    pending.append(gc[high])
    for b2 in range(top):
        t = high ^ (1 << b2)
        gz[t] = remote(gp.at[high, 0], gp.at[t, 0], gz_s.at[t], gz_r.at[t], group(1 << b2, 0))
        pending.append(gz[t])

    def high_on():
        gz[high].wait_recv()
        gc[high].start()
        for b2 in reversed(range(top)):
            gz[high ^ (1 << b2)].start()

    @pl.when(c == 0)
    def _():
        gz[high].wait_send()
        pl.semaphore_signal(gate, inc=1, device_id=group(0, 1), device_id_type=MESH_ID)
        near_start()
        high_on()

    @pl.when(c == 1)
    def _():
        pl.semaphore_wait(gate, 1)
        gz[high].start()
        gc[high].wait_recv()

    i2[high, 0].wait_recv()
    i2[high, 1].wait_recv()
    map_rows(high, [c], lambda: gp[high, c])

    @pl.when(c == 1)
    def _():
        high_on()

    @pl.when(c == 0)
    def _():
        gc[high].wait_recv()

    own_core = map_copies(high, [c])

    @pl.when(at_end)
    def _():
        own_core[0].start()

    map_rows(high, [1 - c], lambda: gp[high, 1 - c])

    @pl.when(inside)
    def _():
        own_core[0].start()

    send_map(high, [1 - c])
    for b in reversed(range(top)):
        for m in range(1 << b, Z, 2 << b):
            gz[m].wait_recv()
            pass_on(m, b)
    def slot_of(dx, dy, half):
        return ((dx * Y + dy) - 1) * 2 + half

    def single_rows(dx, dy, half):
        bx = lax.rem(x + dx, X)
        by = flip(y, dy)
        return pl.multiple_of(((bx * Y + by) * 2 + half) * H, H)

    def single_part(dx, dy, half, put, m0=0, m1=Z):
        r0 = single_rows(dx, dy, half)
        n = (m1 - m0) * 2 * S

        def step(i, _):
            lanes = pl.ds(pl.multiple_of(i * NN, NN), NN)
            v = jnp.dot(slow[pl.ds(r0, H), m0 * 2 * S:m1 * 2 * S],
                        gp[pl.ds(m0, m1 - m0), :, :, lanes].reshape(n, NN), preferred_element_type=F32)
            put(lanes, v)
            return 0

        lax.fori_loop(0, G // NN, step, 0)

    def put_send(slot, extra=()):
        def put(lanes, v):
            for i in extra:
                v = v + grecv[i, :, lanes].astype(F32)
            gsend[slot, :, lanes] = v.astype(BF16)
        return put

    def put_own(half):
        def put(lanes, v):
            own_single[half * H:(half + 1) * H, lanes] = v
        return put

    def put_rest(sl, half):
        def put(lanes, v):
            v = v + own_single[half * H:(half + 1) * H, lanes]
            gsend[sl, :, lanes] = v.astype(BF16)
        return put

    r_m1 = lambda d: d
    r_m2 = lambda d: XN + d
    r_m3 = lambda d: 2 * XN + d
    r_m5 = lambda d: 3 * XN + d
    r_m4, r_m6 = 4 * XN, 4 * XN + 1
    gcp = {}

    def send_single(slot, r_slot, where):
        cp = remote(gsend.at[slot], grecv.at[r_slot], gs_s.at[r_slot], gs_r.at[r_slot], where)
        cp.start()
        gcp[r_slot] = cp
        pending.append(cp)

    for m in range(1, Z - 1):
        if m != high:
            gc[m].wait_recv()
    for half in range(2):
        single_part(1, 1, half, put_own(half), 0, Z - 1)
    if Z > 2:
        gc[Z - 1].wait_recv()
    for d in range(XN):
        for half in range(2):
            sl = slot_of(d + 1, 1, half)
            if d == 0:
                single_part(1, 1, half, put_rest(sl, half), Z - 1, Z)
            else:
                single_part(d + 1, 1, half, put_send(sl))
            if half == 0:
                send_single(sl, r_m1(d), plane(d + 1, 0))
            else:
                send_single(sl, r_m2(d), plane(0, 1))
    for m in far:
        map_piece(m)
    for d in range(XN):
        s0 = slot_of(d + 1, 0, 0)
        single_part(d + 1, 0, 0, put_send(s0))
        send_single(s0, r_m3(d), plane(d + 1, 0))
    s0 = slot_of(0, 1, 1)
    single_part(0, 1, 1, put_send(s0))
    send_single(s0, r_m4, plane(0, 1))

    for m in near:
        map_piece(m)

    for d in range(XN):
        gcp[r_m2(d)].wait_recv()
        s0 = slot_of(d + 1, 0, 1)
        single_part(d + 1, 0, 1, put_send(s0, [r_m2(d)]))
        send_single(s0, r_m5(d), plane(d + 1, 0))
    for d in range(XN):
        gcp[r_m1(d)].wait_recv()
    s0 = slot_of(0, 1, 0)
    single_part(0, 1, 0, put_send(s0, [r_m1(d) for d in range(XN)]))
    send_single(s0, r_m6, plane(0, 1))

    for half in range(2):
        single_part(0, 0, half, put_own(half))
    cp_single = []
    halves = [[r_m3(d) for d in range(XN)] + [r_m6], [r_m5(d) for d in range(XN)] + [r_m4]]
    for half in range(2):
        for i in halves[half]:
            gcp[i].wait_recv()

        def step(i, _):
            lanes = pl.ds(pl.multiple_of(i * NN, NN), NN)
            v = own_single[half * H:(half + 1) * H, lanes]
            for i2_ in halves[half]:
                v = v + grecv[i2_, :, lanes].astype(F32)
            own_single[half * H:(half + 1) * H, lanes] = v * float(k.CELLS) ** 0.5
            return 0

        lax.fori_loop(0, G // NN, step, 0)
        rows_h = pl.ds(half * H, H)
        cp_single.append(pltpu.make_async_copy(
            own_single.at[rows_h], out_single.at[rows_h], loc_sem.at[4 + half]))
        cp_single[half].start()

    for m, e in groups:
        other = (flip(z, m), slice(None), flip(c, e))
        remote(ybuf.at[pl.ds(0, X)], out_map.at[other[0], :, other[2]], y_s.at[m, e], y_r.at[m, e],
               group(m, e)).wait_recv()
    ycp[0, 0].wait()
    for cp in cp_single:
        cp.wait()
    for cp in pending:
        cp.wait_send()
    for b in range(top):
        gz[1 << b].wait_send()

    @pl.when(c == 1)
    def _():
        gz[high].wait_send()

    @pl.when(at_end)
    def _():
        sent([high])

    @pl.when(inside)
    def _():
        sent(far)


def forward_and_back(k, logits, single_cell, spatial, ids, mask, cell_prior, order):
    Z, X, Y, A, Q, S, G, R, H = k.Z, k.X, k.Y, k.A, k.Q, k.S, k.G, k.R, k.H
    YR, NC, GA, XN = k.YR, k.NC, k.GA, k.X - 1
    vm = pl.BlockSpec(memory_space=pltpu.VMEM)
    hbm = pl.BlockSpec(memory_space=pl.ANY)
    dma = lambda *s: pltpu.SemaphoreType.DMA(s)
    ncl, ngs = 4 * XN + 2, 4 * XN + 2
    scratch = [
        pltpu.VMEM((Z, 2, X, YR, S), BF16),
        pltpu.VMEM((NC, G), BF16),
        pltpu.VMEM((NC, A * S), BF16),
        pltpu.VMEM((A * S, NC), BF16),
        pltpu.VMEM((A * X, YR, S), BF16),
        pltpu.VMEM((Z, 2, 8, S), F32),
        pltpu.VMEM((Z, 2, 8, S), F32),
        pltpu.VMEM((Z, S, G), F32),
        pltpu.VMEM((Z, S, G), BF16),
        pltpu.VMEM((Z, S, G), BF16),
        pltpu.VMEM((Z - 1, S, G), BF16),
        pltpu.VMEM((S, G), BF16),
        pltpu.VMEM((Z, 2, S, G), BF16),
        pltpu.VMEM((2 * (Q - 1), H, G), BF16),
        pltpu.VMEM((ngs, H, G), BF16),
        pltpu.VMEM((8, NC), F32),
        pltpu.VMEM((Q - 1, 8, NC), F32),
        pltpu.VMEM((16, NC), BF16),
        pltpu.VMEM((16, A * S), BF16),
        pltpu.VMEM((Z, 2, 8, S), F32),
        pltpu.VMEM((Z, 2, 8, S), F32),
        pltpu.VMEM((A, 8, GA), F32),
        pltpu.VMEM((Z, 2, 8, GA), F32),
        pltpu.VMEM((8, GA), F32),
        pltpu.VMEM((Q - 1, 8, GA), F32),
        pltpu.VMEM((A, 8, GA), F32),
        pltpu.VMEM((Z, 2, 8, GA), F32),
        pltpu.VMEM((8, GA), F32),
        pltpu.VMEM((Q - 1, 8, GA), F32),
        pltpu.VMEM((A, 8, GA), F32),
        pltpu.VMEM((R, G), F32),
        dma(6),
        dma(Z, 2), dma(Z, 2),
        dma(ncl), dma(ncl),
        dma(Z, 2), dma(Z, 2),
        dma(Z, HALVES), dma(Z, HALVES),
        dma(Z - 1, HALVES), dma(Z - 1, HALVES),
        dma(Q - 1), dma(Q - 1),
        dma(Z, 2), dma(Z, 2),
        dma(Z, 2), dma(Z, 2),
        dma(Q - 1), dma(Q - 1),
        dma(Z, 2), dma(Z, 2),
        dma(Z), dma(Z),
        dma(Z), dma(Z),
        dma(Z, 2), dma(Z, 2),
        dma(Z, 2), dma(Z, 2),
        dma(ngs), dma(ngs),
        dma(Z, 2), dma(Z, 2),
        pltpu.SemaphoreType.REGULAR,
        dma(Q - 1), dma(Q - 1),
    ]
    return pl.pallas_call(
        functools.partial(kernel, k),
        name="mapping",
        out_shape=[
            jax.ShapeDtypeStruct((Z, X, 2, YR, S), BF16),
            jax.ShapeDtypeStruct((R, G), F32),
            jax.ShapeDtypeStruct((8, 128), F32),
        ],
        in_specs=[hbm, hbm, hbm, vm, vm, vm, vm, vm],
        out_specs=[hbm, hbm, vm],
        scratch_shapes=scratch,
        compiler_params=pltpu.CompilerParams(
            collective_id=0, has_side_effects=True, vmem_limit_bytes=64000 * 1024),
        cost_estimate=pl.CostEstimate(
            flops=6 * NC * A * S * G, bytes_accessed=32 << 20, transcendentals=2 * NC * A * S),
    )(logits.reshape(Z, X, 2, YR, S), logits.reshape(A * X, YR, S), single_cell, spatial,
      ids.reshape(1, S), mask.reshape(1, S), cell_prior.reshape(-1, k.PL), order.reshape(1, k.NB))


def body(mesh, map_logits, single_cell, spatial, slide_ids, spot_mask, cell_prior, gene_order):
    cells, spots = map_logits.shape
    k = Sizes(mesh, cells, spatial.shape[1], spots, gene_order.shape[0])
    gmap, gsingle, loss = forward_and_back(
        k, map_logits, single_cell, spatial, slide_ids, spot_mask, cell_prior, gene_order)
    grad_map = gmap.reshape(cells, spots).astype(F32)
    return loss[0, :3], grad_map, gsingle


def solution(mesh):
    k = Sizes(mesh, 1 << 20, 1 << 20, 128, 1)
    fine = Mesh(mesh.devices.reshape(k.Z, k.X, 2, k.Y), AXES)
    in_specs = (P(None, AXES), P(AXES, None), P(AXES, None), P(AXES), P(AXES), P(), P())
    out_specs = (P(), P(None, AXES), P(AXES, None))
    return jax.shard_map(functools.partial(body, mesh), mesh=fine, in_specs=in_specs,
                         out_specs=out_specs, check_vma=False)
```

```python
import functools

import jax
import jax.numpy as jnp
from jax import lax
from jax.experimental import pallas as pl
from jax.experimental.pallas import tpu as pltpu
from jax.sharding import Mesh, PartitionSpec as P

SLIDES = 3
HALVES = 2
FLOOR = 1e-06
F32 = jnp.float32
BF16 = jnp.bfloat16
AXES = ("z", "x", "c", "y")
MESH_ID = pl.DeviceIdType.MESH


def flip(value, mask):
    bit = 1
    while bit <= mask:
        if mask & bit:
            value = value + (1 - 2 * ((value // bit) % 2)) * bit
        bit *= 2
    return value


class Sizes:
    def __init__(self, mesh, cells, genes, spots, blocks):
        n = mesh.shape["spot"] // 2
        zs = 1
        while zs * zs * 4 <= 2 * n:
            zs *= 2
        self.Z, self.X, self.Y = zs, n // zs, mesh.shape["grp"]
        assert self.Y == 2 and self.Z * self.X == n and self.Z >= 2
        self.LV = self.Z.bit_length() - 1
        self.A = 2 * self.Z
        self.Q = self.X * self.Y
        self.CELLS, self.G, self.S, self.NB = cells, genes, spots, blocks
        self.R = cells // (self.A * self.Q)
        self.H = self.R // 2
        self.YR = self.Y * self.R
        self.NC = self.X * self.YR
        self.GA = genes // self.A
        self.RC = min(512, self.YR)
        self.PL = min(128, self.YR)
        self.PLANE = 2 * self.Q == self.A
        self.NN = min(512, genes)


def kernel(k, logits, logits_flat, own_cells, spatial, ids, mask, cell_prior, order,
           out_map, out_single, out_loss,
           lbuf, cells, slow, slow_t, ybuf, info, info2,
           pacc, p1, psib, rs_in, meas,
           gp, gsend, grecv,
           mass_out, mass_in, ratio_hl, mext, dpart, din,
           mstat, mstat_in, gm_out, gm_in, stat, s1, ubuf, s2, wall, own_single,
           loc_sem, lg_s, lg_r, cl_s, cl_r, in_s, in_r, ps_s, ps_r, rs_s, rs_r, ms_s, ms_r,
           d_s, d_r, s1_s, s1_r, s2_s, s2_r, s3_s, s3_r, gz_s, gz_r, gc_s, gc_r, i2_s, i2_r,
           y_s, y_r, gs_s, gs_r, mt_s, mt_r, gate, gm_s, gm_r):
    Z, X, Y, A, Q, S, G, R, H = k.Z, k.X, k.Y, k.A, k.Q, k.S, k.G, k.R, k.H
    YR, NC, GA, RC, NN = k.YR, k.NC, k.GA, k.RC, k.NN
    z, x, c, y = [lax.axis_index(a) for a in AXES]
    yo = 1 - y

    def group(m, e):
        return (flip(z, m), x, c + e - 2 * c * e, y)

    def plane(dx, dy):
        return (z, lax.rem(x + dx, X), c, flip(y, dy))

    def remote(src, dst, send, recv, where):
        return pltpu.make_async_remote_copy(
            src_ref=src, dst_ref=dst, send_sem=send, recv_sem=recv,
            device_id=where, device_id_type=MESH_ID)

    groups = [(m, e) for m in reversed(range(Z)) for e in (1, 0) if (m, e) != (0, 0)]
    planes = [(dx, dy) for dx in reversed(range(X)) for dy in (1, 0) if (dx, dy) != (0, 0)]
    me = z * 2 + c

    def part_of(dx, dy, e):
        return (lax.rem(x + dx, X) * Y + flip(y, dy)) * 2 + c + e - 2 * c * e

    if k.PLANE:
        mine = part_of(0, 0, 0)
        sharers = [(dx * Y + dy, e, part_of(dx, dy, e),
                    (z, lax.rem(x + dx, X), c + e - 2 * c * e, flip(y, dy)))
                   for dx in reversed(range(X)) for dy in (1, 0) for e in (1, 0)
                   if (dx, dy, e) != (0, 0, 0)]
        others = [(m - 1, group(m, 0)) for m in reversed(range(1, Z))]
    else:
        mine = me
        sharers = [(m, e, flip(z, m) * 2 + flip(c, e), group(m, e)) for m, e in groups]
        others = [(i, plane(dx, dy)) for i, (dx, dy) in enumerate(planes)]

    def tree_sum(first, parts):
        v = [first] + list(parts)
        while len(v) > 1:
            v = [v[i] + v[i + 1] if i + 1 < len(v) else v[i] for i in range(0, len(v), 2)]
        return v[0]

    pending = []

    cp_flat = pltpu.make_async_copy(logits_flat, ybuf, loc_sem.at[0])
    cp_flat.start()
    cp_own = pltpu.make_async_copy(logits.at[z, :, c], lbuf.at[0, 0], loc_sem.at[1])
    cp_own.start()
    cp_cells = pltpu.make_async_copy(
        own_cells, cells.at[pl.ds(pl.multiple_of((x * Y + y) * R, R), R)], loc_sem.at[2])
    cp_cells.start()
    barrier = pltpu.get_barrier_semaphore()
    for m, e in groups:
        pl.semaphore_signal(barrier, inc=1, device_id=group(m, e), device_id_type=MESH_ID)
    for dx, dy in planes:
        pl.semaphore_signal(barrier, inc=1, device_id=plane(dx, dy), device_id_type=MESH_ID)
    greeted = len(groups) + len(planes)
    if k.PLANE:
        for dx, dy in planes:
            pl.semaphore_signal(barrier, inc=1, device_id=(*plane(dx, dy)[:2], 1 - c, flip(y, dy)),
                                device_id_type=MESH_ID)
        greeted += len(planes)
    pl.semaphore_wait(barrier, greeted)

    def rows(bx, by, half):
        return cells.at[pl.ds(pl.multiple_of(((bx * Y + by) * 2 + half) * H, H), H)]

    XN = X - 1

    def cell_copy(slot, src, bx, by, half, where):
        return remote(src, rows(bx, by, half), cl_s.at[slot], cl_r.at[slot], where)

    own_half = [own_cells.at[pl.ds(0, H)], own_cells.at[pl.ds(H, H)]]
    x_first = [cell_copy(d, own_half[0], x, y, 0, plane(d + 1, 0)) for d in range(XN)]
    x_last = [cell_copy(XN + d, own_half[1], x, y, 1, plane(d + 1, 0)) for d in range(XN)]
    y_first = cell_copy(2 * XN, own_half[1], x, y, 1, plane(0, 1))
    y_last = cell_copy(2 * XN + 1, own_half[0], x, y, 0, plane(0, 1))
    for cp in x_first + [y_first]:
        cp.start()

    high = Z // 2
    far = [m for m in range(Z) if m & high and m != high]
    near = [m for m in range(1, Z) if not m & high]
    lg = {(m, e): remote(logits.at[flip(z, m), :, flip(c, e)], lbuf.at[m, e],
                         lg_s.at[m, e], lg_r.at[m, e], group(m, e)) for m, e in groups}

    pending.extend(cp for (m, e), cp in lg.items() if m in [0] + near)

    def sent(ms):
        for m in ms:
            for e in range(2):
                lg[m, e].wait_send()

    def send_logits(ms, es=(0, 1)):
        for m in ms:
            for e in es:
                lg[m, e].start()

    at_end = (z == 0) | (z == Z - 1)
    inside = jnp.logical_not(at_end)
    lg[0, 1].start()

    @pl.when(at_end)
    def _():
        send_logits(near + far)

    @pl.when(inside)
    def _():
        send_logits([high])

    for cp in x_last + [y_last]:
        cp.start()
    pending.extend(x_first + x_last + [y_first, y_last])

    cp_flat.wait()

    def add_exp(i, acc):
        e = jnp.exp(ybuf[i].astype(F32))
        return acc + jnp.sum(e.reshape(YR // 8, 8, S), axis=0)

    acc = lax.fori_loop(0, A * X, add_exp, jnp.zeros((8, S), F32))
    inv_sum = 1.0 / jnp.sum(acc, axis=0, keepdims=True)
    idr = ids[...]
    maskf = mask[...].astype(F32)
    mrow = [jnp.where(idr == s, maskf, 0.0) for s in range(SLIDES)]
    info[0, 0] = jnp.concatenate([inv_sum] + mrow + [jnp.zeros((8 - 1 - SLIDES, S), F32)], axis=0)
    inf = {}
    for m, e in groups:
        inf[m, e] = remote(info.at[0, 0], info.at[m, e], in_s.at[m, e], in_r.at[m, e], group(m, e))
        inf[m, e].start()
        pending.append(inf[m, e])

    W = G // k.NB
    for b in range(k.NB):
        v = jnp.zeros((S, W), F32)
        for j in range(k.NB):
            here = (order[0:1, j:j + 1] == b).astype(F32)
            v = v + here * spatial[:, j * W:(j + 1) * W].astype(F32)
        meas[:, b * W:(b + 1) * W] = v.astype(BF16)
    mcols = jnp.concatenate(mrow + [maskf] + [jnp.zeros((8 - 1 - SLIDES, S), F32)], axis=0).T
    mcol = [mcols[:, s:s + 1] for s in range(SLIDES)]
    wcol = mcols[:, SLIDES:SLIDES + 1]
    meas_sq = jnp.zeros((S, 1), F32)
    for j in range(A):
        v = meas[:, j * GA:(j + 1) * GA].astype(F32)
        v = v * v
        meas_sq = meas_sq + jnp.sum(v, axis=1, keepdims=True)
        for s in range(SLIDES):
            mstat[j, s:s + 1, :] = jnp.sum(mcol[s] * v, axis=0, keepdims=True)
        mstat[j, SLIDES:8, :] = jnp.zeros((8 - SLIDES, GA), F32)
    inv_meas = lax.rsqrt(meas_sq + FLOOR)
    mst = {}
    for i, e, part, where in sharers:
        mst[i, e] = remote(mstat.at[part], mstat_in.at[i, e], mt_s.at[i, e], mt_r.at[i, e], where)
        mst[i, e].start()
    pending.extend(mst.values())

    fwd_a, fwd_b = [], []
    for d in range(XN):
        bx = lax.rem(x - (d + 1) + X, X)
        cell_copy(d, own_half[0], bx, y, 0, plane(d + 1, 0)).wait_recv()
        cp = cell_copy(2 * XN + 2 + d, rows(bx, y, 0), bx, y, 0, plane(0, 1))
        cp.start()
        fwd_a.append(cp)
    y_first.wait_recv()
    for d in range(XN):
        cp = cell_copy(3 * XN + 2 + d, rows(x, yo, 1), x, yo, 1, plane(d + 1, 0))
        cp.start()
        fwd_b.append(cp)
    pending.extend(fwd_a + fwd_b)

    cp_own.wait()
    cp_cells.wait()

    def shares_of(m, e, i):
        per = YR // RC
        l = lbuf[m, e, i // per, pl.ds(pl.multiple_of(lax.rem(i, per) * RC, RC), RC), :]
        return jnp.exp(l.astype(F32)) * info[m, e, 0:1, :]

    def t_row(m, i):
        return (m * 2 + i) * S

    def slot(cc):
        return c if cc == 0 else 1 - c

    def wait_cross(m, cc):
        e = slot(cc)
        remote(info.at[0, 0], info.at[m, e], in_s.at[m, e], in_r.at[m, e],
               group(m, e)).wait_recv()
        remote(lbuf.at[0, 0], lbuf.at[m, e], lg_s.at[m, e], lg_r.at[m, e],
               group(m, e)).wait_recv()

    def wait_pair(m):
        for e in range(2):
            if (m, e) != (0, 0):
                inf[m, e].wait_recv()
                lg[m, e].wait_recv()

    def make_shares(m, e, row):
        lane = (m * 2 + e) * S
        if type(e) is not int:
            lane = pl.multiple_of(lane, S)

        def step(i, _):
            sh = shares_of(m, e, i).astype(BF16)
            r0 = pl.multiple_of(i * RC, RC)
            slow[pl.ds(r0, RC), pl.ds(lane, S)] = sh
            slow_t[row:row + S, pl.ds(r0, RC)] = sh.T
            return 0

        lax.fori_loop(0, NC // RC, step, 0)

    def pair_shares(m):
        wait_pair(m)
        for e in range(2):
            make_shares(m, e, t_row(m, e))

    def cross_shares(m, cc):
        make_shares(m, slot(cc), t_row(m, cc))

    gene_part = [pl.ds(h * (G // HALVES), G // HALVES) for h in range(HALVES)]

    class Parts:
        def __init__(self, make):
            self.cps = [make(h) for h in range(HALVES)]

        def start(self):
            for cp in self.cps:
                cp.start()

        def wait_send(self):
            for cp in self.cps:
                cp.wait_send()

    def sibling_part(m):
        return Parts(lambda h: remote(
            p1.at[m, :, gene_part[h]], psib.at[m, :, gene_part[h]], ps_s.at[m, h], ps_r.at[m, h],
            group(0, 1)))

    ps = [sibling_part(m) for m in range(Z)]
    pending.extend(ps)

    def gene_loop(put, h=0, parts=1):
        n = G // NN // parts

        def step(i, _):
            put(pl.ds(pl.multiple_of(i * NN, NN), NN))
            return 0

        lax.fori_loop(h * n, (h + 1) * n, step, 0)

    def predict_pair(m):
        row = t_row(m, 0)

        def put(lanes):
            r = jnp.dot(slow_t[row:row + 2 * S, :], cells[:, lanes], preferred_element_type=F32)
            pacc[m, :, lanes] = r[:S]
            p1[m, :, lanes] = r[S:].astype(BF16)

        gene_loop(put)
        ps[m].start()

    def predict_cross(m, cc):
        row = t_row(m, cc)

        def part(lanes):
            return jnp.dot(slow_t[row:row + S, :], cells[:, lanes], preferred_element_type=F32)

        @pl.when(c == cc)
        def _():
            def put(lanes):
                pacc[m, :, lanes] = part(lanes)

            gene_loop(put)

        @pl.when(c != cc)
        def _():
            def put(lanes):
                p1[m, :, lanes] = part(lanes).astype(BF16)

            for h in range(HALVES):
                gene_loop(put, h, HALVES)
                ps[m].cps[h].start()

    def level_slot(b, m):
        return sum(Z >> (j + 1) for j in range(b)) + (m >> (b + 1))

    def level_part(b, m):
        sl, step_m = level_slot(b, m), 1 << b
        return Parts(lambda h: remote(
            psib.at[m ^ step_m, :, gene_part[h]], rs_in.at[sl, :, gene_part[h]],
            rs_s.at[sl, h], rs_r.at[sl, h], group(step_m, 0)))

    rs = {(b, m): level_part(b, m) for b in range(k.LV) for m in range(0, Z, 2 << b)}
    pending.extend(rs.values())

    def piece_sum(m, b, h):
        ps[m].cps[h].wait_recv()
        for j in range(b):
            rs[j, m].cps[h].wait_recv()

        def total(lanes):
            t = pacc[m, :, lanes] + psib[m, :, lanes].astype(F32)
            for j in range(b):
                t = t + rs_in[level_slot(j, m), :, lanes].astype(F32)
            return t
        return total

    per_part = A // HALVES

    def sum_level(b, m, send=True):
        for h in range(HALVES):
            total = piece_sum(m, b, h)
            for j in range(h * per_part, (h + 1) * per_part):
                lanes = slice(j * GA, (j + 1) * GA)
                psib[m, :, lanes] = total(lanes).astype(BF16)
            if send:
                rs[b, m ^ (1 << b)].cps[h].start()

    def far_levels(cc):
        @pl.when(c == cc)
        def _():
            for b in range(top):
                send_level(b, of_level(b, far))

    def send_level(b, ms):
        for m in ms:
            sum_level(b, m)

    top = k.LV - 1
    def of_level(b, ms):
        return [m for m in reversed(ms) if m % (2 << b) == 1 << b]

    pair_shares(0)

    @pl.when(at_end)
    def _():
        sent(far)
        send_logits([high])

    @pl.when(inside)
    def _():
        sent([high])
        send_logits(near)

    pair_shares(high)

    @pl.when(inside & (c == 0))
    def _():
        send_logits(far, (1, 0))

    @pl.when(at_end)
    def _():
        for m in far:
            for cc in range(2):
                wait_cross(m, cc)
                cross_shares(m, cc)

    for m in near:
        pair_shares(m)
    for cp in x_last + [y_last] + fwd_a + fwd_b:
        cp.wait_recv()

    @pl.when(at_end)
    def _():
        for cc in range(2):
            for m in far:
                predict_cross(m, cc)
        for cc in range(2):
            far_levels(cc)

    predict_pair(high)
    for b in range(top):
        for m in of_level(b, near):
            predict_pair(m)
        send_level(b, of_level(b, near))
    @pl.when(at_end)
    def _():
        predict_pair(0)

    @pl.when(inside)
    def _():
        for m in far:
            wait_cross(m, 0)

        @pl.when(c == 1)
        def _():
            send_logits(far, (1, 0))

        for m in far:
            cross_shares(m, 0)
            predict_cross(m, 0)
        far_levels(0)
        predict_pair(0)

        @pl.when(c == 0)
        def _():
            sum_level(top, high, False)

        for m in far:
            wait_cross(m, 1)
            cross_shares(m, 1)
            predict_cross(m, 1)

        @pl.when(c == 0)
        def _():
            rs[top, 0].start()

        far_levels(1)

    @pl.when(at_end | (c == 1))
    def _():
        sum_level(top, high)

    mem_rows = jnp.concatenate(
        [info[m, e, 1:1 + SLIDES, :] for m in range(Z) for e in range(2)], axis=1)
    mem16 = jnp.concatenate([mem_rows, jnp.zeros((16 - SLIDES, A * S), F32)], axis=0).astype(BF16)
    part_mass = lax.dot_general(mem16, slow[...], (((1,), (1,)), ((), ())), preferred_element_type=F32)
    col_tally = jnp.sum(mem_rows, axis=1, keepdims=True)
    gmeas = mstat[mine]
    for i, e, part, where in sharers:
        mst[i, e].wait_recv()
        gmeas = gmeas + mstat_in[i, e]
    packed = [gmeas[s:s + 1] for s in range(SLIDES)] + [jnp.zeros((1, NC - SLIDES * GA), F32)]
    mass_out[...] = jnp.concatenate(
        [part_mass[:SLIDES], jnp.broadcast_to(col_tally, (SLIDES, NC)),
         jnp.concatenate(packed, axis=1), jnp.zeros((1, NC), F32)], axis=0)
    gmc = []
    if k.PLANE:
        gm_out[...] = gmeas
        for i, where in others:
            gmc.append(remote(gm_out, gm_in.at[i], gm_s.at[i], gm_r.at[i], where))
            gmc[-1].start()
        pending.extend(gmc)
    mcp = []
    for i, (dx, dy) in enumerate(planes):
        cp = remote(mass_out, mass_in.at[i], ms_s.at[i], ms_r.at[i], plane(dx, dy))
        cp.start()
        mcp.append(cp)
    pending.extend(mcp)
    for cp in mcp:
        cp.wait_recv()
    msum = mass_out[...]
    for i in range(Q - 1):
        msum = msum + mass_in[i]
    mass = msum[:SLIDES]
    gmeas = jnp.concatenate(
        [msum[6:7, s * GA:(s + 1) * GA] for s in range(SLIDES)], axis=0)
    inv_gmeas = lax.rsqrt(gmeas + FLOOR)
    tally = jnp.maximum(msum[SLIDES:2 * SLIDES, 0:1], 1.0)
    quota = mass / tally
    prior_sum = jnp.sum(jnp.sum(cell_prior[...], axis=0, keepdims=True), axis=1, keepdims=True)
    prior = jnp.concatenate(
        [cell_prior[pl.ds(((z * X + bx) * 2 + c) * (YR // k.PL) + i, 1), :]
         for bx in range(X) for i in range(YR // k.PL)], axis=1) / prior_sum
    kl = jnp.sum(prior * (jnp.log(prior) - jnp.log(quota)), axis=1, keepdims=True)
    rat = prior / quota
    rat_hi = rat.astype(BF16)
    rat_lo = (rat - rat_hi.astype(F32)).astype(BF16)
    ratio_hl[...] = jnp.concatenate(
        [rat_hi, rat_lo, jnp.zeros((16 - 2 * SLIDES, NC), BF16)], axis=0)
    dd = jnp.dot(ratio_hl[...], slow[...], preferred_element_type=F32)
    dd = dd[:SLIDES] + dd[SLIDES:2 * SLIDES]
    dsum = jnp.sum(dd * mem_rows, axis=0, keepdims=True)
    mext[...] = jnp.concatenate(
        [mem_rows, mem_rows, jnp.zeros((16 - 2 * SLIDES, A * S), F32)], axis=0).astype(BF16)
    dcp = {}
    for m in range(Z):
        for e in range(2):
            lane = (m * 2 + e) * S
            dpart[m, e] = jnp.broadcast_to(dsum[:, lane:lane + S], (8, S))
    for m, e in groups:
        cp = remote(dpart.at[m, e], din.at[m, e], d_s.at[m, e], d_r.at[m, e], group(m, e))
        cp.start()
        dcp[m, e] = cp
        pending.append(cp)

    pred_sq = jnp.zeros((S, 1), F32)
    pred_meas = jnp.zeros((S, 1), F32)
    lane_id = lax.broadcasted_iota(jnp.int32, (1, GA), 1)
    for j in range(A):
        lanes = slice(j * GA, (j + 1) * GA)
        if j % per_part == 0:
            total = piece_sum(0, k.LV, j // per_part)
        p = total(lanes)
        pacc[0, :, lanes] = p
        q = meas[:, lanes].astype(F32)
        pq, pp = p * q, p * p
        pred_sq = pred_sq + jnp.sum(pp, axis=1, keepdims=True)
        pred_meas = pred_meas + jnp.sum(pq, axis=1, keepdims=True)
        for s in range(SLIDES):
            stat[j, s:s + 1, :] = jnp.sum(mcol[s] * pq, axis=0, keepdims=True)
            stat[j, 3 + s:4 + s, :] = jnp.sum(mcol[s] * pp, axis=0, keepdims=True)
    inv_pred = lax.rsqrt(pred_sq + FLOOR)
    spot_cos = pred_meas * inv_pred * inv_meas
    spot_sum = jnp.sum(wcol * spot_cos, axis=0, keepdims=True)
    scal = jnp.where(lane_id == 0, spot_sum, 0.0)
    for s in range(SLIDES):
        scal = scal + jnp.where(lane_id == 1 + s, kl[s:s + 1] * (1.0 / Q), 0.0)
    for j in range(A):
        stat[j, 6:8, :] = jnp.concatenate([scal, jnp.zeros((1, GA), F32)], axis=0)

    cps = []
    for i, e, part, where in sharers:
        cp = remote(stat.at[part], s1.at[i, e], s1_s.at[i, e], s1_r.at[i, e], where)
        cp.start()
        cps.append(cp)
    pending.extend(cps)
    u = stat[mine]
    for (i, e, part, where), cp in zip(sharers, cps):
        cp.wait_recv()
        u = u + s1[i, e]
    ubuf[...] = u
    cps = []
    for i, where in others:
        cp = remote(ubuf, s2.at[i], s2_s.at[i], s2_r.at[i], where)
        cp.start()
        cps.append(cp)
    pending.extend(cps)
    for cp in cps + gmc:
        cp.wait_recv()
    u = tree_sum(u, [s2[i] for i in range(len(others))])
    if k.PLANE:
        gmeas = tree_sum(gm_out[...], [gm_in[i] for i in range(len(others))])[:SLIDES]
        inv_gmeas = lax.rsqrt(gmeas + FLOOR)
    share = tally * (1.0 / G)
    a = lax.rsqrt(u[3:6] + FLOOR)
    b = inv_gmeas
    gcos = u[0:3] * a * b
    wall[mine] = jnp.concatenate(
        [share * a * b, share * gcos * a * a,
         jnp.sum(share * gcos, axis=0, keepdims=True), u[6:7]], axis=0)
    cps = []
    for i, e, part, where in sharers:
        cp = remote(wall.at[mine], wall.at[mine], s3_s.at[i, e], s3_r.at[i, e], where)
        cp.start()
        cps.append(cp)
    pending.extend(cps)
    for i, e, part, where in sharers:
        remote(wall.at[part], wall.at[part], s3_s.at[i, e], s3_r.at[i, e], where).wait_recv()

    lead = -(wcol * inv_pred * inv_meas)
    back = wcol * spot_cos * inv_pred * inv_pred
    dot1 = jnp.zeros((S, 1), F32)
    gene_total = jnp.zeros((1, GA), F32)
    for j in range(A):
        lanes = slice(j * GA, (j + 1) * GA)
        w = wall[j]
        direct = mcol[0] * w[0:1] + mcol[1] * w[1:2] + mcol[2] * w[2:3]
        damp = mcol[0] * w[3:4] + mcol[1] * w[4:5] + mcol[2] * w[5:6]
        gene_total = gene_total + w[6:7]
        p = pacc[0, :, lanes]
        g = (lead - direct) * meas[:, lanes].astype(F32) + (back + damp) * p
        glow = g.astype(BF16)
        gp[0, 0, :, lanes] = glow
        dot1 = dot1 + jnp.sum(glow.astype(F32) * p, axis=1, keepdims=True)

    gz, gc = {}, {}

    def to_core(m):
        cp = remote(gp.at[m, 0], gp.at[m, 1], gc_s.at[m], gc_r.at[m], group(0, 1))
        cp.start()
        gc[m] = cp
        pending.append(cp)

    def to_plane(m, b):
        t = m ^ (1 << b)
        cp = remote(gp.at[m, 0], gp.at[t, 0], gz_s.at[t], gz_r.at[t], group(1 << b, 0))
        cp.start()
        gz[t] = cp
        pending.append(cp)

    to_core(0)
    gz[high] = remote(gp.at[0, 0], gp.at[high, 0], gz_s.at[high], gz_r.at[high], group(high, 0))

    for b in range(top):
        t = 1 << b
        gz[t] = remote(gp.at[0, 0], gp.at[t, 0], gz_s.at[t], gz_r.at[t], group(t, 0))

    def near_start():
        for b in reversed(range(top)):
            gz[1 << b].start()

    @pl.when(c == 0)
    def _():
        gz[high].start()

    @pl.when(c == 1)
    def _():
        near_start()

    for m, e in groups:
        dcp[m, e].wait_recv()
    dtot = dpart[0, 0]
    for m, e in groups:
        dtot = dtot + din[m, e]
    dot_row = jnp.broadcast_to(dot1, (S, S)).T[0:8] - dtot
    info2[0, 0] = dot_row
    i2 = {}
    for m, e in groups:
        cp = remote(info2.at[0, 0], info2.at[m, e], i2_s.at[m, e], i2_r.at[m, e], group(m, e))
        cp.start()
        i2[m, e] = cp
        pending.append(cp)

    fin = wall[0]
    total_tally = jnp.sum(tally, axis=0, keepdims=True)
    gsum = jnp.sum(gene_total, axis=1, keepdims=True)
    dens = jnp.zeros((1, 1), F32)
    for s in range(SLIDES):
        dens = dens + tally[s:s + 1] * fin[7:8, 1 + s:2 + s]
    lid = lax.broadcasted_iota(jnp.int32, (8, 128), 1)
    out_loss[...] = (jnp.where(lid == 0, fin[7:8, 0:1], 0.0) + jnp.where(lid == 1, gsum, 0.0)
                     + jnp.where(lid == 2, dens, 0.0)) / total_tally

    ycp = {}

    def map_rows(m, es, gpm):
        n = len(es)

        def step(i, _):
            r0 = pl.multiple_of(i * RC, RC)
            low = lax.dot_general(cells[pl.ds(r0, RC), :], gpm(),
                                  (((1,), (1,)), ((), ())), preferred_element_type=F32)
            mx = [mext[:, pl.ds(pl.multiple_of((m * 2 + e) * S, S), S)] for e in es]
            rt = lax.dot_general(ratio_hl[:, pl.ds(r0, RC)], jnp.concatenate(mx, axis=1),
                                 (((0,), (0,)), ((), ())), preferred_element_type=F32)
            low = low - rt
            per = YR // RC
            for i_e, e in enumerate(es):
                sh = shares_of(m, e, i) * float(k.CELLS)
                v = sh * (low[:, i_e * S:(i_e + 1) * S] - info2[m, e, 0:1, :])
                ybuf[(m * 2 + e) * X + i // per,
                     pl.ds(pl.multiple_of(lax.rem(i, per) * RC, RC), RC), :] = v.astype(BF16)
            return 0

        lax.fori_loop(0, NC // RC, step, 0)

    def map_copies(m, es):
        cps = []
        for e in es:
            src = ybuf.at[pl.ds((m * 2 + e) * X, X)]
            if m == 0 and type(e) is int and e == 0:
                cps.append(pltpu.make_async_copy(src, out_map.at[z, :, c], loc_sem.at[3]))
                ycp[0, 0] = cps[-1]
            else:
                cps.append(remote(src, out_map.at[z, :, c], y_s.at[m, e], y_r.at[m, e],
                                  group(m, e)))
                pending.append(cps[-1])
        return cps

    def send_map(m, es):
        for cp in map_copies(m, es):
            cp.start()

    def map_piece(m):
        for e in range(2):
            if (m, e) != (0, 0):
                i2[m, e].wait_recv()
        map_rows(m, [0, 1], lambda: gp[m].reshape(2 * S, G))
        send_map(m, [0, 1])

    gc[0].wait_recv()
    map_piece(0)

    def pass_on(m, b):
        for b2 in reversed(range(b)):
            to_plane(m, b2)
        to_core(m)

    gc[high] = remote(gp.at[high, 0], gp.at[high, 1], gc_s.at[high], gc_r.at[high], group(0, 1))
    pending.append(gc[high])
    for b2 in range(top):
        t = high ^ (1 << b2)
        gz[t] = remote(gp.at[high, 0], gp.at[t, 0], gz_s.at[t], gz_r.at[t], group(1 << b2, 0))
        pending.append(gz[t])

    def high_on():
        gz[high].wait_recv()
        gc[high].start()
        for b2 in reversed(range(top)):
            gz[high ^ (1 << b2)].start()

    @pl.when(c == 0)
    def _():
        gz[high].wait_send()
        pl.semaphore_signal(gate, inc=1, device_id=group(0, 1), device_id_type=MESH_ID)
        near_start()
        high_on()

    @pl.when(c == 1)
    def _():
        pl.semaphore_wait(gate, 1)
        gz[high].start()
        gc[high].wait_recv()

    i2[high, 0].wait_recv()
    i2[high, 1].wait_recv()
    map_rows(high, [c], lambda: gp[high, c])

    @pl.when(c == 1)
    def _():
        high_on()

    @pl.when(c == 0)
    def _():
        gc[high].wait_recv()

    own_core = map_copies(high, [c])

    @pl.when(at_end)
    def _():
        own_core[0].start()

    map_rows(high, [1 - c], lambda: gp[high, 1 - c])

    @pl.when(inside)
    def _():
        own_core[0].start()

    send_map(high, [1 - c])
    for b in reversed(range(top)):
        for m in range(1 << b, Z, 2 << b):
            gz[m].wait_recv()
            pass_on(m, b)
    def slot_of(dx, dy, half):
        return ((dx * Y + dy) - 1) * 2 + half

    def single_rows(dx, dy, half):
        bx = lax.rem(x + dx, X)
        by = flip(y, dy)
        return pl.multiple_of(((bx * Y + by) * 2 + half) * H, H)

    def single_part(dx, dy, half, put, m0=0, m1=Z):
        r0 = single_rows(dx, dy, half)
        n = (m1 - m0) * 2 * S

        def step(i, _):
            lanes = pl.ds(pl.multiple_of(i * NN, NN), NN)
            v = jnp.dot(slow[pl.ds(r0, H), m0 * 2 * S:m1 * 2 * S],
                        gp[pl.ds(m0, m1 - m0), :, :, lanes].reshape(n, NN), preferred_element_type=F32)
            put(lanes, v)
            return 0

        lax.fori_loop(0, G // NN, step, 0)

    def put_send(slot, extra=()):
        def put(lanes, v):
            for i in extra:
                v = v + grecv[i, :, lanes].astype(F32)
            gsend[slot, :, lanes] = v.astype(BF16)
        return put

    def put_own(half):
        def put(lanes, v):
            own_single[half * H:(half + 1) * H, lanes] = v
        return put

    def put_rest(sl, half):
        def put(lanes, v):
            v = v + own_single[half * H:(half + 1) * H, lanes]
            gsend[sl, :, lanes] = v.astype(BF16)
        return put

    r_m1 = lambda d: d
    r_m2 = lambda d: XN + d
    r_m3 = lambda d: 2 * XN + d
    r_m5 = lambda d: 3 * XN + d
    r_m4, r_m6 = 4 * XN, 4 * XN + 1
    gcp = {}

    def send_single(slot, r_slot, where):
        cp = remote(gsend.at[slot], grecv.at[r_slot], gs_s.at[r_slot], gs_r.at[r_slot], where)
        cp.start()
        gcp[r_slot] = cp
        pending.append(cp)

    for m in range(1, Z - 1):
        if m != high:
            gc[m].wait_recv()
    for half in range(2):
        single_part(1, 1, half, put_own(half), 0, Z - 1)
    if Z > 2:
        gc[Z - 1].wait_recv()
    for d in range(XN):
        for half in range(2):
            sl = slot_of(d + 1, 1, half)
            if d == 0:
                single_part(1, 1, half, put_rest(sl, half), Z - 1, Z)
            else:
                single_part(d + 1, 1, half, put_send(sl))
            if half == 0:
                send_single(sl, r_m1(d), plane(d + 1, 0))
            else:
                send_single(sl, r_m2(d), plane(0, 1))
    for m in far:
        map_piece(m)
    for d in range(XN):
        s0 = slot_of(d + 1, 0, 0)
        single_part(d + 1, 0, 0, put_send(s0))
        send_single(s0, r_m3(d), plane(d + 1, 0))
    s0 = slot_of(0, 1, 1)
    single_part(0, 1, 1, put_send(s0))
    send_single(s0, r_m4, plane(0, 1))

    for m in near:
        map_piece(m)

    for d in range(XN):
        gcp[r_m2(d)].wait_recv()
        s0 = slot_of(d + 1, 0, 1)
        single_part(d + 1, 0, 1, put_send(s0, [r_m2(d)]))
        send_single(s0, r_m5(d), plane(d + 1, 0))
    for d in range(XN):
        gcp[r_m1(d)].wait_recv()
    s0 = slot_of(0, 1, 0)
    single_part(0, 1, 0, put_send(s0, [r_m1(d) for d in range(XN)]))
    send_single(s0, r_m6, plane(0, 1))

    for half in range(2):
        single_part(0, 0, half, put_own(half))
    cp_single = []
    halves = [[r_m3(d) for d in range(XN)] + [r_m6], [r_m5(d) for d in range(XN)] + [r_m4]]
    for half in range(2):
        for i in halves[half]:
            gcp[i].wait_recv()

        def step(i, _):
            lanes = pl.ds(pl.multiple_of(i * NN, NN), NN)
            v = own_single[half * H:(half + 1) * H, lanes]
            for i2_ in halves[half]:
                v = v + grecv[i2_, :, lanes].astype(F32)
            own_single[half * H:(half + 1) * H, lanes] = v * float(k.CELLS) ** 0.5
            return 0

        lax.fori_loop(0, G // NN, step, 0)
        rows_h = pl.ds(half * H, H)
        cp_single.append(pltpu.make_async_copy(
            own_single.at[rows_h], out_single.at[rows_h], loc_sem.at[4 + half]))
        cp_single[half].start()

    for m, e in groups:
        other = (flip(z, m), slice(None), flip(c, e))
        remote(ybuf.at[pl.ds(0, X)], out_map.at[other[0], :, other[2]], y_s.at[m, e], y_r.at[m, e],
               group(m, e)).wait_recv()
    ycp[0, 0].wait()
    for cp in cp_single:
        cp.wait()
    for cp in pending:
        cp.wait_send()
    for b in range(top):
        gz[1 << b].wait_send()

    @pl.when(c == 1)
    def _():
        gz[high].wait_send()

    @pl.when(at_end)
    def _():
        sent([high])

    @pl.when(inside)
    def _():
        sent(far)


def forward_and_back(k, logits, single_cell, spatial, ids, mask, cell_prior, order):
    Z, X, Y, A, Q, S, G, R, H = k.Z, k.X, k.Y, k.A, k.Q, k.S, k.G, k.R, k.H
    YR, NC, GA, XN = k.YR, k.NC, k.GA, k.X - 1
    vm = pl.BlockSpec(memory_space=pltpu.VMEM)
    hbm = pl.BlockSpec(memory_space=pl.ANY)
    dma = lambda *s: pltpu.SemaphoreType.DMA(s)
    ncl, ngs = 4 * XN + 2, 4 * XN + 2
    scratch = [
        pltpu.VMEM((Z, 2, X, YR, S), BF16),
        pltpu.VMEM((NC, G), BF16),
        pltpu.VMEM((NC, A * S), BF16),
        pltpu.VMEM((A * S, NC), BF16),
        pltpu.VMEM((A * X, YR, S), BF16),
        pltpu.VMEM((Z, 2, 8, S), F32),
        pltpu.VMEM((Z, 2, 8, S), F32),
        pltpu.VMEM((Z, S, G), F32),
        pltpu.VMEM((Z, S, G), BF16),
        pltpu.VMEM((Z, S, G), BF16),
        pltpu.VMEM((Z - 1, S, G), BF16),
        pltpu.VMEM((S, G), BF16),
        pltpu.VMEM((Z, 2, S, G), BF16),
        pltpu.VMEM((2 * (Q - 1), H, G), BF16),
        pltpu.VMEM((ngs, H, G), BF16),
        pltpu.VMEM((8, NC), F32),
        pltpu.VMEM((Q - 1, 8, NC), F32),
        pltpu.VMEM((16, NC), BF16),
        pltpu.VMEM((16, A * S), BF16),
        pltpu.VMEM((Z, 2, 8, S), F32),
        pltpu.VMEM((Z, 2, 8, S), F32),
        pltpu.VMEM((A, 8, GA), F32),
        pltpu.VMEM((Z, 2, 8, GA), F32),
        pltpu.VMEM((8, GA), F32),
        pltpu.VMEM((Q - 1, 8, GA), F32),
        pltpu.VMEM((A, 8, GA), F32),
        pltpu.VMEM((Z, 2, 8, GA), F32),
        pltpu.VMEM((8, GA), F32),
        pltpu.VMEM((Q - 1, 8, GA), F32),
        pltpu.VMEM((A, 8, GA), F32),
        pltpu.VMEM((R, G), F32),
        dma(6),
        dma(Z, 2), dma(Z, 2),
        dma(ncl), dma(ncl),
        dma(Z, 2), dma(Z, 2),
        dma(Z, HALVES), dma(Z, HALVES),
        dma(Z - 1, HALVES), dma(Z - 1, HALVES),
        dma(Q - 1), dma(Q - 1),
        dma(Z, 2), dma(Z, 2),
        dma(Z, 2), dma(Z, 2),
        dma(Q - 1), dma(Q - 1),
        dma(Z, 2), dma(Z, 2),
        dma(Z), dma(Z),
        dma(Z), dma(Z),
        dma(Z, 2), dma(Z, 2),
        dma(Z, 2), dma(Z, 2),
        dma(ngs), dma(ngs),
        dma(Z, 2), dma(Z, 2),
        pltpu.SemaphoreType.REGULAR,
        dma(Q - 1), dma(Q - 1),
    ]
    return pl.pallas_call(
        functools.partial(kernel, k),
        name="mapping",
        out_shape=[
            jax.ShapeDtypeStruct((Z, X, 2, YR, S), BF16),
            jax.ShapeDtypeStruct((R, G), F32),
            jax.ShapeDtypeStruct((8, 128), F32),
        ],
        in_specs=[hbm, hbm, hbm, vm, vm, vm, vm, vm],
        out_specs=[hbm, hbm, vm],
        scratch_shapes=scratch,
        compiler_params=pltpu.CompilerParams(
            collective_id=0, has_side_effects=True, vmem_limit_bytes=64000 * 1024),
        cost_estimate=pl.CostEstimate(
            flops=6 * NC * A * S * G, bytes_accessed=32 << 20, transcendentals=2 * NC * A * S),
    )(logits.reshape(Z, X, 2, YR, S), logits.reshape(A * X, YR, S), single_cell, spatial,
      ids.reshape(1, S), mask.reshape(1, S), cell_prior.reshape(-1, k.PL), order.reshape(1, k.NB))


def body(mesh, map_logits, single_cell, spatial, slide_ids, spot_mask, cell_prior, gene_order):
    cells, spots = map_logits.shape
    k = Sizes(mesh, cells, spatial.shape[1], spots, gene_order.shape[0])
    gmap, gsingle, loss = forward_and_back(
        k, map_logits, single_cell, spatial, slide_ids, spot_mask, cell_prior, gene_order)
    grad_map = gmap.reshape(cells, spots).astype(F32)
    return loss[0, :3], grad_map, gsingle


def solution(mesh):
    k = Sizes(mesh, 1 << 20, 1 << 20, 128, 1)
    fine = Mesh(mesh.devices.reshape(k.Z, k.X, 2, k.Y), AXES)
    in_specs = (P(None, AXES), P(AXES, None), P(AXES, None), P(AXES), P(AXES), P(), P())
    out_specs = (P(), P(None, AXES), P(AXES, None))
    return jax.shard_map(functools.partial(body, mesh), mesh=fine, in_specs=in_specs,
                         out_specs=out_specs, check_vma=False)
```
